128 devices in a mesh: section: 2 (over core), expert: 16 (over z, y), tensor: 4 (over x).
Axes of the slice: x: 4, y: 4, z: 4, core: 2. Of those that a mesh axis runs over, the one named last changes fastest.
Arguments:
- block_input: bfloat16 [2, 1536, 2048], P(None, 'expert'), may hold values from -6 to 6
- cotangent: bfloat16 [2, 1536, 2048], P(None, 'expert'), may hold values from -6 to 6
- segments: int32 [2, 16, 96], P(None, 'expert'), may hold values from 0 to 1, as said below
- routes: int32 [2, 2, 1536, 8], P('section', None, 'expert'), may hold values from 0 to 31, all different within a row; in each aligned block of 24 rows (0 to 23, 24 to 47, ..., all dimensions but the last counted through in order) at most 9 rows name the same one
- norm_attn: bfloat16 [2, 2048], P('section'), may hold values from 0.5 to 1.5
- w_query: bfloat16 [2, 2048, 4096], P('section', None, 'tensor'), may hold values from -0.125 to 0.125
- key_matrix: bfloat16 [2, 2048, 512], P('section', None, 'tensor'), may hold values from -0.125 to 0.125
- value_matrix: bfloat16 [2, 2048, 512], P('section', None, 'tensor'), may hold values from -0.125 to 0.125
- norm_query: bfloat16 [2, 128], P('section'), may hold values from 0.5 to 1.5
- norm_key: bfloat16 [2, 128], P('section'), may hold values from 0.5 to 1.5
- w_output: bfloat16 [2, 4096, 2048], P('section', 'tensor'), may hold values from -0.375 to 0.375
- norm_moe: bfloat16 [2, 2048], P('section'), may hold values from 0.5 to 1.5
- w_router: bfloat16 [2, 2048, 32], P('section'), may hold values from -0.0625 to 0.0625
- w_gate: bfloat16 [2, 32, 2048, 768], P('section', 'expert', None, 'tensor'), may hold values from -0.125 to 0.125
- w_up: bfloat16 [2, 32, 2048, 768], P('section', 'expert', None, 'tensor'), may hold values from -0.125 to 0.125
- w_down: bfloat16 [2, 32, 768, 2048], P('section', 'expert', 'tensor'), may hold values from -0.875 to 0.875
Outputs:
- block_output: bfloat16 [2, 2, 1536, 2048], P('section', None, 'expert')
- input_grad: float32 [2, 2, 1536, 2048], P('section', None, 'expert')
- grad_norm_attn: float32 [2, 2048], P('section')
- grad_query: float32 [2, 2048, 4096], P('section', None, 'tensor')
- grad_key: float32 [2, 2048, 512], P('section', None, 'tensor')
- grad_value: float32 [2, 2048, 512], P('section', None, 'tensor')
- grad_norm_query: float32 [2, 128], P('section')
- grad_norm_key: float32 [2, 128], P('section')
- grad_output: float32 [2, 4096, 2048], P('section', 'tensor')
- grad_norm_moe: float32 [2, 2048], P('section')
- grad_router: float32 [2, 2048, 32], P('section')
- grad_gate: float32 [2, 32, 2048, 768], P('section', 'expert', None, 'tensor')
- grad_up: float32 [2, 32, 2048, 768], P('section', 'expert', None, 'tensor')
- grad_down: float32 [2, 32, 768, 2048], P('section', 'expert', 'tensor')
The draws below stay inside these ranges and needn't reach their ends.
Inputs may be any that keep to these rules, and one draw needn't show every extreme that they name: In each aligned block of 24 rows (the routes of one device of a data group), the 8 experts of a row differ and no expert is named more than 9 times; in every draw some expert is named exactly 9 times in some block. `segments`: along each group's 96 positions the numbers never fall: the first sequence, then the second. Each sequence has 32 to 64 tokens, and in every draw some sequence has exactly 64.
All inputs are finite; a program needn't handle non-finite values.
Results may differ from the reference program's by a relative error of at most 0.04.
Values may be sent and summed in bfloat16 or wider, within the bound.
A program may use at most 320 MiB of HBM per device.

```python
import math
import jax
import jax.numpy as jnp
import numpy as np
from jax import lax

MODEL_DIM = 2048
QUERY_HEADS = 32
KEY_VALUE_HEADS = 4
HEAD_SIZE = 128
FFE = 768
TOPK = 8
MICRO_BATCHES = 2
MICRO_TOKENS = 96
LAYER_COUNT = 2
DATA_GROUPS = 16
TOKENS = 1536
EXPERTS = 32
TQ = 24
CAP = 9
SEQ_MOST = 64
N_EXPERT = 16
N_TENSOR = 4


def draw_segments(key, part):
    key = jax.random.fold_in(key, 11)
    length_key, spot_key = jax.random.split(key)
    pair_count = MICRO_BATCHES * DATA_GROUPS
    first_lengths = jax.random.randint(length_key, (pair_count,), MICRO_TOKENS - SEQ_MOST, SEQ_MOST + 1)
    longest_spot = jax.random.randint(spot_key, (), 0, pair_count)
    first_lengths = jnp.where(jnp.arange(pair_count) == longest_spot, SEQ_MOST, first_lengths)
    positions = jnp.arange(MICRO_TOKENS, dtype=jnp.int32)
    numbers = (positions[None, :] >= first_lengths[:, None]).astype(jnp.int32)
    return numbers.reshape(MICRO_BATCHES, DATA_GROUPS, MICRO_TOKENS)


def levels(key, dims, cuts, low, high):
    loudness = 1.0
    for dim, parts in cuts:
        heights = jax.random.uniform(jax.random.fold_in(jax.random.fold_in(key, 6), dim), (parts,), jnp.float32, low / len(cuts), high / len(cuts))
        loudness = loudness * jnp.repeat(jnp.exp(heights), dims[dim] // parts).reshape((-1,) + (1,) * (len(dims) - 1 - dim))
    return loudness


def assign_block(own_key, own, number, rows, count, top, bound, slope):
    ranking = jax.random.permutation(own_key, count)
    heavy_load, usual = shares(count, rows * top, bound, slope, True), shares(count, rows * top, bound, slope, False)
    places = jnp.arange(count)

    def named(lengths, offset_by):
        used = int((lengths > 0).sum())
        fixed = max(1, used // 4)
        moved = fixed + (places - fixed + offset_by * (used - fixed)) % max(1, count - fixed)
        return jnp.zeros((count,), jnp.int32).at[ranking[jnp.where(places < fixed, places, moved)]].set(jnp.asarray(lengths, jnp.int32))

    lengths = jnp.where(number % 4 == 0, named(heavy_load, number // 4), named(usual, number - number // 4 - 1))
    mixed = jax.random.permutation(jax.random.fold_in(own, 3), count)
    donor, receiver = mixed[0:count // 2 * 2:2], mixed[1:count // 2 * 2:2]
    margin = jnp.minimum(lengths[donor] - 1, bound - lengths[receiver]) // 2
    margin = jnp.where((donor == ranking[0]) | (receiver == ranking[0]) | (lengths[receiver] == 0), 0, jnp.maximum(margin, 0))
    moved = jax.random.randint(jax.random.fold_in(own, 4), (count // 2,), 0, 1 << 20) % (margin + 1)
    lengths = lengths.at[donor].add(-moved).at[receiver].add(moved)
    items = jnp.searchsorted(jnp.cumsum(lengths), jnp.arange(rows * top), side="right").astype(jnp.int32)
    table = items.reshape(top, rows).T
    table = table[jax.random.permutation(jax.random.fold_in(own, 1), rows)]
    offset_by = jax.random.randint(jax.random.fold_in(own, 2), (rows, 1), 0, top)
    return jnp.take_along_axis(table, (jnp.arange(top)[None, :] + offset_by) % top, axis=1)


def shares(count, total, bound, lean, full):
    portions = [(1 << 20) // math.isqrt(rank ** lean) + 1 for rank in range(1, count + 1)]
    largest = bound if full else min(bound, max(-(-total // count), total * portions[0] // sum(portions)))
    least = 1 if total - largest >= count - 1 else 0
    holding, surplus = [largest] + [least] * (count - 1), total - largest - least * (count - 1)
    while surplus > 0:
        candidates = [i for i in range(1, count) if holding[i] < largest] or [i for i in range(1, count) if holding[i] < bound]
        whole, left = sum([portions[i] for i in candidates]), surplus
        for i in candidates:
            addition = min(bound - holding[i], max(1, left * portions[i] // whole), surplus)
            holding[i] = holding[i] + addition
            surplus = surplus - addition
    return np.array(holding)


def centred(stream_key, extent, deviation, most, shards=(), held_as=jnp.bfloat16):
    entries = jax.random.normal(stream_key, extent, jnp.float32) * deviation
    if len(shards) > 0:
        entries = levels(stream_key, extent, shards, -0.22, 0.18) * entries
    return jnp.clip(entries, min=-most, max=most).astype(held_as)


def setup_inputs(seed: int = 0) -> dict:
    splits = jax.random.split(jax.random.key(seed), 17)
    block_input = centred(splits[0], (MICRO_BATCHES, TOKENS, MODEL_DIM), 1.0, 6.0, ((1, 16),))
    cotangent = centred(splits[1], (MICRO_BATCHES, TOKENS, MODEL_DIM), 1.0, 6.0, ((1, 16),))
    segments = draw_segments(jax.random.fold_in(splits[16], 71), 0)
    routes_keys = jax.random.split(jax.random.fold_in(splits[3], 1), LAYER_COUNT * MICRO_BATCHES * TOKENS // TQ)
    routes_turns = jax.random.permutation(jax.random.fold_in(splits[3], 3), LAYER_COUNT * MICRO_BATCHES * TOKENS // TQ)
    routes = jax.vmap(lambda own, number: assign_block(jax.random.fold_in(splits[3], 2), own, number, TQ, EXPERTS, TOPK, CAP, 1))(routes_keys, routes_turns).reshape((LAYER_COUNT, MICRO_BATCHES, TOKENS, TOPK))
    norm_attn = jnp.clip(1.0 + 0.1 * jax.random.normal(splits[4], (LAYER_COUNT, MODEL_DIM), jnp.float32), 0.5, 1.5).astype(jnp.bfloat16)
    w_query = centred(splits[5], (LAYER_COUNT, MODEL_DIM, QUERY_HEADS * HEAD_SIZE), MODEL_DIM ** -0.5, 0.125, ((0, 2), (2, 4)))
    key_matrix = centred(splits[6], (LAYER_COUNT, MODEL_DIM, KEY_VALUE_HEADS * HEAD_SIZE), MODEL_DIM ** -0.5, 0.125, ((0, 2), (2, 4)))
    value_matrix = centred(splits[7], (LAYER_COUNT, MODEL_DIM, KEY_VALUE_HEADS * HEAD_SIZE), MODEL_DIM ** -0.5, 0.125, ((0, 2), (2, 4)))
    norm_query = jnp.clip(1.0 + 0.1 * jax.random.normal(splits[8], (LAYER_COUNT, HEAD_SIZE), jnp.float32), 0.5, 1.5).astype(jnp.bfloat16)
    norm_key = jnp.clip(1.0 + 0.1 * jax.random.normal(splits[9], (LAYER_COUNT, HEAD_SIZE), jnp.float32), 0.5, 1.5).astype(jnp.bfloat16)
    w_output = centred(splits[10], (LAYER_COUNT, QUERY_HEADS * HEAD_SIZE, MODEL_DIM), (QUERY_HEADS * HEAD_SIZE // 16) ** -0.5, 0.375, ((0, 2), (1, 4)))
    norm_moe = jnp.clip(1.0 + 0.1 * jax.random.normal(splits[11], (LAYER_COUNT, MODEL_DIM), jnp.float32), 0.5, 1.5).astype(jnp.bfloat16)
    w_router = centred(splits[12], (LAYER_COUNT, MODEL_DIM, EXPERTS), 0.011, 0.0625, ((0, 2),))
    w_gate = centred(splits[13], (LAYER_COUNT, EXPERTS, MODEL_DIM, FFE), MODEL_DIM ** -0.5, 0.125, ((0, 2), (1, 16), (3, 4)))
    w_up = centred(splits[14], (LAYER_COUNT, EXPERTS, MODEL_DIM, FFE), MODEL_DIM ** -0.5, 0.125, ((0, 2), (1, 16), (3, 4)))
    w_down = centred(splits[15], (LAYER_COUNT, EXPERTS, FFE, MODEL_DIM), (FFE // 16) ** -0.5, 0.875, ((0, 2), (1, 16), (2, 4)))
    return dict(block_input=block_input, cotangent=cotangent, segments=segments, routes=routes, norm_attn=norm_attn, w_query=w_query, key_matrix=key_matrix, value_matrix=value_matrix, norm_query=norm_query, norm_key=norm_key, w_output=w_output, norm_moe=norm_moe, w_router=w_router, w_gate=w_gate, w_up=w_up, w_down=w_down)


EPS = 1e-06
THETA = 1000000.0
MASKED = -1e+30

@jax.custom_vjp
def low(v):
    return lax.optimization_barrier(v.astype(jnp.bfloat16)).astype(jnp.float32)

@jax.custom_vjp
def low_back(v):
    return v

def low_keep(v):
    return (low(v), None)

def low_pass(kept, grad):
    return (grad,)

def back_keep(v):
    return (v, None)

def back_low(kept, grad):
    return (low(grad),)
low.defvjp(low_keep, low_pass)
low_back.defvjp(back_keep, back_low)

def matmul_hi(left_arr, right_arr):
    return jnp.matmul(left_arr, right_arr, precision=lax.Precision.HIGHEST)

def rms_scale(vector, gain_vec):
    mean_sq = lax.optimization_barrier(jnp.mean(vector * vector, axis=-1, keepdims=True))
    return vector * lax.rsqrt(mean_sq + EPS) * gain_vec

def rotary(vector, cosine, sine_table):
    half_dim = vector.shape[-1] // 2
    first_half = vector[..., :half_dim]
    second_half = vector[..., half_dim:]
    return jnp.concatenate([first_half * cosine - second_half * sine_table, second_half * cosine + first_half * sine_table], axis=-1)

def seq_tables(segments):
    row_ids = jnp.arange(MICRO_TOKENS, dtype=jnp.int32)
    earlier = lax.optimization_barrier(jnp.sum((segments[..., None, :] < segments[..., :, None]).astype(jnp.int32), axis=-1))
    position = (row_ids - earlier).astype(jnp.float32)
    inv_freq = jnp.exp(jnp.arange(HEAD_SIZE // 2, dtype=jnp.float32) * (-math.log(THETA) / (HEAD_SIZE // 2)))
    angles = position[..., None] * inv_freq
    allowed = (segments[..., None, :] == segments[..., :, None]) & (row_ids[None, :] <= row_ids[:, None])
    return (jnp.cos(angles), jnp.sin(angles), allowed)

def layer(residual, weights, chosen, cosine, sine_table, allowed):
    gain_attn, query_w, key_w, value_w, gain_query, gain_key, output_w, gain_moe, router_w, gate_w, up_w, down_w = weights
    heads_per_group = QUERY_HEADS // KEY_VALUE_HEADS
    query_shape = (MICRO_BATCHES, DATA_GROUPS, MICRO_TOKENS, KEY_VALUE_HEADS, heads_per_group, HEAD_SIZE)
    key_shape = (MICRO_BATCHES, DATA_GROUPS, MICRO_TOKENS, KEY_VALUE_HEADS, HEAD_SIZE)
    normed = low(rms_scale(residual, gain_attn))
    queries = low_back(matmul_hi(normed, query_w)).reshape(query_shape)
    key_rows = low_back(matmul_hi(normed, key_w)).reshape(key_shape)
    value_rows = low(low_back(matmul_hi(normed, value_w))).reshape(key_shape)
    cos_q = cosine[:, :, :, None, None, :]
    sin_q = sine_table[:, :, :, None, None, :]
    cos_k = cosine[:, :, :, None, :]
    sin_k = sine_table[:, :, :, None, :]
    queries = low(rotary(rms_scale(queries, gain_query), cos_q, sin_q))
    key_rows = low(rotary(rms_scale(key_rows, gain_key), cos_k, sin_k))
    scores = jnp.einsum('mgqjrd,mgkjd->mgjrqk', queries, key_rows, precision=lax.Precision.HIGHEST) * (1.0 / math.sqrt(HEAD_SIZE))
    scores = jnp.where(allowed[:, :, None, None], low_back(scores), MASKED)
    row_max = lax.optimization_barrier(jnp.max(scores, axis=-1, keepdims=True))
    raised = jnp.exp(scores - row_max)
    probs_low = low(raised / lax.optimization_barrier(jnp.sum(raised, axis=-1, keepdims=True)))
    attended = jnp.einsum('mgjrqk,mgkjd->mgqjrd', probs_low, value_rows, precision=lax.Precision.HIGHEST)
    attended = low_back(low(attended.reshape(MICRO_BATCHES, TOKENS, QUERY_HEADS * HEAD_SIZE)))
    mid_resid = residual + low_back(matmul_hi(attended, output_w))
    moe_in = low(rms_scale(mid_resid, gain_moe))
    logits = low_back(matmul_hi(moe_in, router_w))
    gate_weights = jax.nn.softmax(jnp.take_along_axis(logits, chosen, axis=-1), axis=-1)
    copies = low_back(jnp.broadcast_to(moe_in[:, :, None, :], (MICRO_BATCHES, TOKENS, TOPK, MODEL_DIM))).reshape(-1, MODEL_DIM)
    flat_routes = chosen.reshape(-1)
    onehot = (flat_routes[:, None] == jnp.arange(EXPERTS, dtype=jnp.int32)[None, :]).astype(jnp.int32)
    slot_index = lax.optimization_barrier(jnp.sum(onehot * jnp.cumsum(onehot, axis=0), axis=1)) - 1
    room_size = MICRO_BATCHES * N_EXPERT * N_TENSOR * CAP
    places = (flat_routes * room_size + slot_index).astype(jnp.int32)
    buffer = jnp.zeros((EXPERTS * room_size, MODEL_DIM), jnp.float32).at[places].set(copies).reshape(EXPERTS, room_size, MODEL_DIM)
    gate_act = low_back(jnp.einsum('ecd,edf->ecf', buffer, gate_w, precision=lax.Precision.HIGHEST))
    up_act = low_back(jnp.einsum('ecd,edf->ecf', buffer, up_w, precision=lax.Precision.HIGHEST))
    hidden = low(jax.nn.silu(gate_act) * up_act)
    produced = low_back(low(jnp.einsum('ecf,efd->ecd', hidden, down_w, precision=lax.Precision.HIGHEST)))
    picked = produced.reshape(-1, MODEL_DIM)[places].reshape(MICRO_BATCHES, TOKENS, TOPK, MODEL_DIM)
    moe_out = low(lax.optimization_barrier(jnp.sum(gate_weights[..., None] * picked, axis=2)))
    return mid_resid + moe_out

def reference(block_input, cotangent, segments, routes, norm_attn, w_query, key_matrix, value_matrix, norm_query, norm_key, w_output, norm_moe, w_router, w_gate, w_up, w_down):
    cosine, sine_table, allowed = seq_tables(segments)
    params = tuple((weight.astype(jnp.float32) for weight in (norm_attn, w_query, key_matrix, value_matrix, norm_query, norm_key, w_output, norm_moe, w_router, w_gate, w_up, w_down)))
    start_rows = block_input.astype(jnp.float32)

    def forward(first_in, offset, weights):
        first_out = layer(first_in, tuple((weight[0] for weight in weights)), routes[0], cosine, sine_table, allowed)
        sent_low = low(first_out)
        second_in = low_back(sent_low) + offset
        second_out = layer(second_in, tuple((weight[1] for weight in weights)), routes[1], cosine, sine_table, allowed)
        return (second_out, sent_low)
    second_out, pull_back, sent_low = jax.vjp(forward, start_rows, jnp.zeros_like(start_rows), params, has_aux=True)
    d_first, d_second, d_weights = pull_back(cotangent.astype(jnp.float32))
    block_output = jnp.stack([sent_low, second_out]).astype(jnp.bfloat16)
    input_grad = jnp.stack([d_first, d_second])
    return (block_output, input_grad, d_weights[0], d_weights[1], d_weights[2], d_weights[3], d_weights[4], d_weights[5], d_weights[6], d_weights[7], d_weights[8], d_weights[9], d_weights[10], d_weights[11])
```

```python
import functools
import math

import jax
import jax.numpy as jnp
from jax import lax
from jax.experimental import pallas as pl
from jax.experimental.pallas import tpu as pltpu
from jax.sharding import PartitionSpec as P

RING = 4
BF16 = jnp.bfloat16
F32 = jnp.float32


def wrap(value):
    return lax.rem(value + 2 * RING, RING)


class Place:
    def __init__(self):
        self.section = lax.axis_index("section")
        expert = lax.axis_index("expert")
        self.x = lax.axis_index("tensor")
        self.z = lax.div(expert, RING)
        self.y = lax.rem(expert, RING)

    def index(self, axis):
        return getattr(self, axis)

    def device(self, axis, delta):
        at = {"x": self.x, "y": self.y, "z": self.z}
        at[axis] = wrap(at[axis] + delta)
        return (self.section, at["z"] * RING + at["y"], at["x"])

    def peer(self):
        return (1 - self.section, self.z * RING + self.y, self.x)


def meet(devices):
    barrier = pltpu.get_barrier_semaphore()
    for device in devices:
        pl.semaphore_signal(barrier, inc=1, device_id=device, device_id_type=pl.DeviceIdType.MESH)
    pl.semaphore_wait(barrier, len(devices))


class Sender:
    def __init__(self, send_sems, recv_sems):
        self.send_sems, self.recv_sems = send_sems, recv_sems
        self.used = 0
        self.started = []

    def send(self, source, target, device):
        copy = pltpu.make_async_remote_copy(
            src_ref=source,
            dst_ref=target,
            send_sem=self.send_sems.at[self.used],
            recv_sem=self.recv_sems.at[self.used],
            device_id=device,
            device_id_type=pl.DeviceIdType.MESH,
        )
        self.used += 1
        copy.start()
        self.started.append(copy)
        return copy

    def send_either(self, flag, source, otherwise, target, device):
        first, second = [
            pltpu.make_async_remote_copy(
                src_ref=origin,
                dst_ref=target,
                send_sem=self.send_sems.at[self.used],
                recv_sem=self.recv_sems.at[self.used],
                device_id=device,
                device_id_type=pl.DeviceIdType.MESH,
            )
            for origin in (source, otherwise)
        ]
        self.used += 1
        pl.when(flag)(first.start)
        pl.when(jnp.logical_not(flag))(second.start)
        self.started.append(first)
        return first

    def finish(self):
        for copy in self.started:
            copy.wait_send()


def cut(width, count):
    tiles = width // 128
    edges = [tiles * i // count for i in range(count + 1)]
    return [(128 * a, 128 * (b - a)) for a, b in zip(edges[:-1], edges[1:])]


def region(place, order, phase, at, columns):
    spot = {}
    for i, axis in enumerate(order):
        spot[axis] = slice(None) if i < phase else (at if i == phase else place.index(axis))
    return (*[spot[axis] for axis in "zyx" if axis in spot], slice(None), pl.ds(*columns))


SENDS = 3 * (3 + 3 + 6)


def halves(columns):
    left, right = cut(columns[1], 2)
    return (columns[0] + left[0], left[1]), (columns[0] + right[0], right[1])


def thirds(buffer):
    return [(buffer, order, columns) for order, columns in zip(("xyz", "yzx", "zxy"), cut(buffer.shape[-1], 3))]


def gather(place, sender, plans, own=None, settle=None, beside=()):
    last_phase = len(plans[0][1]) - 1
    for phase in range(last_phase + 1):
        waits = []
        for buffer, order, columns in plans:
            axis = order[phase]
            me = place.index(axis)

            def push(delta, piece):
                here = buffer.at[region(place, order, phase, me, piece)]
                source = own.at[:, pl.ds(*piece)] if own is not None and phase == 0 else here
                return sender.send(source, here, place.device(axis, delta))

            if phase == last_phase:
                left, right = halves(columns)
                onward = (push(1, left), push(-1, right))
                waits += [push(1, right), push(-1, left)]
                waits.append((onward, buffer, order, axis, me, left, right))
            else:
                waits += [push(1, columns), push(-1, columns), push(2, columns)]
        if phase < len(beside):
            beside[phase]()
        last = []
        for wait in waits:
            if isinstance(wait, tuple):
                (up, down), buffer, order, axis, me, left, right = wait
                up.wait_recv()
                passing = buffer.at[region(place, order, phase, wrap(me - 1), left)]
                last.append(sender.send(passing, passing, place.device(axis, 1)))
                down.wait_recv()
                passing = buffer.at[region(place, order, phase, wrap(me + 1), right)]
                last.append(sender.send(passing, passing, place.device(axis, -1)))
            else:
                last.append(wait)
        for copy in last:
            copy.wait_recv()
        if phase == 0 and settle is not None:
            settle()


def neighbours(place, axes="xyz"):
    return [place.device(axis, delta) for axis in axes for delta in (1, -1, 2)]


def reduce(place, sender, plans, slots, beside=()):
    last_phase = len(plans[0][1]) - 1
    for turn_number, phase in enumerate(range(last_phase, -1, -1)):
        waits = []
        for (buffer, order, columns), slot in zip(plans, slots):
            axis, slot = order[phase], slot[phase]
            me = place.index(axis)

            def push(delta, at, piece, target, buffer=buffer, order=order, axis=axis, me=me):
                source = buffer.at[region(place, order, phase, wrap(me + at), piece)]
                return sender.send(source, target, place.device(axis, delta))

            if phase == last_phase:
                left, right = halves(columns)
                up, down = push(1, 2, left, slot[0]), push(-1, 2, right, slot[1])
                near = push(1, 1, right, slot[2]), push(-1, -1, left, slot[3])
                waits.append((push, up, down, near))
            else:
                waits.append([push(delta, delta, columns, slot[i]) for i, delta in enumerate((1, -1, 2))])
        if turn_number < len(beside):
            beside[turn_number]()
        if phase == last_phase:
            later = []
            for (buffer, order, columns), slot, (push, up, down, near) in zip(plans, slots, waits):
                slot = slot[phase]
                me = place.index(order[phase])
                left, right = halves(columns)
                up.wait_recv()
                add_into(buffer, region(place, order, phase, wrap(me + 1), left), slot[0])
                on_up = push(1, 1, left, slot[4])
                down.wait_recv()
                add_into(buffer, region(place, order, phase, wrap(me - 1), right), slot[1])
                on_down = push(-1, -1, right, slot[5])
                later.append((*near, on_up, on_down))
            for (buffer, order, columns), slot, copies in zip(plans, slots, later):
                slot = slot[phase]
                me = place.index(order[phase])
                left, right = halves(columns)
                for copy in copies:
                    copy.wait_recv()
                add_into(buffer, region(place, order, phase, me, left), slot[3], slot[4])
                add_into(buffer, region(place, order, phase, me, right), slot[2], slot[5])
        else:
            for (buffer, order, columns), slot, copies in zip(plans, slots, waits):
                for copy in copies:
                    copy.wait_recv()
                add_into(buffer, region(place, order, phase, place.index(order[phase]), columns), *slot[phase])


def slot_scratch(plans):
    scratch = []
    for rows, axes, columns in plans:
        left, right = halves(columns)
        for phase in range(axes):
            widths = (left, right, right, left, left, right) if phase == axes - 1 else (columns,) * 3
            scratch += [pltpu.VMEM((RING,) * phase + (rows, width), BF16) for _, width in widths]
    return scratch


def third_slots(rows, columns):
    return slot_scratch([(rows, 3, piece) for piece in cut(columns, 3)])


def sort_slots(refs, plans, axes):
    refs = list(refs)
    counts = [6 if phase == axes - 1 else 3 for phase in range(axes)]
    return [[[refs.pop(0) for _ in range(count)] for count in counts] for _ in range(plans)]


def add_into(buffer, at, *terms):
    *spots, rows, columns = at
    free = [i for i, spot in enumerate(spots) if isinstance(spot, slice)]

    def one(n, _):
        spot = list(spots)
        picks = []
        for i in reversed(free):
            spot[i] = lax.rem(n, RING)
            picks.insert(0, spot[i])
            n = lax.div(n, RING)
        here = (*spot, rows, columns)
        total = buffer[here].astype(F32)
        for term in terms:
            total = total + term[(*picks, slice(None), slice(None))].astype(F32)
        buffer[here] = total.astype(BF16)
        return 0

    if free:
        lax.fori_loop(0, RING ** len(free), one, 0)
    else:
        one(0, 0)


EPS = 1e-06
THETA = 1000000.0
MASKED = -1e30
GATED = 128
VMEM_LIMIT = 56 << 20


def params(number):
    return pltpu.CompilerParams(collective_id=number, has_side_effects=True, vmem_limit_bytes=VMEM_LIMIT)


IN_VMEM = pl.BlockSpec(memory_space=pltpu.VMEM)
ANYWHERE = pl.BlockSpec(memory_space=pl.ANY)


def copy_sems(count):
    return [pltpu.SemaphoreType.DMA((count,)), pltpu.SemaphoreType.DMA((count,))]


def dot_nn(left, right):
    return lax.dot_general(left, right, (((1,), (0,)), ((), ())), preferred_element_type=F32)


def dot_nt(left, right):
    return lax.dot_general(left, right, (((1,), (1,)), ((), ())), preferred_element_type=F32)


def dot_tn(left, right):
    return lax.dot_general(left, right, (((0,), (0,)), ((), ())), preferred_element_type=F32)


def inverse_rms(rows):
    return lax.rsqrt(jnp.mean(rows * rows, axis=-1, keepdims=True) + EPS)


def rms_back(rows, gain, grad):
    scale = inverse_rms(rows)
    unit = rows * scale
    lifted = grad * gain
    return scale * (lifted - unit * jnp.mean(lifted * unit, axis=-1, keepdims=True)), grad * unit


def scatter_x(place, sender, part, slots):
    copies = [
        sender.send(part.at[wrap(place.x + delta)], slots.at[i], place.device("x", delta))
        for i, delta in enumerate((1, -1, 2))
    ]
    for copy in copies:
        copy.wait_recv()
    total = part[place.x].astype(F32)
    for i in range(3):
        total = total + slots[i].astype(F32)
    return total


def gather_x(place, sender, whole):
    mine = whole.at[place.x]
    copies = [sender.send(mine, mine, place.device("x", delta)) for delta in (1, -1, 2)]
    for copy in copies:
        copy.wait_recv()


def mix_kernel(layer, part, resid, pack0, pack1, routes0, routes1, mid, gates, rows_all, own, slots, send, recv, local):
    place = Place()
    meet(neighbours(place))
    sender = Sender(send, recv)
    chosen = of_layer(layer, routes0[place.x], routes1[place.x])
    lanes = lax.broadcasted_iota(jnp.int32, gates.shape, 1)
    named = chosen[:, 0:1] == lanes
    for i in range(1, chosen.shape[1]):
        named = named | (chosen[:, i : i + 1] == lanes)
    gain = of_layer(layer, pack0[PACK_ROUTER + 1 : PACK_ROUTER + 2], pack1[PACK_ROUTER + 1 : PACK_ROUTER + 2])
    router = of_layer(layer, pack0[:PACK_ROUTER], pack1[:PACK_ROUTER])
    total = scatter_x(place, sender, part, slots)
    mid_rows = resid[place.x].astype(F32) + total
    mid[...] = mid_rows
    moe_in = (mid_rows * inverse_rms(mid_rows) * gain.astype(F32)).astype(BF16)
    logits = jnp.where(named, dot_nt(moe_in, router), MASKED)
    raised = jnp.where(named, jnp.exp(logits - jnp.max(logits, axis=-1, keepdims=True)), 0.0)
    weights = raised / jnp.sum(raised, axis=-1, keepdims=True)
    gates[...] = weights
    own[:, : moe_in.shape[1]] = moe_in
    own[:, moe_in.shape[1] :] = weights.astype(BF16)
    keep = pltpu.make_async_copy(own, rows_all.at[place.z, place.y, place.x], local)
    keep.start()
    gather(place, sender, thirds(rows_all), own, keep.wait)
    sender.finish()


def mix(layer, part, resid, packs, routes):
    _, rows, width = part.shape
    return pl.pallas_call(
        functools.partial(mix_kernel, layer),
        name="mix",
        out_shape=(
            jax.ShapeDtypeStruct((rows, width), F32),
            jax.ShapeDtypeStruct((rows, GATED), F32),
            jax.ShapeDtypeStruct((RING, RING, RING, rows, width + GATED), BF16),
        ),
        in_specs=[IN_VMEM] * 6,
        out_specs=(IN_VMEM, IN_VMEM, ANYWHERE),
        scratch_shapes=[
            pltpu.VMEM((rows, width + GATED), BF16),
            pltpu.VMEM((3, rows, width), BF16),
            *copy_sems(3 + SENDS),
            pltpu.SemaphoreType.DMA,
        ],
        compiler_params=params(1 + layer),
    )(part, resid, *packs, *routes)


def settle_kernel(partial, mid, out, buffer, send, recv, local, *slots):
    place = Place()
    load = pltpu.make_async_copy(partial, buffer, local)
    load.start()
    meet(neighbours(place))
    sender = Sender(send, recv)
    load.wait()
    reduce(place, sender, thirds(buffer), sort_slots(slots, 3, 3))
    moe_rows = buffer[place.z, place.y, place.x].astype(F32)
    out[place.x] = (mid[...] + moe_rows).astype(BF16)
    gather_x(place, sender, out)
    sender.finish()


def settle_layer(partial, mid):
    rows, width = partial.shape[-2:]
    return pl.pallas_call(
        settle_kernel,
        name="settle",
        out_shape=jax.ShapeDtypeStruct((RING, rows, width), BF16),
        in_specs=[ANYWHERE, IN_VMEM],
        out_specs=IN_VMEM,
        scratch_shapes=[
            pltpu.VMEM(partial.shape, BF16),
            *copy_sems(3 + SENDS),
            pltpu.SemaphoreType.DMA,
            *third_slots(rows, width),
        ],
        compiler_params=params(3),
    )(partial, mid)


def share_kernel(rows_in, rows_all, send, recv, local):
    place = Place()
    meet(neighbours(place))
    sender = Sender(send, recv)
    own = rows_in.at[place.x]
    keep = pltpu.make_async_copy(own, rows_all.at[place.z, place.y, place.x], local)
    keep.start()
    gather(place, sender, thirds(rows_all), own, keep.wait)
    sender.finish()


def share_rows(rows_in):
    _, rows, width = rows_in.shape
    return pl.pallas_call(
        share_kernel,
        name="share",
        out_shape=jax.ShapeDtypeStruct((RING, RING, RING, rows, width), BF16),
        in_specs=[IN_VMEM],
        out_specs=ANYWHERE,
        scratch_shapes=[*copy_sems(SENDS), pltpu.SemaphoreType.DMA],
        compiler_params=params(4),
    )(rows_in)


def moe_back_kernel(layer, partial, mid, gates, pack0, pack1, d_part, gain_term, router_term, buffer, send, recv, local, *slots):
    place = Place()
    load = pltpu.make_async_copy(partial, buffer, local)
    load.start()
    meet(neighbours(place))
    sender = Sender(send, recv)
    gain = of_layer(layer, pack0[PACK_ROUTER + 1 : PACK_ROUTER + 2], pack1[PACK_ROUTER + 1 : PACK_ROUTER + 2]).astype(F32)
    router = of_layer(layer, pack0[:PACK_ROUTER], pack1[:PACK_ROUTER])
    load.wait()
    reduce(place, sender, thirds(buffer), sort_slots(slots, 3, 3))
    width = mid.shape[1]
    sums = buffer[place.z, place.y, place.x].astype(F32)
    weights = gates[...]
    d_gates = sums[:, width:]
    d_logits = (weights * (d_gates - jnp.sum(d_gates * weights, axis=-1, keepdims=True))).astype(BF16)
    d_moe_in = sums[:, :width] + dot_nn(d_logits, router)
    mid_rows = mid[...]
    d_mid, terms = rms_back(mid_rows, gain, d_moe_in)
    d_part[place.x] = d_mid.astype(BF16)
    gather_x(place, sender, d_part)
    gain_term[...] = jnp.sum(terms, axis=0, keepdims=True)
    moe_in = (mid_rows * inverse_rms(mid_rows) * gain).astype(BF16)
    router_term[...] = dot_tn(d_logits, moe_in)[: router_term.shape[0]]
    sender.finish()


def moe_back(layer, partial, mid, gates, packs, expert_count):
    rows, width = mid.shape
    return pl.pallas_call(
        functools.partial(moe_back_kernel, layer),
        name="moe_back",
        out_shape=(
            jax.ShapeDtypeStruct((RING, rows, width), BF16),
            jax.ShapeDtypeStruct((1, width), F32),
            jax.ShapeDtypeStruct((expert_count, width), F32),
        ),
        in_specs=[ANYWHERE] + [IN_VMEM] * 4,
        out_specs=(IN_VMEM,) * 3,
        scratch_shapes=[
            pltpu.VMEM(partial.shape, BF16),
            *copy_sems(3 + SENDS),
            pltpu.SemaphoreType.DMA,
            *third_slots(rows, width + GATED),
        ],
        compiler_params=params(5 + layer),
    )(partial, mid, gates, *packs)


def attn_back_kernel(layer, part, resid, pack0, pack1, d_mid, d_input, gain_term, own, slots, send, recv, local):
    place = Place()
    last = layer == 0
    meet(neighbours(place, "x" if last else "xyz"))
    sender = Sender(send, recv)
    total = scatter_x(place, sender, part, slots)
    gain = of_layer(layer, pack0[PACK_ROUTER : PACK_ROUTER + 1], pack1[PACK_ROUTER : PACK_ROUTER + 1]).astype(F32)
    d_resid, terms = rms_back(resid[place.x].astype(F32), gain, total)
    gain_term[...] = jnp.sum(terms, axis=0, keepdims=True)
    d_rows = (d_mid[place.x].astype(F32) + d_resid).astype(BF16)
    if last:
        d_input[place.x] = d_rows
        gather_x(place, sender, d_input)
    else:
        own[...] = d_rows
        keep = pltpu.make_async_copy(own, d_input.at[place.z, place.y, place.x], local)
        keep.start()
        gather(place, sender, thirds(d_input), own, keep.wait)
    sender.finish()


def attn_back_rows(layer, part, resid, packs, d_mid):
    _, rows, width = part.shape
    last = layer == 0
    out = (RING, rows, width) if last else (RING, RING, RING, rows, width)
    return pl.pallas_call(
        functools.partial(attn_back_kernel, layer),
        name="attn_back_last" if last else "attn_back",
        out_shape=(jax.ShapeDtypeStruct(out, BF16), jax.ShapeDtypeStruct((1, width), F32)),
        in_specs=[IN_VMEM] * 5,
        out_specs=(IN_VMEM if last else ANYWHERE, IN_VMEM),
        scratch_shapes=[
            pltpu.VMEM((rows, width), BF16),
            pltpu.VMEM((3, rows, width), BF16),
            *copy_sems(6 if last else 3 + SENDS),
            pltpu.SemaphoreType.DMA,
        ],
        compiler_params=params(7 + layer),
    )(part, resid, *packs, d_mid)


TILE = 256


def load_weights(layer, own, other, targets, sems):
    gate, up, down = targets
    half = gate.shape[0] // 2
    section = lax.axis_index("section")

    def pairs(source):
        return [
            (source[0].at[0], gate.at[pl.ds(0, half)]),
            (source[0].at[1], gate.at[pl.ds(half, half)]),
            (source[1].at[0], up.at[pl.ds(0, half)]),
            (source[1].at[1], up.at[pl.ds(half, half)]),
            (source[2].at[0], down.at[pl.ds(0, half)]),
            (source[2].at[1], down.at[pl.ds(half, half)]),
        ]

    @pl.when(section == layer)
    def _():
        for i, (source, target) in enumerate(pairs(own)):
            pltpu.make_async_copy(source, target, sems.at[i]).start()

    @pl.when(section != layer)
    def _():
        for i, (source, target) in enumerate(pairs(other)):
            pltpu.make_async_copy(source, target, sems.at[i]).start()

    return [pltpu.make_async_copy(source, target, sems.at[i]) for i, (source, target) in enumerate(pairs(own))]


def gate_columns(table, half):
    first = 2 * lax.axis_index("expert")
    lanes = lax.broadcasted_iota(jnp.int32, table.shape, 1)
    table = table.astype(F32)
    one = jnp.sum(jnp.where(lanes == first, table, 0.0), axis=1, keepdims=True)
    two = jnp.sum(jnp.where(lanes == first + 1, table, 0.0), axis=1, keepdims=True)
    units = lax.broadcasted_iota(jnp.int32, (table.shape[0], 2 * half), 1)
    return jnp.where(units < half, one, two)


def expert_kernel(layer, rows, own0, own1, own2, other0, other1, other2, out, acts, gate, up, down, sems):
    width = out.shape[1]
    step = pl.program_id(0)

    @pl.when(step == 0)
    def _():
        for copy in load_weights(layer, (own0, own1, own2), (other0, other1, other2), (gate, up, down), sems):
            copy.wait()

    moe_in = rows[:, :width]
    gate_act = dot_nt(moe_in, gate[...])
    up_act = dot_nt(moe_in, up[...])
    units = gate_act.shape[1]
    acts[:, :units] = gate_act.astype(BF16)
    acts[:, units:] = up_act.astype(BF16)
    hidden = gate_act / (1.0 + jnp.exp(-gate_act)) * up_act
    hidden = hidden * gate_columns(rows[:, width:], units // 2)
    out[...] = dot_nn(hidden.astype(BF16), down[...]).astype(BF16)


def experts(layer, rows_all, own, other):
    count = RING**3 * rows_all.shape[3]
    width = rows_all.shape[4] - GATED
    units = 2 * own[0].shape[1]
    rows = rows_all.reshape(count, width + GATED)
    out, acts = pl.pallas_call(
        functools.partial(expert_kernel, layer),
        name="experts",
        grid=(count // TILE,),
        out_shape=(
            jax.ShapeDtypeStruct((count, width), BF16),
            jax.ShapeDtypeStruct((count, 2 * units), BF16),
        ),
        in_specs=[pl.BlockSpec((TILE, width + GATED), lambda i: (i, 0))] + [ANYWHERE] * 6,
        out_specs=(
            pl.BlockSpec((TILE, width), lambda i: (i, 0)),
            pl.BlockSpec((TILE, 2 * units), lambda i: (i, 0)),
        ),
        scratch_shapes=[pltpu.VMEM((units, width), BF16)] * 3 + [pltpu.SemaphoreType.DMA((6,))],
        compiler_params=pltpu.CompilerParams(vmem_limit_bytes=VMEM_LIMIT),
    )(rows, *own, *other)
    return out.reshape(*rows_all.shape[:4], width), acts


def expert_back_kernel(
    layer, rows, grads, acts, own0, own1, own2, other0, other1, other2, out, grad_in, grad_down,
    gate, up, down, sum_in, sum_down, sems
):
    width = grads.shape[1]
    units = acts.shape[1] // 2
    step = pl.program_id(0)

    @pl.when(step == 0)
    def _():
        copies = load_weights(layer, (own0, own1, own2), (other0, other1, other2), (gate, up, down), sems)
        sum_in[...] = jnp.zeros_like(sum_in)
        sum_down[...] = jnp.zeros_like(sum_down)
        for copy in copies:
            copy.wait()

    grad = grads[...]
    weights = gate_columns(rows[:, width:], units // 2)
    back = dot_nt(grad, down[...])
    gate_act = acts[:, :units].astype(F32)
    up_act = acts[:, units:].astype(F32)
    sigmoid = 1.0 / (1.0 + jnp.exp(-gate_act))
    silu = gate_act * sigmoid
    hidden = silu * up_act
    products = hidden * back
    first = 2 * lax.axis_index("expert")
    in_one = lax.broadcasted_iota(jnp.int32, products.shape, 1) < units // 2
    one = jnp.sum(jnp.where(in_one, products, 0.0), axis=1, keepdims=True)
    two = jnp.sum(jnp.where(in_one, 0.0, products), axis=1, keepdims=True)
    lanes = lax.broadcasted_iota(jnp.int32, (products.shape[0], GATED), 1)
    d_gates = jnp.where(lanes == first, one, jnp.where(lanes == first + 1, two, 0.0))
    d_hidden = back * weights
    d_gate = (d_hidden * up_act * sigmoid * (1.0 + gate_act * (1.0 - sigmoid))).astype(BF16)
    d_up = (d_hidden * silu).astype(BF16)
    out[:, :width] = (dot_nn(d_gate, gate[...]) + dot_nn(d_up, up[...])).astype(BF16)
    out[:, width:] = d_gates.astype(BF16)
    moe_in = rows[:, :width]
    sum_in[:units] += dot_tn(d_gate, moe_in)
    sum_in[units:] += dot_tn(d_up, moe_in)
    sum_down[...] += dot_tn((hidden * weights).astype(BF16), grad)

    @pl.when(step == pl.num_programs(0) - 1)
    def _():
        grad_in[...] = sum_in[...].astype(BF16)
        grad_down[...] = sum_down[...].astype(BF16)


def experts_back(layer, rows_all, grads_all, acts, own, other):
    count = RING**3 * rows_all.shape[3]
    width = rows_all.shape[4] - GATED
    units = 2 * own[0].shape[1]
    out, grad_in, grad_down = pl.pallas_call(
        functools.partial(expert_back_kernel, layer),
        name="experts_back",
        grid=(count // TILE,),
        out_shape=(
            jax.ShapeDtypeStruct((count, width + GATED), BF16),
            jax.ShapeDtypeStruct((2 * units, width), BF16),
            jax.ShapeDtypeStruct((units, width), BF16),
        ),
        in_specs=[
            pl.BlockSpec((TILE, width + GATED), lambda i: (i, 0)),
            pl.BlockSpec((TILE, width), lambda i: (i, 0)),
            pl.BlockSpec((TILE, 2 * units), lambda i: (i, 0)),
        ]
        + [ANYWHERE] * 6,
        out_specs=(
            pl.BlockSpec((TILE, width + GATED), lambda i: (i, 0)),
            pl.BlockSpec((2 * units, width), lambda i: (0, 0)),
            pl.BlockSpec((units, width), lambda i: (0, 0)),
        ),
        scratch_shapes=[pltpu.VMEM((units, width), BF16)] * 3
        + [pltpu.VMEM((2 * units, width), F32), pltpu.VMEM((units, width), F32), pltpu.SemaphoreType.DMA((6,))],
        compiler_params=pltpu.CompilerParams(vmem_limit_bytes=VMEM_LIMIT),
    )(rows_all.reshape(count, width + GATED), grads_all.reshape(count, width), acts, *own, *other)
    return out.reshape(*rows_all.shape), grad_in, grad_down


def pull(layer, own, other, targets, sems):
    section = lax.axis_index("section")

    @pl.when(section == layer)
    def _():
        for i, (source, target) in enumerate(zip(own, targets)):
            pltpu.make_async_copy(source, target, sems.at[i]).start()

    @pl.when(section != layer)
    def _():
        for i, (source, target) in enumerate(zip(other, targets)):
            pltpu.make_async_copy(source, target, sems.at[i]).start()

    return [pltpu.make_async_copy(source, target, sems.at[i]) for i, (source, target) in enumerate(zip(own, targets))]


def of_layer(layer, own, other):
    return jnp.where(lax.axis_index("section") == layer, own, other)


def tables(seg_column, seg_row, dim):
    rows = seg_column.shape[0]
    at_row = lax.broadcasted_iota(jnp.int32, (rows, rows), 0)
    at_column = lax.broadcasted_iota(jnp.int32, (rows, rows), 1)
    earlier = jnp.sum((seg_row < seg_column).astype(F32), axis=1, keepdims=True)
    position = lax.broadcasted_iota(jnp.int32, (rows, dim), 0).astype(F32) - earlier
    lane = lax.broadcasted_iota(jnp.int32, (rows, dim), 1)
    half = dim // 2
    place = jnp.where(lane < half, lane, lane - half).astype(F32)
    angle = position * jnp.exp(place * (-math.log(THETA) / half))
    sine = jnp.sin(angle)
    return jnp.cos(angle), jnp.where(lane < half, -sine, sine), (seg_row == seg_column) & (at_column <= at_row)


def turn(rows, cosine, sine):
    return rows * cosine + pltpu.roll(rows, rows.shape[1] // 2, 1) * sine


def turn_back(grad, cosine, sine):
    return grad * cosine + pltpu.roll(grad * sine, grad.shape[1] // 2, 1)


PACK_ROUTER = 128
PACK_ROWS = 144
HEADS_STEP = 2


def attention_kernel(
    layer, rows, seg_column, seg_row, pack0, pack1, q0, k0, v0, o0, q1, k1, v1, o1,
    part, attended, query_raw, key_raw, value_low, wq, wk, wv, wo, total, sems
):
    dim = wk.shape[1]
    heads = wq.shape[1] // dim
    step = HEADS_STEP * dim
    steps = heads // HEADS_STEP

    def pieces(q, k, v, o):
        columns = [q.at[:, pl.ds(i * step, step)] for i in range(steps)]
        return [k, v, *columns, *[o.at[pl.ds(i * step, step)] for i in range(steps)]]

    loads = pull(layer, pieces(q0, k0, v0, o0), pieces(q1, k1, v1, o1), pieces(wq, wk, wv, wo), sems)
    resid = rows[...].astype(F32)
    gain = of_layer(layer, pack0[PACK_ROUTER : PACK_ROUTER + 1], pack1[PACK_ROUTER : PACK_ROUTER + 1]).astype(F32)
    gains = of_layer(layer, pack0[PACK_ROUTER + 2 : PACK_ROUTER + 3], pack1[PACK_ROUTER + 2 : PACK_ROUTER + 3]).astype(F32)
    gain_query, gain_key = gains[:, :dim], gains[:, dim : 2 * dim]
    cosine, sine, allowed = tables(seg_column[...], seg_row[...], dim)
    normed = (resid * inverse_rms(resid) * gain).astype(BF16)
    loads[0].wait()
    raw = dot_nn(normed, wk[...])
    key_raw[...] = raw
    key = turn(raw * inverse_rms(raw) * gain_key, cosine, sine).astype(BF16)
    loads[1].wait()
    value = dot_nn(normed, wv[...]).astype(BF16)
    value_low[...] = value
    for i in range(steps):
        loads[2 + i].wait()
        raws = dot_nn(normed, wq[:, i * step : (i + 1) * step])
        query_raw[:, i * step : (i + 1) * step] = raws
        for h in range(HEADS_STEP):
            raw = raws[:, h * dim : (h + 1) * dim]
            query = turn(raw * inverse_rms(raw) * gain_query, cosine, sine).astype(BF16)
            scores = jnp.where(allowed, dot_nt(query, key) * (1.0 / math.sqrt(dim)), MASKED)
            raised = jnp.exp(scores - jnp.max(scores, axis=1, keepdims=True))
            probs = (raised / jnp.sum(raised, axis=1, keepdims=True)).astype(BF16)
            at = i * step + h * dim
            attended[:, at : at + dim] = dot_nn(probs, value).astype(BF16)
        loads[2 + steps + i].wait()
        piece = dot_nn(attended[:, i * step : (i + 1) * step], wo[i * step : (i + 1) * step])
        if i == 0:
            total[...] = piece
        else:
            total[...] += piece
    quarter = part.shape[1]
    for i in range(part.shape[0]):
        part[i] = total[i * quarter : (i + 1) * quarter].astype(BF16)


def weight_scratch(dense):
    return [pltpu.VMEM(w.shape, BF16) for w in dense]


def attention(layer, rows, segs, packs, own, other):
    count, width = rows.shape
    dim, inner = own[1].shape[1], own[0].shape[1]
    return pl.pallas_call(
        functools.partial(attention_kernel, layer),
        name="attention",
        out_shape=(
            jax.ShapeDtypeStruct((RING, count // RING, width), BF16),
            jax.ShapeDtypeStruct((count, inner), BF16),
            jax.ShapeDtypeStruct((count, inner), F32),
            jax.ShapeDtypeStruct((count, dim), F32),
            jax.ShapeDtypeStruct((count, dim), BF16),
        ),
        in_specs=[IN_VMEM] * 5 + [ANYWHERE] * 8,
        out_specs=(IN_VMEM,) * 5,
        scratch_shapes=[
            *weight_scratch(own),
            pltpu.VMEM((count, width), F32),
            pltpu.SemaphoreType.DMA((2 + 2 * (inner // dim // HEADS_STEP),)),
        ],
        compiler_params=pltpu.CompilerParams(vmem_limit_bytes=VMEM_LIMIT),
    )(rows, *segs, *packs, *own, *other)


def attention_back_kernel(
    layer, rows, seg_column, seg_row, pack0, pack1, attended, query_raw, key_raw, value_low, upstream, d_part,
    q0, k0, v0, o0, q1, k1, v1, o1,
    part, d_mid, normed_out, d_proj, d_mid_low, gain_terms, wq, wk, wv, wo, total, d_heads, sems
):
    dim = wk.shape[1]
    heads = wq.shape[1] // dim
    inner = heads * dim
    step = HEADS_STEP * dim
    steps = heads // HEADS_STEP
    quarter = d_part.shape[1]

    def pieces(q, k, v, o):
        return [*[o.at[pl.ds(i * step, step)] for i in range(steps)],
                *[q.at[:, pl.ds(i * step, step)] for i in range(steps)], k, v]

    loads = pull(layer, pieces(q0, k0, v0, o0), pieces(q1, k1, v1, o1), pieces(wq, wk, wv, wo), sems)
    for i in range(RING):
        grad = upstream[i].astype(F32) + d_part[i].astype(F32)
        d_mid[i] = grad
        total[i * quarter : (i + 1) * quarter] = grad
    grad_low = total[...].astype(BF16)
    d_mid_low[...] = grad_low
    resid = rows[...].astype(F32)
    gain = of_layer(layer, pack0[PACK_ROUTER : PACK_ROUTER + 1], pack1[PACK_ROUTER : PACK_ROUTER + 1]).astype(F32)
    gains = of_layer(layer, pack0[PACK_ROUTER + 2 : PACK_ROUTER + 3], pack1[PACK_ROUTER + 2 : PACK_ROUTER + 3]).astype(F32)
    gain_query, gain_key = gains[:, :dim], gains[:, dim : 2 * dim]
    cosine, sine, allowed = tables(seg_column[...], seg_row[...], dim)
    normed_out[...] = (resid * inverse_rms(resid) * gain).astype(BF16)
    raw_key = key_raw[...]
    key = turn(raw_key * inverse_rms(raw_key) * gain_key, cosine, sine).astype(BF16)
    value = value_low[...]
    scale = 1.0 / math.sqrt(dim)
    d_key = jnp.zeros(key.shape, F32)
    d_value = jnp.zeros(key.shape, F32)
    gain_total = jnp.zeros(gain_query.shape, F32)
    for i in range(steps):
        loads[i].wait()
        d_heads[...] = dot_nt(grad_low, wo[i * step : (i + 1) * step]).astype(BF16)
        for h in range(HEADS_STEP):
            at = i * step + h * dim
            raw = query_raw[:, at : at + dim]
            query = turn(raw * inverse_rms(raw) * gain_query, cosine, sine).astype(BF16)
            scores = jnp.where(allowed, dot_nt(query, key) * scale, MASKED)
            raised = jnp.exp(scores - jnp.max(scores, axis=1, keepdims=True))
            probs = raised / jnp.sum(raised, axis=1, keepdims=True)
            d_head = d_heads[:, h * dim : (h + 1) * dim]
            d_probs = dot_nt(d_head, value)
            d_value = d_value + dot_tn(probs.astype(BF16), d_head)
            d_scores = (probs * (d_probs - jnp.sum(d_probs * probs, axis=1, keepdims=True))).astype(BF16)
            d_query = turn_back(dot_nn(d_scores, key) * scale, cosine, sine)
            d_key = d_key + dot_tn(d_scores, query) * scale
            d_raw, terms = rms_back(raw, gain_query, d_query)
            gain_total = gain_total + jnp.sum(terms, axis=0, keepdims=True)
            d_proj[:, at : at + dim] = d_raw.astype(BF16)
        loads[steps + i].wait()
        piece = dot_nt(d_proj[:, i * step : (i + 1) * step], wq[:, i * step : (i + 1) * step])
        if i == 0:
            total[...] = piece
        else:
            total[...] += piece
    d_raw, terms = rms_back(raw_key, gain_key, turn_back(d_key, cosine, sine))
    d_proj[:, inner : inner + dim] = d_raw.astype(BF16)
    d_proj[:, inner + dim :] = d_value.astype(BF16)
    gain_terms[...] = jnp.zeros(gain_terms.shape, F32)
    gain_terms[:, :dim] = gain_total
    gain_terms[:, dim : 2 * dim] = jnp.sum(terms, axis=0, keepdims=True)
    loads[2 * steps].wait()
    loads[2 * steps + 1].wait()
    total[...] += dot_nt(d_proj[:, inner : inner + dim], wk[...]) + dot_nt(d_proj[:, inner + dim :], wv[...])
    for i in range(RING):
        part[i] = total[i * quarter : (i + 1) * quarter].astype(BF16)


def attention_back(layer, rows, segs, packs, saved, upstream, d_part, own, other):
    count, width = rows.shape
    dim, inner = own[1].shape[1], own[0].shape[1]
    return pl.pallas_call(
        functools.partial(attention_back_kernel, layer),
        name="attention_back",
        out_shape=(
            jax.ShapeDtypeStruct(d_part.shape, BF16),
            jax.ShapeDtypeStruct(d_part.shape, F32),
            jax.ShapeDtypeStruct((count, width), BF16),
            jax.ShapeDtypeStruct((count, inner + 2 * dim), BF16),
            jax.ShapeDtypeStruct((count, width), BF16),
            jax.ShapeDtypeStruct((1, width), F32),
        ),
        in_specs=[IN_VMEM] * 11 + [ANYWHERE] * 8,
        out_specs=(IN_VMEM,) * 6,
        scratch_shapes=[
            *weight_scratch(own),
            pltpu.VMEM((count, width), F32),
            pltpu.VMEM((count, HEADS_STEP * dim), BF16),
            pltpu.SemaphoreType.DMA((2 + 2 * (inner // dim // HEADS_STEP),)),
        ],
        compiler_params=pltpu.CompilerParams(vmem_limit_bytes=VMEM_LIMIT),
    )(rows, *segs, *packs, *saved, upstream, d_part, *own, *other)


SMALL = 48


def finish_kernel(
    n0, p0, a0, m0, n1, p1, a1, m1, r0, g0, h0, q0, r1, g1, h1, q1, in0, down0, in1, down1, out0, out1, ig0, ig1,
    first, second, small_out, got_in, got_down, outputs, input_grads,
    first_sums, second_sums, normed, proj, heads, mids, mine, theirs, arrived, passing, small_slots, send, recv, local, *slots
):
    place = Place()
    lower = place.section == 0
    peer = place.peer()
    sender = Sender(send, recv)
    rows = n0.shape[0]

    def keep(index, flag, source, otherwise, target):
        one, two = (pltpu.make_async_copy(origin, target, local.at[index]) for origin in (source, otherwise))
        pl.when(flag)(one.start)
        pl.when(jnp.logical_not(flag))(two.start)
        return one

    pairs = ((n0, n1, normed), (p0, p1, proj), (a0, a1, heads), (m0, m1, mids))
    kept = [keep(i, lower, low, high, target.at[pl.ds(0, rows)]) for i, (low, high, target) in enumerate(pairs)]
    kept.append(keep(4, lower, out0, out1, outputs.at[place.section]))
    kept.append(keep(5, lower, ig0, ig1, input_grads.at[place.section]))
    for at, low, high in ((0, r0, r1), (32, g0, g1), (33, h0, h1), (34, q0, q1)):
        count = low.shape[0]
        mine[at : at + count] = jnp.where(lower, low[...], high[...])
        passing[at : at + count] = jnp.where(lower, high[...], low[...])
    empty = jnp.zeros((SMALL - 35, passing.shape[1]), F32)
    mine[35:] = empty
    passing[35:] = empty
    theirs[...] = passing[...].astype(BF16)
    meet([peer, *neighbours(place)])
    factors = [
        sender.send_either(lower, high, low, target.at[pl.ds(rows, rows)], peer) for low, high, target in pairs
    ]
    small_copy = sender.send(theirs, arrived, peer)
    late = [
        sender.send_either(lower, out1, out0, outputs.at[place.section], peer),
        sender.send_either(lower, ig1, ig0, input_grads.at[place.section], peer),
        sender.send_either(lower, in1, in0, got_in, peer),
        sender.send_either(lower, down1, down0, got_down, peer),
    ]
    for copy in kept:
        copy.wait()
    for copy in factors:
        copy.wait_recv()
    lanes = 128

    def output_blocks(i, _):
        pair = dot_tn(heads[:, pl.ds(pl.multiple_of(i * lanes, lanes), lanes)], mids[...]).astype(BF16)
        half = lanes // 2
        at = 2 * i
        second_sums[lax.div(at, RING), lax.rem(at, RING)] = pair[:half]
        second_sums[lax.div(at, RING), lax.rem(at, RING) + 1] = pair[half:]
        return 0

    def input_blocks(i, _):
        block = dot_tn(normed[:, pl.ds(pl.multiple_of(i * lanes, lanes), lanes)], proj[...])
        first_sums[lax.div(i, RING), lax.rem(i, RING)] = block.astype(BF16)
        return 0

    lax.fori_loop(0, heads.shape[1] // lanes, output_blocks, 0)
    lax.fori_loop(0, normed.shape[1] // lanes, input_blocks, 0)
    sums = [(first_sums, "yz", (0, first.shape[-1])), (second_sums, "zy", (0, second.shape[-1]))]
    plans = [(first, "yz", (0, first.shape[-1])), (second, "zy", (0, second.shape[-1]))]
    state = {}

    def exchange(step, total):
        passing[...] = total
        buffer = small_slots.at[step, 3]
        buffer[...] = total.astype(BF16)
        state["copies"] = [
            sender.send(buffer, small_slots.at[step, i], place.device("xyz"[step], delta))
            for i, delta in enumerate((1, -1, 2))
        ]

    def collect(step):
        for copy in state["copies"]:
            copy.wait_recv()
        total = passing[...]
        for i in range(3):
            total = total + small_slots[step, i].astype(F32)
        return total

    def small_last():
        small_out[...] = collect(2)

    small_copy.wait_recv()
    exchange(0, mine[...] + arrived[...].astype(F32))
    reduce(place, sender, sums, sort_slots(slots, 2, 2), (lambda: exchange(1, collect(0)), lambda: exchange(2, collect(1))))
    first[place.z, place.y] = first_sums[place.z, place.y]
    second[place.z, place.y] = second_sums[place.z, place.y]
    gather(place, sender, plans, None, None, (small_last,))
    for copy in late:
        copy.wait_recv()
    sender.finish()


def finish(factors, smalls, expert_grads, outs, input_grads):
    rows, width = factors[0][0].shape
    proj = factors[0][1].shape[1]
    inner = factors[0][2].shape[1]
    blocks = RING * RING
    first = (RING, RING, width // blocks, proj)
    second = (RING, RING, inner // blocks, width)
    both = (2, *outs[0].shape)
    return pl.pallas_call(
        finish_kernel,
        name="finish",
        out_shape=(
            jax.ShapeDtypeStruct(first, BF16),
            jax.ShapeDtypeStruct(second, BF16),
            jax.ShapeDtypeStruct((SMALL, width), F32),
            jax.ShapeDtypeStruct(expert_grads[0][0].shape, BF16),
            jax.ShapeDtypeStruct(expert_grads[0][1].shape, BF16),
            jax.ShapeDtypeStruct(both, BF16),
            jax.ShapeDtypeStruct(both, BF16),
        ),
        in_specs=[ANYWHERE] * 8 + [IN_VMEM] * 8 + [ANYWHERE] * 8,
        out_specs=(IN_VMEM,) * 3 + (ANYWHERE,) * 4,
        scratch_shapes=[
            pltpu.VMEM(first, BF16),
            pltpu.VMEM(second, BF16),
            pltpu.VMEM((2 * rows, width), BF16),
            pltpu.VMEM((2 * rows, proj), BF16),
            pltpu.VMEM((2 * rows, inner), BF16),
            pltpu.VMEM((2 * rows, width), BF16),
            pltpu.VMEM((SMALL, width), F32),
            pltpu.VMEM((SMALL, width), BF16),
            pltpu.VMEM((SMALL, width), BF16),
            pltpu.VMEM((SMALL, width), F32),
            pltpu.VMEM((3, 4, SMALL, width), BF16),
            *copy_sems(9 + 9 + 36),
            pltpu.SemaphoreType.DMA((6,)),
            *slot_scratch([(first[2], 2, (0, proj)), (second[2], 2, (0, width))]),
        ],
        compiler_params=params(9),
    )(*factors[0], *factors[1], *smalls[0], *smalls[1], *expert_grads[0], *expert_grads[1], *outs, *input_grads)


def swap(vector):
    return lax.ppermute(vector, "section", [(0, 1), (1, 0)])


def body(
    block_input,
    cotangent,
    segments,
    routes,
    norm_attn,
    w_query,
    key_matrix,
    value_matrix,
    norm_query,
    norm_key,
    w_output,
    norm_moe,
    w_router,
    w_gate,
    w_up,
    w_down,
):
    section = lax.axis_index("section")
    lower = section == 0
    _, group_rows, width = block_input.shape
    expert_count = w_router.shape[2]
    quarter = group_rows // RING
    dim = norm_query.shape[1]

    dense_own = (w_query[0], key_matrix[0], value_matrix[0], w_output[0])
    expert_own = (jnp.swapaxes(w_gate[0], 1, 2), jnp.swapaxes(w_up[0], 1, 2), w_down[0])
    pack_own = jnp.concatenate(
        [
            jnp.pad(w_router[0].T, ((0, PACK_ROUTER - expert_count), (0, 0))),
            norm_attn,
            norm_moe,
            jnp.pad(jnp.concatenate([norm_query, norm_key], axis=1), ((0, PACK_ROWS - PACK_ROUTER - 3), (0, width - 2 * dim))),
        ],
        axis=0,
    )
    routes_own = lax.dynamic_index_in_dim(routes[0], section, 0, keepdims=False)
    routes_other = swap(lax.dynamic_index_in_dim(routes[0], 1 - section, 0, keepdims=False))
    packs = (pack_own, swap(pack_own))
    dense_other = tuple(swap(w) for w in dense_own)
    expert_other = tuple(swap(w) for w in expert_own)
    chosen = tuple(r.reshape(RING, quarter, r.shape[-1]) for r in (routes_own, routes_other))

    def pick(array):
        return lax.dynamic_index_in_dim(array, section, 0, keepdims=False)

    def quarters(array):
        return array.reshape(RING, quarter, array.shape[-1])

    segment = pick(segments)
    segs = (segment.reshape(group_rows, 1), segment.reshape(1, group_rows))

    rows_in = pick(block_input)
    upstream = quarters(pick(cotangent))
    grads_all = share_rows(upstream)
    saved, layer_ins, outs = [], [], []
    for layer in range(2):
        layer_ins.append(rows_in)
        part, *attn_saved = attention(layer, rows_in, segs, packs, dense_own, dense_other)
        mid, gates, rows_all = mix(layer, part, quarters(rows_in), packs, chosen)
        partial, acts = experts(layer, rows_all, expert_own, expert_other)
        out = settle_layer(partial, mid)
        saved.append((attn_saved, mid, gates, rows_all, acts))
        rows_in = out.reshape(group_rows, width)
        outs.append(out)

    factors, smalls, expert_grads, input_grads = [None] * 2, [None] * 2, [None] * 2, [None] * 2
    for layer in (1, 0):
        attn_saved, mid, gates, rows_all, acts = saved[layer]
        partial, grad_in, grad_down = experts_back(layer, rows_all, grads_all, acts, expert_own, expert_other)
        expert_grads[layer] = (grad_in, grad_down)
        d_part, moe_gain_term, router_term = moe_back(layer, partial, mid, gates, packs, expert_count)
        attended, query_raw, key_raw, value_low = attn_saved
        part, d_mid, normed, d_proj, d_mid_low, head_gain_terms = attention_back(
            layer, layer_ins[layer], segs, packs, attn_saved, upstream, d_part, dense_own, dense_other
        )
        factors[layer] = (normed, d_proj, attended, d_mid_low)
        d_input, attn_gain_term = attn_back_rows(layer, part, quarters(layer_ins[layer]), packs, d_mid)
        if layer == 1:
            grads_all = d_input
            d_input = lax.dynamic_index_in_dim(
                d_input.reshape(RING * RING, RING, quarter, width), lax.axis_index("expert"), 0, keepdims=False
            )
        upstream = d_input
        input_grads[layer] = upstream
        smalls[layer] = (router_term, moe_gain_term, attn_gain_term, head_gain_terms)

    first, second, small, got_in, got_down, outputs, d_inputs = finish(factors, smalls, expert_grads, outs, input_grads)
    inner = w_query.shape[2]
    projections = first.reshape(width, first.shape[-1]).astype(F32)[None]

    def total(low, high, got):
        return jnp.where(lower, low, high).astype(F32) + got.astype(F32)

    grad_in = total(expert_grads[0][0], expert_grads[1][0], got_in)
    grad_down = total(expert_grads[0][1], expert_grads[1][1], got_down)
    units = w_gate.shape[3]
    grad_in = grad_in.reshape(2, 2, units, width)
    return (
        outputs.reshape(1, 2, group_rows, width),
        d_inputs.astype(F32).reshape(1, 2, group_rows, width),
        small[33:34],
        projections[:, :, :inner],
        projections[:, :, inner : inner + dim],
        projections[:, :, inner + dim :],
        small[34:35, :dim],
        small[34:35, dim : 2 * dim],
        second.reshape(inner, width).astype(F32)[None],
        small[32:33],
        small[:expert_count].T[None],
        jnp.swapaxes(grad_in[0], 1, 2)[None],
        jnp.swapaxes(grad_in[1], 1, 2)[None],
        grad_down.reshape(1, 2, units, width),
    )


def solution(mesh):
    placed = (
        P(None, "expert", None),
        P(None, "expert", None),
        P(None, "expert", None),
        P("section", None, "expert", None),
        P("section", None),
        P("section", None, "tensor"),
        P("section", None, "tensor"),
        P("section", None, "tensor"),
        P("section", None),
        P("section", None),
        P("section", "tensor", None),
        P("section", None),
        P("section", None, None),
        P("section", "expert", None, "tensor"),
        P("section", "expert", None, "tensor"),
        P("section", "expert", "tensor", None),
    )
    return jax.shard_map(
        body,
        mesh=mesh,
        in_specs=placed,
        out_specs=(
            P("section", None, "expert", None),
            P("section", None, "expert", None),
            P("section", None),
            P("section", None, "tensor"),
            P("section", None, "tensor"),
            P("section", None, "tensor"),
            P("section", None),
            P("section", None),
            P("section", "tensor", None),
            P("section", None),
            P("section", None, None),
            P("section", "expert", None, "tensor"),
            P("section", "expert", None, "tensor"),
            P("section", "expert", "tensor", None),
        ),
        check_vma=False,
    )
```

```python
import functools
import math

import jax
import jax.numpy as jnp
from jax import lax
from jax.experimental import pallas as pl
from jax.experimental.pallas import tpu as pltpu
from jax.sharding import PartitionSpec as P

RING = 4
BF16 = jnp.bfloat16
F32 = jnp.float32


def wrap(value):
    return lax.rem(value + 2 * RING, RING)


class Place:
    def __init__(self):
        self.section = lax.axis_index("section")
        expert = lax.axis_index("expert")
        self.x = lax.axis_index("tensor")
        self.z = lax.div(expert, RING)
        self.y = lax.rem(expert, RING)

    def index(self, axis):
        return getattr(self, axis)

    def device(self, axis, delta):
        at = {"x": self.x, "y": self.y, "z": self.z}
        at[axis] = wrap(at[axis] + delta)
        return (self.section, at["z"] * RING + at["y"], at["x"])

    def peer(self):
        return (1 - self.section, self.z * RING + self.y, self.x)


def greet(devices):
    barrier = pltpu.get_barrier_semaphore()
    for device in devices:
        pl.semaphore_signal(barrier, inc=1, device_id=device, device_id_type=pl.DeviceIdType.MESH)
    return lambda: pl.semaphore_wait(barrier, len(devices))


def meet(devices):
    greet(devices)()


class Copy:
    def __init__(self, sender, copy):
        self.sender, self.copy = sender, copy

    def wait_recv(self):
        self.sender.when(self.copy.wait_recv)


class Sender:
    def __init__(self, send_sems, recv_sems, flag=None):
        self.send_sems, self.recv_sems = send_sems, recv_sems
        self.flag = flag
        self.used = 0
        self.started = []

    def when(self, effect):
        if self.flag is None:
            effect()
        else:
            pl.when(self.flag)(effect)

    def make(self, source, target, device):
        copy = pltpu.make_async_remote_copy(
            src_ref=source,
            dst_ref=target,
            send_sem=self.send_sems.at[self.used],
            recv_sem=self.recv_sems.at[self.used],
            device_id=device,
            device_id_type=pl.DeviceIdType.MESH,
        )
        return copy

    def send(self, source, target, device):
        copy = self.make(source, target, device)
        self.used += 1
        self.when(copy.start)
        self.started.append(copy)
        return Copy(self, copy)

    def send_either(self, flag, source, otherwise, target, device):
        first, second = self.make(source, target, device), self.make(otherwise, target, device)
        self.used += 1
        pl.when(flag)(first.start)
        pl.when(jnp.logical_not(flag))(second.start)
        self.started.append(first)
        return Copy(self, first)

    def hand(self, flag, pairs, device):
        copies = []
        for source, target in pairs:
            copies.append(self.make(source, target, device))
            self.used += 1

        @pl.when(flag)
        def _():
            for copy in copies:
                copy.start()

        def settle():
            @pl.when(flag)
            def _():
                for copy in copies:
                    copy.wait_send()

            @pl.when(jnp.logical_not(flag))
            def _():
                for copy in copies:
                    copy.wait_recv()

        return settle

    def finish(self):
        def effect():
            for copy in self.started:
                copy.wait_send()

        self.when(effect)


def run(job):
    for _ in job:
        pass


def cut(width, count):
    tiles = width // 128
    edges = [tiles * i // count for i in range(count + 1)]
    return [(128 * a, 128 * (b - a)) for a, b in zip(edges[:-1], edges[1:])]


def region(place, order, phase, at, columns):
    spot = {}
    for i, axis in enumerate(order):
        spot[axis] = slice(None) if i < phase else (at if i == phase else place.index(axis))
    return (*[spot[axis] for axis in "zyx" if axis in spot], slice(None), pl.ds(*columns))


SENDS = 3 * (3 + 3 + 6)


def halves(columns):
    left, right = cut(columns[1], 2)
    return (columns[0] + left[0], left[1]), (columns[0] + right[0], right[1])


def thirds(buffer):
    return [(buffer, order, columns) for order, columns in zip(("xyz", "yzx", "zxy"), cut(buffer.shape[-1], 3))]


def gather(place, sender, plans, own=None, settle=None, beside=()):
    last_phase = len(plans[0][1]) - 1
    for phase in range(last_phase + 1):
        waits = []
        for buffer, order, columns in plans:
            axis = order[phase]
            me = place.index(axis)

            def push(delta, piece, buffer=buffer, order=order, axis=axis, me=me):
                here = buffer.at[region(place, order, phase, me, piece)]
                source = own.at[:, pl.ds(*piece)] if own is not None and phase == 0 else here
                return sender.send(source, here, place.device(axis, delta))

            if phase == last_phase:
                left, right = halves(columns)
                onward = (push(1, left), push(-1, right))
                waits += [push(1, right), push(-1, left)]
                waits.append((onward, buffer, order, axis, me, left, right))
            else:
                waits += [push(1, columns), push(-1, columns), push(2, columns)]
        if phase < len(beside):
            beside[phase]()
        yield
        last = []
        for wait in waits:
            if isinstance(wait, tuple):
                (up, down), buffer, order, axis, me, left, right = wait
                up.wait_recv()
                passing = buffer.at[region(place, order, phase, wrap(me - 1), left)]
                last.append(sender.send(passing, passing, place.device(axis, 1)))
                down.wait_recv()
                passing = buffer.at[region(place, order, phase, wrap(me + 1), right)]
                last.append(sender.send(passing, passing, place.device(axis, -1)))
            else:
                last.append(wait)
        if phase == last_phase:
            yield
        for copy in last:
            copy.wait_recv()
        if phase == 0 and settle is not None:
            settle()


def neighbours(place, axes="xyz"):
    return [place.device(axis, delta) for axis in axes for delta in (1, -1, 2)]


def reduce(place, sender, plans, slots, beside=()):
    last_phase = len(plans[0][1]) - 1
    for turn_number, phase in enumerate(range(last_phase, -1, -1)):
        waits = []
        for (buffer, order, columns), slot in zip(plans, slots):
            axis, slot = order[phase], slot[phase]
            me = place.index(axis)

            def push(delta, at, piece, target, buffer=buffer, order=order, axis=axis, me=me):
                source = buffer.at[region(place, order, phase, wrap(me + at), piece)]
                return sender.send(source, target, place.device(axis, delta))

            if phase == last_phase:
                left, right = halves(columns)
                up, down = push(1, 2, left, slot[0]), push(-1, 2, right, slot[1])
                near = push(1, 1, right, slot[2]), push(-1, -1, left, slot[3])
                waits.append((push, up, down, near))
            else:
                waits.append([push(delta, delta, columns, slot[i]) for i, delta in enumerate((1, -1, 2))])
        if turn_number < len(beside):
            beside[turn_number]()
        yield
        if phase == last_phase:
            later = []
            for (buffer, order, columns), slot, (push, up, down, near) in zip(plans, slots, waits):
                slot = slot[phase]
                me = place.index(order[phase])
                left, right = halves(columns)
                up.wait_recv()
                add_into(sender, buffer, region(place, order, phase, wrap(me + 1), left), slot[0])
                on_up = push(1, 1, left, slot[4])
                down.wait_recv()
                add_into(sender, buffer, region(place, order, phase, wrap(me - 1), right), slot[1])
                on_down = push(-1, -1, right, slot[5])
                later.append((*near, on_up, on_down))
            yield
            for (buffer, order, columns), slot, copies in zip(plans, slots, later):
                slot = slot[phase]
                me = place.index(order[phase])
                left, right = halves(columns)
                for copy in copies:
                    copy.wait_recv()
                add_into(sender, buffer, region(place, order, phase, me, left), slot[3], slot[4])
                add_into(sender, buffer, region(place, order, phase, me, right), slot[2], slot[5])
        else:
            for (buffer, order, columns), slot, copies in zip(plans, slots, waits):
                for copy in copies:
                    copy.wait_recv()
                add_into(sender, buffer, region(place, order, phase, place.index(order[phase]), columns), *slot[phase])


def slot_scratch(plans):
    scratch = []
    for rows, axes, columns in plans:
        left, right = halves(columns)
        for phase in range(axes):
            widths = (left, right, right, left, left, right) if phase == axes - 1 else (columns,) * 3
            scratch += [pltpu.VMEM((RING,) * phase + (rows, width), BF16) for _, width in widths]
    return scratch


def third_slots(rows, columns):
    return slot_scratch([(rows, 3, piece) for piece in cut(columns, 3)])


def sort_slots(refs, plans, axes):
    refs = list(refs)
    counts = [6 if phase == axes - 1 else 3 for phase in range(axes)]
    return [[[refs.pop(0) for _ in range(count)] for count in counts] for _ in range(plans)]


def add_into(sender, buffer, at, *terms):
    *spots, rows, columns = at
    free = [i for i, spot in enumerate(spots) if isinstance(spot, slice)]

    def one(n, _):
        spot = list(spots)
        picks = []
        for i in reversed(free):
            spot[i] = lax.rem(n, RING)
            picks.insert(0, spot[i])
            n = lax.div(n, RING)
        here = (*spot, rows, columns)
        total = buffer[here].astype(F32)
        for term in terms:
            total = total + term[(*picks, slice(None), slice(None))].astype(F32)
        buffer[here] = total.astype(BF16)
        return 0

    def all_blocks():
        if free:
            lax.fori_loop(0, RING ** len(free), one, 0)
        else:
            one(0, 0)

    sender.when(all_blocks)


EPS = 1e-06
THETA = 1000000.0
MASKED = -1e30
GATED = 128
VMEM_LIMIT = 56 << 20


def params(number):
    return pltpu.CompilerParams(collective_id=number, has_side_effects=True, vmem_limit_bytes=VMEM_LIMIT)


IN_VMEM = pl.BlockSpec(memory_space=pltpu.VMEM)
ANYWHERE = pl.BlockSpec(memory_space=pl.ANY)


def copy_sems(count):
    return [pltpu.SemaphoreType.DMA((count,)), pltpu.SemaphoreType.DMA((count,))]


def dot_nn(left, right):
    return lax.dot_general(left, right, (((1,), (0,)), ((), ())), preferred_element_type=F32)


def dot_nt(left, right):
    return lax.dot_general(left, right, (((1,), (1,)), ((), ())), preferred_element_type=F32)


def dot_tn(left, right):
    return lax.dot_general(left, right, (((0,), (0,)), ((), ())), preferred_element_type=F32)


def inverse_rms(rows):
    return lax.rsqrt(jnp.mean(rows * rows, axis=-1, keepdims=True) + EPS)


def rms_back(rows, gain, grad):
    scale = inverse_rms(rows)
    unit = rows * scale
    lifted = grad * gain
    return scale * (lifted - unit * jnp.mean(lifted * unit, axis=-1, keepdims=True)), grad * unit


def send_x(place, sender, part, slots):
    return [
        sender.send(part.at[wrap(place.x + delta)], slots.at[i], place.device("x", delta))
        for i, delta in enumerate((1, -1, 2))
    ]


def sum_x(place, copies, part, slots):
    for copy in copies:
        copy.wait_recv()
    total = part[place.x].astype(F32)
    for i in range(3):
        total = total + slots[i].astype(F32)
    return total


def gather_x(place, sender, whole):
    mine = whole.at[place.x]
    copies = [sender.send(mine, mine, place.device("x", delta)) for delta in (1, -1, 2)]
    for copy in copies:
        copy.wait_recv()


def settle_job(place, sender, load, buffer, slots, mid, out):
    load.wait()
    yield from reduce(place, sender, thirds(buffer), sort_slots(slots, 3, 3))
    moe_rows = buffer[place.z, place.y, place.x].astype(F32)
    out[place.x] = (mid[...] + moe_rows).astype(BF16)
    mine = out.at[place.x]
    copies = [sender.send(mine, mine, place.device("x", delta)) for delta in (1, -1, 2)]
    yield
    for copy in copies:
        copy.wait_recv()


def settle_kernel(partial, mid, out, buffer, send, recv, local, *slots):
    place = Place()
    load = pltpu.make_async_copy(partial, buffer, local)
    load.start()
    meet(neighbours(place))
    sender = Sender(send, recv)
    run(settle_job(place, sender, load, buffer, slots, mid, out))
    sender.finish()


def settle_layer(partial, mid):
    rows, width = partial.shape[-2:]
    return pl.pallas_call(
        settle_kernel,
        name="settle",
        out_shape=jax.ShapeDtypeStruct((RING, rows, width), BF16),
        in_specs=[ANYWHERE, IN_VMEM],
        out_specs=IN_VMEM,
        scratch_shapes=[
            pltpu.VMEM(partial.shape, BF16),
            *copy_sems(3 + SENDS),
            pltpu.SemaphoreType.DMA,
            *third_slots(rows, width),
        ],
        compiler_params=params(3),
    )(partial, mid)


def moe_back_kernel(
    layer, partial, mid, gates, pack0, pack1, d_part, gain_term, router_term, buffer, send, recv, local, *slots
):
    place = Place()
    load = pltpu.make_async_copy(partial, buffer, local)
    load.start()
    meet(neighbours(place))
    sender = Sender(send, recv)
    gain = of_layer(layer, pack0[PACK_ROUTER + 1 : PACK_ROUTER + 2], pack1[PACK_ROUTER + 1 : PACK_ROUTER + 2]).astype(F32)
    router = of_layer(layer, pack0[:PACK_ROUTER], pack1[:PACK_ROUTER])
    load.wait()
    run(reduce(place, sender, thirds(buffer), sort_slots(slots, 3, 3)))
    width = mid.shape[1]
    sums = buffer[place.z, place.y, place.x].astype(F32)
    weights = gates[...]
    d_gates = sums[:, width:]
    d_logits = (weights * (d_gates - jnp.sum(d_gates * weights, axis=-1, keepdims=True))).astype(BF16)
    d_moe_in = sums[:, :width] + dot_nn(d_logits, router)
    mid_rows = mid[...]
    d_mid, terms = rms_back(mid_rows, gain, d_moe_in)
    d_part[place.x] = d_mid.astype(BF16)
    gather_x(place, sender, d_part)
    gain_term[...] = jnp.sum(terms, axis=0, keepdims=True)
    moe_in = (mid_rows * inverse_rms(mid_rows) * gain).astype(BF16)
    router_term[...] = dot_tn(d_logits, moe_in)[: router_term.shape[0]]
    sender.finish()


def moe_back(layer, partial, mid, gates, packs, expert_count):
    rows, width = mid.shape
    return pl.pallas_call(
        functools.partial(moe_back_kernel, layer),
        name="moe_back",
        out_shape=(
            jax.ShapeDtypeStruct((RING, rows, width), BF16),
            jax.ShapeDtypeStruct((1, width), F32),
            jax.ShapeDtypeStruct((expert_count, width), F32),
        ),
        in_specs=[ANYWHERE] + [IN_VMEM] * 4,
        out_specs=(IN_VMEM,) * 3,
        scratch_shapes=[
            pltpu.VMEM(partial.shape, BF16),
            *copy_sems(3 + SENDS),
            pltpu.SemaphoreType.DMA,
            *third_slots(rows, width + GATED),
        ],
        compiler_params=params(5 + layer),
    )(partial, mid, gates, *packs)


TILE = 256


def load_weights(layer, own, other, targets, sems):
    gate, up, down = targets
    half = gate.shape[0] // 2
    section = lax.axis_index("section")

    def pairs(source):
        return [
            (source[0].at[0], gate.at[pl.ds(0, half)]),
            (source[0].at[1], gate.at[pl.ds(half, half)]),
            (source[1].at[0], up.at[pl.ds(0, half)]),
            (source[1].at[1], up.at[pl.ds(half, half)]),
            (source[2].at[0], down.at[pl.ds(0, half)]),
            (source[2].at[1], down.at[pl.ds(half, half)]),
        ]

    @pl.when(section == layer)
    def _():
        for i, (source, target) in enumerate(pairs(own)):
            pltpu.make_async_copy(source, target, sems.at[i]).start()

    @pl.when(section != layer)
    def _():
        for i, (source, target) in enumerate(pairs(other)):
            pltpu.make_async_copy(source, target, sems.at[i]).start()

    return [pltpu.make_async_copy(source, target, sems.at[i]) for i, (source, target) in enumerate(pairs(own))]


def gate_columns(table, half):
    first = 2 * lax.axis_index("expert")
    lanes = lax.broadcasted_iota(jnp.int32, table.shape, 1)
    table = table.astype(F32)
    one = jnp.sum(jnp.where(lanes == first, table, 0.0), axis=1, keepdims=True)
    two = jnp.sum(jnp.where(lanes == first + 1, table, 0.0), axis=1, keepdims=True)
    units = lax.broadcasted_iota(jnp.int32, (table.shape[0], 2 * half), 1)
    return jnp.where(units < half, one, two)


class Stream:
    def __init__(self, hbm, slots, sems, pieces=None):
        self.hbm, self.slots, self.sems = hbm, slots, sems
        self.pieces = pieces

    def copies(self, i, out):
        rows = pl.ds(i * TILE, TILE)
        made = []
        at = 0
        for n, ref in enumerate(self.hbm):
            far, near = ref.at[rows], self.slots.at[i % 2, :, pl.ds(at, ref.shape[1])]
            at += ref.shape[1]
            pair = (near, far) if out else (far, near)
            made.append(pltpu.make_async_copy(*pair, self.sems.at[i % 2, n]))
        return made

    def fetch(self, i):
        for copy in self.copies(i, False):
            copy.start()

    def fetched(self, i):
        for copy in self.copies(i, False):
            copy.wait()
        return self.slots.at[i % 2]

    def store(self, i):
        for copy in self.copies(i, True):
            copy.start()

    def stored(self, i):
        for copy in self.copies(i, True):
            copy.wait()


def stream_scratch(widths, pieces=1):
    scratch = []
    for width in widths:
        scratch += [pltpu.VMEM((2, TILE, width), BF16), pltpu.SemaphoreType.DMA((2, pieces))]
    return scratch


def expert_kernel(
    layer, rows, shared, own0, own1, own2, other0, other1, other2, out, acts, spread,
    gate, up, down, sems, row_slots, row_sems, out_slots, out_sems, act_slots, act_sems, send, recv, local
):
    place = Place()
    met = greet(neighbours(place))
    sender = Sender(send, recv)
    width = out.shape[1]
    units = gate.shape[0]
    tiles = rows.shape[0] // TILE
    weights = load_weights(layer, (own0, own1, own2), (other0, other1, other2), (gate, up, down), sems)
    keep = pltpu.make_async_copy(shared.at[place.x], spread.at[place.z, place.y, place.x], local)
    keep.start()

    def share():
        met()
        columns = shared.shape[2]
        orders = ("xyz", "yzx", "zxy")
        plans = [(spread, order, piece) for order, piece in zip(orders, cut(columns, 2 if layer == 0 else 1))]
        if layer:
            plans = [(spread, "zxy", (0, columns))]
        yield from gather(place, sender, plans, shared.at[place.x], keep.wait)

    job = share()
    ins, outs, kept = Stream([rows], row_slots, row_sems), Stream([out], out_slots, out_sems), Stream([acts], act_slots, act_sems)
    ins.fetch(0)
    for i in range(tiles):
        if i + 1 < tiles:
            ins.fetch(i + 1)
        tile = ins.fetched(i)
        if i == 0:
            for copy in weights:
                copy.wait()
        moe_in = tile[:, :width]
        gate_act = dot_nt(moe_in, gate[...])
        up_act = dot_nt(moe_in, up[...])
        hidden = gate_act / (1.0 + jnp.exp(-gate_act)) * up_act
        hidden = hidden * gate_columns(tile[:, width:], units // 2)
        if i >= 2:
            kept.stored(i - 2)
            outs.stored(i - 2)
        act_slots[i % 2, :, :units] = gate_act.astype(BF16)
        act_slots[i % 2, :, units:] = up_act.astype(BF16)
        out_slots[i % 2] = dot_nn(hidden.astype(BF16), down[...]).astype(BF16)
        kept.store(i)
        outs.store(i)
        next(job, None)
    run(job)
    for i in (tiles - 2, tiles - 1):
        kept.stored(i)
        outs.stored(i)
    sender.finish()


def experts(layer, rows_all, shared, own, other):
    quarter = rows_all.shape[3]
    count = RING**3 * quarter
    width = rows_all.shape[4] - GATED
    units = 2 * own[0].shape[1]
    rows = rows_all.reshape(count, width + GATED)
    out, acts, spread = pl.pallas_call(
        functools.partial(expert_kernel, layer),
        name="experts",
        out_shape=(
            jax.ShapeDtypeStruct((count, width), BF16),
            jax.ShapeDtypeStruct((count, 2 * units), BF16),
            jax.ShapeDtypeStruct((RING, RING, RING, quarter, shared.shape[2]), BF16),
        ),
        in_specs=[ANYWHERE, IN_VMEM] + [ANYWHERE] * 6,
        out_specs=(ANYWHERE,) * 3,
        scratch_shapes=[pltpu.VMEM((units, width), BF16)] * 3
        + [pltpu.SemaphoreType.DMA((6,))]
        + stream_scratch((width + GATED, width, 2 * units))
        + [*copy_sems(SENDS), pltpu.SemaphoreType.DMA],
        compiler_params=params(10 + layer),
    )(rows, shared, *own, *other)
    return out.reshape(*rows_all.shape[:4], width), acts, spread


def expert_back_kernel(layer, pieces, rows, *refs):
    refs = list(refs)

    def take(count):
        taken = refs[:count]
        del refs[:count]
        return taken

    grads, (acts,), own, other = take(pieces), take(1), take(3), take(3)
    extra = take(2 if layer else 6)
    out, grad_in, grad_down = take(3)
    made = take(1 if layer else 4)
    gate, up, down, sum_in, sum_down, sems = take(6)
    row_slots, row_sems, grad_slots, grad_sems, act_slots, act_sems, out_slots, out_sems, send, recv, local = take(11)
    place = Place()
    peer = place.peer()
    width = grad_in.shape[1]
    units = gate.shape[0]
    tiles = rows.shape[0] // TILE
    handed = None
    if layer:
        met = greet(neighbours(place))
        sender = Sender(send, recv)
        partial, mid = extra
        (settled,) = made
        buffer, *slots = refs
        load = pltpu.make_async_copy(partial, buffer, local.at[0])
        load.start()

        def side():
            met()
            yield from settle_job(place, sender, load, buffer, slots, mid, settled)

        job = side()
    else:
        met = greet([peer, *neighbours(place, "yz")])
        upper = place.section == 1
        sender = Sender(send, recv, upper)
        first_own, second_own, got_in, got_down = made
        stacks, (first, second), slots = refs[:4], refs[4:6], refs[6:]
        loads = [pltpu.make_async_copy(*pair, local.at[i]) for i, pair in enumerate(zip(extra[:4], stacks))]
        for copy in loads:
            copy.start()
        handing = Sender(refs[-2], refs[-1])
        slots = refs[6:-2]

        def side():
            for copy in loads:
                copy.wait()
            pl.when(upper)(lambda: gradient_products(*stacks, first, second))
            met()
            state["handed"] = handing.hand(place.section == 0, [(extra[4], got_in), (extra[5], got_down)], peer)
            yield from reduce(place, sender, gradient_plans(first, second), sort_slots(slots, 2, 2))
            first_own[...] = first[place.z, place.y]
            second_own[...] = second[place.z, place.y]

        state = {}
        job = side()

    weights = load_weights(layer, own, other, (gate, up, down), sems)
    ins, ups = Stream([rows], row_slots, row_sems), Stream(grads, grad_slots, grad_sems)
    kept, outs = Stream([acts], act_slots, act_sems), Stream([out], out_slots, out_sems)
    for stream in (ins, ups, kept):
        stream.fetch(0)
    first_expert = 2 * lax.axis_index("expert")
    for i in range(tiles):
        for stream in (ins, ups, kept):
            if i + 1 < tiles:
                stream.fetch(i + 1)
        tile, grad, act = ins.fetched(i), ups.fetched(i)[...], kept.fetched(i)
        if i == 0:
            for copy in weights:
                copy.wait()
        gates = gate_columns(tile[:, width:], units // 2)
        back = dot_nt(grad, down[...])
        gate_act = act[:, :units].astype(F32)
        up_act = act[:, units:].astype(F32)
        sigmoid = 1.0 / (1.0 + jnp.exp(-gate_act))
        silu = gate_act * sigmoid
        hidden = silu * up_act
        products = hidden * back
        in_one = lax.broadcasted_iota(jnp.int32, products.shape, 1) < units // 2
        one = jnp.sum(jnp.where(in_one, products, 0.0), axis=1, keepdims=True)
        two = jnp.sum(jnp.where(in_one, 0.0, products), axis=1, keepdims=True)
        lanes = lax.broadcasted_iota(jnp.int32, (products.shape[0], GATED), 1)
        d_gates = jnp.where(lanes == first_expert, one, jnp.where(lanes == first_expert + 1, two, 0.0))
        d_hidden = back * gates
        d_gate = (d_hidden * up_act * sigmoid * (1.0 + gate_act * (1.0 - sigmoid))).astype(BF16)
        d_up = (d_hidden * silu).astype(BF16)
        if i >= 2:
            outs.stored(i - 2)
        out_slots[i % 2, :, :width] = (dot_nn(d_gate, gate[...]) + dot_nn(d_up, up[...])).astype(BF16)
        out_slots[i % 2, :, width:] = d_gates.astype(BF16)
        outs.store(i)
        moe_in = tile[:, :width]
        terms = (
            (sum_in, slice(0, units), dot_tn(d_gate, moe_in)),
            (sum_in, slice(units, 2 * units), dot_tn(d_up, moe_in)),
            (sum_down, slice(0, units), dot_tn((hidden * gates).astype(BF16), grad)),
        )
        for total, at, term in terms:
            if i == 0:
                total[at] = term
            elif i < tiles - 1:
                total[at] += term
            else:
                low = grad_in if total is sum_in else grad_down
                low[at] = (total[at] + term).astype(BF16)
        next(job, None)
    run(job)
    for i in (tiles - 2, tiles - 1):
        outs.stored(i)
    sender.finish()
    if not layer:
        state["handed"]()


def experts_back(layer, rows_all, grads_all, acts, own, other, extra):
    quarter = rows_all.shape[3]
    count = RING**3 * quarter
    width = rows_all.shape[4] - GATED
    units = 2 * own[0].shape[1]
    grads = [g.reshape(count, g.shape[-1]) for g in grads_all]
    if layer:
        partial, mid = extra
        extra = (partial, mid)
        extra_specs, made_specs = [ANYWHERE, IN_VMEM], (IN_VMEM,)
        made = (jax.ShapeDtypeStruct((RING, quarter, width), BF16),)
        scratch = [
            *copy_sems(3 + SENDS),
            pltpu.SemaphoreType.DMA((1,)),
            pltpu.VMEM(partial.shape, BF16),
            *third_slots(quarter, width),
        ]
    else:
        factors, grads_one, dense = extra
        first, second = gradient_shapes(dense)
        normed, proj, heads, mids = factors
        extra = (normed, proj, heads, mids, *grads_one)
        extra_specs, made_specs = [ANYWHERE] * 6, (IN_VMEM, IN_VMEM, ANYWHERE, ANYWHERE)
        made = (
            jax.ShapeDtypeStruct(first[2:], BF16),
            jax.ShapeDtypeStruct(second[2:], BF16),
            jax.ShapeDtypeStruct(grads_one[0].shape, BF16),
            jax.ShapeDtypeStruct(grads_one[1].shape, BF16),
        )
        scratch = [
            *copy_sems(18),
            pltpu.SemaphoreType.DMA((4,)),
            *[pltpu.VMEM(f.shape, BF16) for f in factors],
            pltpu.VMEM(first, BF16),
            pltpu.VMEM(second, BF16),
            *gradient_slots(first, second),
            *copy_sems(2),
        ]
    out, *rest = pl.pallas_call(
        functools.partial(expert_back_kernel, layer, len(grads)),
        name="experts_back",
        out_shape=(
            jax.ShapeDtypeStruct((count, width + GATED), BF16),
            jax.ShapeDtypeStruct((2 * units, width), BF16),
            jax.ShapeDtypeStruct((units, width), BF16),
            *made,
        ),
        in_specs=[ANYWHERE] * (1 + len(grads) + 1 + 6) + extra_specs,
        out_specs=(ANYWHERE, IN_VMEM, IN_VMEM, *made_specs),
        scratch_shapes=[pltpu.VMEM((units, width), BF16)] * 3
        + [pltpu.VMEM((2 * units, width), F32), pltpu.VMEM((units, width), F32), pltpu.SemaphoreType.DMA((6,))]
        + stream_scratch((width + GATED,))
        + stream_scratch((width,), len(grads))
        + stream_scratch((2 * units, width + GATED))
        + scratch,
        compiler_params=params(12 + layer),
    )(rows_all.reshape(count, width + GATED), *grads, acts, *own, *other, *extra)
    return (out.reshape(*rows_all.shape), *rest)


def pull(layer, own, other, targets, sems):
    section = lax.axis_index("section")

    @pl.when(section == layer)
    def _():
        for i, (source, target) in enumerate(zip(own, targets)):
            pltpu.make_async_copy(source, target, sems.at[i]).start()

    @pl.when(section != layer)
    def _():
        for i, (source, target) in enumerate(zip(other, targets)):
            pltpu.make_async_copy(source, target, sems.at[i]).start()

    return [pltpu.make_async_copy(source, target, sems.at[i]) for i, (source, target) in enumerate(zip(own, targets))]


def of_layer(layer, own, other):
    return jnp.where(lax.axis_index("section") == layer, own, other)


def tables(seg_column, seg_row, dim):
    rows = seg_column.shape[0]
    at_row = lax.broadcasted_iota(jnp.int32, (rows, rows), 0)
    at_column = lax.broadcasted_iota(jnp.int32, (rows, rows), 1)
    earlier = jnp.sum((seg_row < seg_column).astype(F32), axis=1, keepdims=True)
    position = lax.broadcasted_iota(jnp.int32, (rows, dim), 0).astype(F32) - earlier
    lane = lax.broadcasted_iota(jnp.int32, (rows, dim), 1)
    half = dim // 2
    place = jnp.where(lane < half, lane, lane - half).astype(F32)
    angle = position * jnp.exp(place * (-math.log(THETA) / half))
    sine = jnp.sin(angle)
    return jnp.cos(angle), jnp.where(lane < half, -sine, sine), (seg_row == seg_column) & (at_column <= at_row)


def turn(rows, cosine, sine):
    return rows * cosine + pltpu.roll(rows, rows.shape[1] // 2, 1) * sine


def turn_back(grad, cosine, sine):
    return grad * cosine + pltpu.roll(grad * sine, grad.shape[1] // 2, 1)


PACK_ROUTER = 128
PACK_ROWS = 144
HEADS_STEP = 2


def attend_mix_kernel(
    layer, rows, seg_column, seg_row, pack0, pack1, routes0, routes1, q0, k0, v0, o0, q1, k1, v1, o1,
    attended, query_raw, key_raw, value_low, mid, gates, rows_all,
    wq, wk, wv, wo, total, part, own, slots, sems, send, recv, local
):
    place = Place()
    met = greet(neighbours(place))
    dim = wk.shape[1]
    heads = wq.shape[1] // dim
    step = HEADS_STEP * dim
    steps = heads // HEADS_STEP

    def pieces(q, k, v, o):
        columns = [q.at[:, pl.ds(i * step, step)] for i in range(steps)]
        return [k, v, *columns, *[o.at[pl.ds(i * step, step)] for i in range(steps)]]

    loads = pull(layer, pieces(q0, k0, v0, o0), pieces(q1, k1, v1, o1), pieces(wq, wk, wv, wo), sems)
    resid = rows[...].astype(F32)
    gain = of_layer(layer, pack0[PACK_ROUTER : PACK_ROUTER + 1], pack1[PACK_ROUTER : PACK_ROUTER + 1]).astype(F32)
    gains = of_layer(layer, pack0[PACK_ROUTER + 2 : PACK_ROUTER + 3], pack1[PACK_ROUTER + 2 : PACK_ROUTER + 3]).astype(F32)
    gain_query, gain_key = gains[:, :dim], gains[:, dim : 2 * dim]
    cosine, sine, allowed = tables(seg_column[...], seg_row[...], dim)
    normed = (resid * inverse_rms(resid) * gain).astype(BF16)
    loads[0].wait()
    raw = dot_nn(normed, wk[...])
    key_raw[...] = raw
    key = turn(raw * inverse_rms(raw) * gain_key, cosine, sine).astype(BF16)
    loads[1].wait()
    value = dot_nn(normed, wv[...]).astype(BF16)
    value_low[...] = value
    for i in range(steps):
        loads[2 + i].wait()
        raws = dot_nn(normed, wq[:, i * step : (i + 1) * step])
        query_raw[:, i * step : (i + 1) * step] = raws
        for h in range(HEADS_STEP):
            raw = raws[:, h * dim : (h + 1) * dim]
            query = turn(raw * inverse_rms(raw) * gain_query, cosine, sine).astype(BF16)
            scores = jnp.where(allowed, dot_nt(query, key) * (1.0 / math.sqrt(dim)), MASKED)
            raised = jnp.exp(scores - jnp.max(scores, axis=1, keepdims=True))
            probs = (raised / jnp.sum(raised, axis=1, keepdims=True)).astype(BF16)
            at = i * step + h * dim
            attended[:, at : at + dim] = dot_nn(probs, value).astype(BF16)
        loads[2 + steps + i].wait()
        piece = dot_nn(attended[:, i * step : (i + 1) * step], wo[i * step : (i + 1) * step])
        if i == 0:
            total[...] = piece
        else:
            total[...] += piece
    quarter = part.shape[1]
    for i in range(part.shape[0]):
        part[i] = total[i * quarter : (i + 1) * quarter].astype(BF16)
        total[i * quarter : (i + 1) * quarter] = resid[i * quarter : (i + 1) * quarter]
    sender = Sender(send, recv)
    met()
    copies = send_x(place, sender, part, slots)
    chosen = of_layer(layer, routes0[place.x], routes1[place.x])
    lanes = lax.broadcasted_iota(jnp.int32, gates.shape, 1)
    named = chosen[:, 0:1] == lanes
    for i in range(1, chosen.shape[1]):
        named = named | (chosen[:, i : i + 1] == lanes)
    gain = of_layer(layer, pack0[PACK_ROUTER + 1 : PACK_ROUTER + 2], pack1[PACK_ROUTER + 1 : PACK_ROUTER + 2])
    router = of_layer(layer, pack0[:PACK_ROUTER], pack1[:PACK_ROUTER])
    mine = total[pl.ds(pl.multiple_of(place.x * quarter, 8), quarter)]
    mid_rows = mine + sum_x(place, copies, part, slots)
    mid[...] = mid_rows
    moe_in = (mid_rows * inverse_rms(mid_rows) * gain.astype(F32)).astype(BF16)
    logits = jnp.where(named, dot_nt(moe_in, router), MASKED)
    raised = jnp.where(named, jnp.exp(logits - jnp.max(logits, axis=-1, keepdims=True)), 0.0)
    weights = raised / jnp.sum(raised, axis=-1, keepdims=True)
    gates[...] = weights
    own[:, : moe_in.shape[1]] = moe_in
    own[:, moe_in.shape[1] :] = weights.astype(BF16)
    keep = pltpu.make_async_copy(own, rows_all.at[place.z, place.y, place.x], local)
    keep.start()
    run(gather(place, sender, thirds(rows_all), own, keep.wait))
    sender.finish()


def weight_scratch(dense):
    return [pltpu.VMEM(w.shape, BF16) for w in dense]


def attend_mix(layer, rows, segs, packs, routes, own, other):
    count, width = rows.shape
    quarter = count // RING
    dim, inner = own[1].shape[1], own[0].shape[1]
    return pl.pallas_call(
        functools.partial(attend_mix_kernel, layer),
        name="attend_mix",
        out_shape=(
            jax.ShapeDtypeStruct((count, inner), BF16),
            jax.ShapeDtypeStruct((count, inner), F32),
            jax.ShapeDtypeStruct((count, dim), F32),
            jax.ShapeDtypeStruct((count, dim), BF16),
            jax.ShapeDtypeStruct((quarter, width), F32),
            jax.ShapeDtypeStruct((quarter, GATED), F32),
            jax.ShapeDtypeStruct((RING, RING, RING, quarter, width + GATED), BF16),
        ),
        in_specs=[IN_VMEM] * 7 + [ANYWHERE] * 8,
        out_specs=(IN_VMEM,) * 6 + (ANYWHERE,),
        scratch_shapes=[
            *weight_scratch(own),
            pltpu.VMEM((count, width), F32),
            pltpu.VMEM((RING, quarter, width), BF16),
            pltpu.VMEM((quarter, width + GATED), BF16),
            pltpu.VMEM((3, quarter, width), BF16),
            pltpu.SemaphoreType.DMA((2 + 2 * (inner // dim // HEADS_STEP),)),
            *copy_sems(3 + SENDS),
            pltpu.SemaphoreType.DMA,
        ],
        compiler_params=params(1 + layer),
    )(rows, *segs, *packs, *routes, *own, *other)


SMALL = 48


def gradient_shapes(dense):
    width, inner = dense[0].shape
    proj = inner + 2 * dense[1].shape[1]
    blocks = RING * RING
    return (RING, RING, width // blocks, proj), (RING, RING, inner // blocks, width)


def gradient_plans(first, second):
    return [(first, "yz", (0, first.shape[-1])), (second, "zy", (0, second.shape[-1]))]


def gradient_slots(first, second):
    return slot_scratch([(first[2], 2, (0, first[3])), (second[2], 2, (0, second[3]))])


def gradient_products(normed, proj, heads, mids, first, second):
    lanes = 128

    def output_blocks(i, _):
        pair = dot_tn(heads[:, pl.ds(pl.multiple_of(i * lanes, lanes), lanes)], mids[...]).astype(BF16)
        half = lanes // 2
        at = 2 * i
        second[lax.div(at, RING), lax.rem(at, RING)] = pair[:half]
        second[lax.div(at, RING), lax.rem(at, RING) + 1] = pair[half:]
        return 0

    def input_blocks(i, _):
        block = dot_tn(normed[:, pl.ds(pl.multiple_of(i * lanes, lanes), lanes)], proj[...])
        first[lax.div(i, RING), lax.rem(i, RING)] = block.astype(BF16)
        return 0

    lax.fori_loop(0, heads.shape[1] // lanes, output_blocks, 0)
    lax.fori_loop(0, normed.shape[1] // lanes, input_blocks, 0)


def attend_back_kernel(
    layer, rows, seg_column, seg_row, pack0, pack1, attended, query_raw, key_raw, value_low, upstream, d_part,
    router_term, moe_gain_term, *refs
):
    last = layer == 0
    refs = list(refs)
    extra = [refs.pop(0) for _ in range(4 if last else 0)]
    q0, k0, v0, o0, q1, k1, v1, o1, d_input, normed_both, d_proj, heads_both, d_mid_low, smalls = refs[:14]
    refs = refs[14:]
    wide = [refs.pop(0) for _ in range(4 if last else 0)]
    wq, wk, wv, wo, total, d_mid, d_heads, part, own, slots, sems, send, recv, local, *side = refs
    place = Place()
    peer = place.peer()
    met = greet([peer, *neighbours(place)])
    count = rows.shape[0]
    job = iter(())
    if last:
        upper = place.section == 1
        first_own, second_own, grad_in, grad_down = extra
        first, second, got_in, got_down = wide
        side_sender = Sender(side[0], side[1], upper)
        handing = Sender(side[2], side[3])

        def widen():
            first[place.z, place.y] = first_own[...]
            second[place.z, place.y] = second_own[...]
            yield
            met()
            yield from gather(place, side_sender, gradient_plans(first, second))

        job = widen()
    dim = wk.shape[1]
    heads = wq.shape[1] // dim
    inner = heads * dim
    step = HEADS_STEP * dim
    steps = heads // HEADS_STEP
    quarter = d_part.shape[1]

    def pieces(q, k, v, o):
        return [*[o.at[pl.ds(i * step, step)] for i in range(steps)],
                *[q.at[:, pl.ds(i * step, step)] for i in range(steps)], k, v]

    loads = pull(layer, pieces(q0, k0, v0, o0), pieces(q1, k1, v1, o1), pieces(wq, wk, wv, wo), sems)
    for i in range(RING):
        grad = upstream[i].astype(F32) + d_part[i].astype(F32)
        d_mid[i] = grad
        total[i * quarter : (i + 1) * quarter] = grad
    grad_low = total[...].astype(BF16)
    d_mid_low[:count] = grad_low
    heads_both[:count] = attended[...]
    resid = rows[...].astype(F32)
    gain = of_layer(layer, pack0[PACK_ROUTER : PACK_ROUTER + 1], pack1[PACK_ROUTER : PACK_ROUTER + 1]).astype(F32)
    gains = of_layer(layer, pack0[PACK_ROUTER + 2 : PACK_ROUTER + 3], pack1[PACK_ROUTER + 2 : PACK_ROUTER + 3]).astype(F32)
    gain_query, gain_key = gains[:, :dim], gains[:, dim : 2 * dim]
    cosine, sine, allowed = tables(seg_column[...], seg_row[...], dim)
    normed_both[:count] = (resid * inverse_rms(resid) * gain).astype(BF16)
    raw_key = key_raw[...]
    key = turn(raw_key * inverse_rms(raw_key) * gain_key, cosine, sine).astype(BF16)
    value = value_low[...]
    scale = 1.0 / math.sqrt(dim)
    d_key = jnp.zeros(key.shape, F32)
    d_value = jnp.zeros(key.shape, F32)
    gain_total = jnp.zeros(gain_query.shape, F32)
    handed_grads = None
    for i in range(steps):
        next(job, None)
        if last and i == 1:
            handed_grads = handing.hand(upper, [(grad_in, got_in), (grad_down, got_down)], peer)
        loads[i].wait()
        d_heads[...] = dot_nt(grad_low, wo[i * step : (i + 1) * step]).astype(BF16)
        for h in range(HEADS_STEP):
            at = i * step + h * dim
            raw = query_raw[:, at : at + dim]
            query = turn(raw * inverse_rms(raw) * gain_query, cosine, sine).astype(BF16)
            scores = jnp.where(allowed, dot_nt(query, key) * scale, MASKED)
            raised = jnp.exp(scores - jnp.max(scores, axis=1, keepdims=True))
            probs = raised / jnp.sum(raised, axis=1, keepdims=True)
            d_head = d_heads[:, h * dim : (h + 1) * dim]
            d_probs = dot_nt(d_head, value)
            d_value = d_value + dot_tn(probs.astype(BF16), d_head)
            d_scores = (probs * (d_probs - jnp.sum(d_probs * probs, axis=1, keepdims=True))).astype(BF16)
            d_query = turn_back(dot_nn(d_scores, key) * scale, cosine, sine)
            d_key = d_key + dot_tn(d_scores, query) * scale
            d_raw, terms = rms_back(raw, gain_query, d_query)
            gain_total = gain_total + jnp.sum(terms, axis=0, keepdims=True)
            d_proj[:count, at : at + dim] = d_raw.astype(BF16)
        loads[steps + i].wait()
        piece = dot_nt(d_proj[:count, i * step : (i + 1) * step], wq[:, i * step : (i + 1) * step])
        if i == 0:
            total[...] = piece
        else:
            total[...] += piece
    d_raw, terms = rms_back(raw_key, gain_key, turn_back(d_key, cosine, sine))
    d_proj[:count, inner : inner + dim] = d_raw.astype(BF16)
    d_proj[:count, inner + dim :] = d_value.astype(BF16)
    smalls[0, 32:] = jnp.zeros((SMALL - 32, smalls.shape[2]), F32)
    smalls[0, :32] = router_term[...]
    smalls[0, 32:33] = moe_gain_term[...]
    smalls[0, 34:35, :dim] = gain_total
    smalls[0, 34:35, dim : 2 * dim] = jnp.sum(terms, axis=0, keepdims=True)
    loads[2 * steps].wait()
    loads[2 * steps + 1].wait()
    total[...] += dot_nt(d_proj[:count, inner : inner + dim], wk[...]) + dot_nt(d_proj[:count, inner + dim :], wv[...])
    for i in range(RING):
        part[i] = total[i * quarter : (i + 1) * quarter].astype(BF16)
    sender = Sender(send, recv)
    if not last:
        met()
    copies = send_x(place, sender, part, slots)
    theirs = pl.ds(count, count)
    ours = pl.ds(0, count)
    handed = sender.hand(
        place.section != layer,
        [(ref.at[ours], ref.at[theirs]) for ref in (normed_both, d_proj, heads_both, d_mid_low)],
        peer,
    )
    mine = resid[:quarter]
    for i in range(1, RING):
        mine = jnp.where(place.x == i, resid[i * quarter : (i + 1) * quarter], mine)
    d_resid, terms = rms_back(mine, gain, sum_x(place, copies, part, slots))
    smalls[0, 33:34] = jnp.sum(terms, axis=0, keepdims=True)
    handed_small = sender.hand(place.section != layer, [(smalls.at[0], smalls.at[1])], peer)
    d_rows = (d_mid[place.x] + d_resid).astype(BF16)
    if last:
        d_input[place.x] = d_rows
        gather_x(place, sender, d_input)
    else:
        own[...] = d_rows
        keep = pltpu.make_async_copy(own, d_input.at[place.z, place.y, place.x], local)
        keep.start()
        run(gather(place, sender, thirds(d_input), own, keep.wait))
    handed()
    handed_small()
    sender.finish()
    if last:
        run(job)
        handed_grads()
        side_sender.finish()


def attend_back(layer, rows, segs, packs, saved, upstream, d_part, terms, extra, own, other):
    last = layer == 0
    wide, side = (), ()
    if last:
        first, second = gradient_shapes(own)
        wide = tuple(jax.ShapeDtypeStruct(shape, BF16) for shape in (first, second, extra[2].shape, extra[3].shape))
        side = (*copy_sems(18), *copy_sems(2))
    count, width = rows.shape
    quarter = count // RING
    dim, inner = own[1].shape[1], own[0].shape[1]
    out = (RING, quarter, width) if layer == 0 else (RING, RING, RING, quarter, width)
    return pl.pallas_call(
        functools.partial(attend_back_kernel, layer),
        name="attend_back_last" if layer == 0 else "attend_back",
        out_shape=(
            jax.ShapeDtypeStruct(out, BF16),
            jax.ShapeDtypeStruct((2 * count, width), BF16),
            jax.ShapeDtypeStruct((2 * count, inner + 2 * dim), BF16),
            jax.ShapeDtypeStruct((2 * count, inner), BF16),
            jax.ShapeDtypeStruct((2 * count, width), BF16),
            jax.ShapeDtypeStruct((2, SMALL, width), F32),
            *wide,
        ),
        in_specs=[IN_VMEM] * 13 + ([IN_VMEM] * 2 + [ANYWHERE] * 2 if last else []) + [ANYWHERE] * 8,
        out_specs=(IN_VMEM if last else ANYWHERE,) + (IN_VMEM,) * (7 if last else 5) + (ANYWHERE,) * (2 if last else 0),
        scratch_shapes=[
            *weight_scratch(own),
            pltpu.VMEM((count, width), F32),
            pltpu.VMEM((RING, quarter, width), F32),
            pltpu.VMEM((count, HEADS_STEP * dim), BF16),
            pltpu.VMEM((RING, quarter, width), BF16),
            pltpu.VMEM((quarter, width), BF16),
            pltpu.VMEM((3, quarter, width), BF16),
            pltpu.SemaphoreType.DMA((2 + 2 * (inner // dim // HEADS_STEP),)),
            *copy_sems(3 + 5 + (3 if layer == 0 else SENDS)),
            pltpu.SemaphoreType.DMA,
            *side,
        ],
        compiler_params=params(7 + layer),
    )(rows, *segs, *packs, *saved, upstream, d_part, *terms, *extra, *own, *other)


def finish_kernel(
    normed0, proj0, heads0, mids0, small0, small1, first_one, second_one, out0, out1, ig0, ig1,
    first, second, small_out, outputs, input_grads,
    first_sums, second_sums, normed, proj, heads, mids, terms, passing, small_slots, send, recv, flagged_send,
    flagged_recv, local, *slots
):
    place = Place()
    lower = place.section == 0
    upper = place.section == 1
    peer = place.peer()
    met = greet([peer, *neighbours(place)])
    sender = Sender(send, recv)
    reducer = Sender(flagged_send, flagged_recv, lower)

    def keep(index, source, otherwise, target):
        one, two = (pltpu.make_async_copy(origin, target, local.at[index]) for origin in (source, otherwise))
        pl.when(lower)(one.start)
        pl.when(upper)(two.start)
        return one

    pairs = ((small0, small1, terms), (out0, out1, outputs.at[place.section]), (ig0, ig1, input_grads.at[place.section]))
    kept = [keep(i, *pair) for i, pair in enumerate(pairs)]
    loads = ((normed0, normed), (proj0, proj), (heads0, heads), (mids0, mids))
    loads = [pltpu.make_async_copy(*pair, local.at[3 + i]) for i, pair in enumerate(loads)]
    ready = [
        pltpu.make_async_copy(*pair, local.at[7 + i]) for i, pair in enumerate(((first_one, first), (second_one, second)))
    ]

    @pl.when(upper)
    def _():
        for copy in ready:
            copy.start()

    @pl.when(lower)
    def _():
        for copy in loads:
            copy.start()
        for copy in loads:
            copy.wait()
        gradient_products(normed, proj, heads, mids, first_sums, second_sums)

    for copy in kept:
        copy.wait()
    met()
    state = {}

    def exchange(step, total):
        passing[...] = total
        buffer = small_slots.at[step, 3]
        buffer[...] = total.astype(BF16)
        state["copies"] = [
            sender.send(buffer, small_slots.at[step, i], place.device("xyz"[step], delta))
            for i, delta in enumerate((1, -1, 2))
        ]

    def collect(step):
        for copy in state["copies"]:
            copy.wait_recv()
        total = passing[...]
        for i in range(3):
            total = total + small_slots[step, i].astype(F32)
        return total

    def small_last():
        small_out[...] = collect(2)

    def swap_rows():
        state["late"] = [
            sender.send_either(lower, out1, out0, outputs.at[place.section], peer),
            sender.send_either(lower, ig1, ig0, input_grads.at[place.section], peer),
        ]
        exchange(0, terms[0] + terms[1])

    def second_step():
        exchange(1, collect(0))

    plans = gradient_plans(first_sums, second_sums)
    run(reduce(place, reducer, plans, sort_slots(slots, 2, 2), (swap_rows, second_step)))

    @pl.when(lower)
    def _():
        first[place.z, place.y] = first_sums[place.z, place.y]
        second[place.z, place.y] = second_sums[place.z, place.y]

    beside = (lambda: exchange(2, collect(1)), small_last)
    run(gather(place, reducer, gradient_plans(first, second), None, None, beside))
    for copy in state["late"]:
        copy.wait_recv()

    @pl.when(upper)
    def _():
        for copy in ready:
            copy.wait()

    sender.finish()
    reducer.finish()


def finish(factors, smalls, ready, outs, input_grads):
    rows, width = factors[0].shape
    first, second = ready[0].shape, ready[1].shape
    both = (2, *outs[0].shape)
    return pl.pallas_call(
        finish_kernel,
        name="finish",
        out_shape=(
            jax.ShapeDtypeStruct(first, BF16),
            jax.ShapeDtypeStruct(second, BF16),
            jax.ShapeDtypeStruct(smalls[0].shape[1:], F32),
            jax.ShapeDtypeStruct(both, BF16),
            jax.ShapeDtypeStruct(both, BF16),
        ),
        in_specs=[ANYWHERE] * 12,
        out_specs=(IN_VMEM,) * 3 + (ANYWHERE,) * 2,
        scratch_shapes=[
            pltpu.VMEM(first, BF16),
            pltpu.VMEM(second, BF16),
            *[pltpu.VMEM(f.shape, BF16) for f in factors],
            pltpu.VMEM(smalls[0].shape, F32),
            pltpu.VMEM(smalls[0].shape[1:], F32),
            pltpu.VMEM((3, 4, *smalls[0].shape[1:]), BF16),
            *copy_sems(2 + 9),
            *copy_sems(36),
            pltpu.SemaphoreType.DMA((9,)),
            *gradient_slots(first, second),
        ],
        compiler_params=params(9),
    )(*factors, *smalls, *ready, *outs, *input_grads)


def swap(vector):
    return lax.ppermute(vector, "section", [(0, 1), (1, 0)])


def body(
    block_input,
    cotangent,
    segments,
    routes,
    norm_attn,
    w_query,
    key_matrix,
    value_matrix,
    norm_query,
    norm_key,
    w_output,
    norm_moe,
    w_router,
    w_gate,
    w_up,
    w_down,
):
    section = lax.axis_index("section")
    lower = section == 0
    _, group_rows, width = block_input.shape
    expert_count = w_router.shape[2]
    quarter = group_rows // RING
    dim = norm_query.shape[1]

    dense_own = (w_query[0], key_matrix[0], value_matrix[0], w_output[0])
    expert_own = (jnp.swapaxes(w_gate[0], 1, 2), jnp.swapaxes(w_up[0], 1, 2), w_down[0])
    pack_own = jnp.concatenate(
        [
            jnp.pad(w_router[0].T, ((0, PACK_ROUTER - expert_count), (0, 0))),
            norm_attn,
            norm_moe,
            jnp.pad(jnp.concatenate([norm_query, norm_key], axis=1), ((0, PACK_ROWS - PACK_ROUTER - 3), (0, width - 2 * dim))),
        ],
        axis=0,
    )
    routes_own = lax.dynamic_index_in_dim(routes[0], section, 0, keepdims=False)
    routes_other = swap(lax.dynamic_index_in_dim(routes[0], 1 - section, 0, keepdims=False))
    packs = (pack_own, swap(pack_own))
    dense_other = tuple(swap(w) for w in dense_own)
    expert_other = tuple(swap(w) for w in expert_own)
    chosen = tuple(r.reshape(RING, quarter, r.shape[-1]) for r in (routes_own, routes_other))

    def pick(array):
        return lax.dynamic_index_in_dim(array, section, 0, keepdims=False)

    def quarters(array):
        return array.reshape(RING, quarter, array.shape[-1])

    segment = pick(segments)
    segs = (segment.reshape(group_rows, 1), segment.reshape(1, group_rows))

    rows_in = pick(block_input)
    upstream = quarters(pick(cotangent))
    edge = 2 * GATED * ((width // GATED) // 3)
    shared = (upstream[:, :, :edge], upstream[:, :, edge:])
    saved, layer_ins, outs, grads_all = [], [], [], []
    for layer in range(2):
        layer_ins.append(rows_in)
        *attn_saved, mid, gates, rows_all = attend_mix(layer, rows_in, segs, packs, chosen, dense_own, dense_other)
        partial, acts, spread = experts(layer, rows_all, shared[layer], expert_own, expert_other)
        grads_all.append(spread)
        saved.append((attn_saved, mid, gates, rows_all, acts))
        if layer == 0:
            out = settle_layer(partial, mid)
            rows_in = out.reshape(group_rows, width)
            outs.append(out)

    attn_saved, mid, gates, rows_all, acts = saved[1]
    partial, *grads_one, out = experts_back(1, rows_all, grads_all, acts, expert_own, expert_other, (partial, mid))
    outs.append(out)
    d_part, *terms = moe_back(1, partial, mid, gates, packs, expert_count)
    d_all, *factors_one, smalls_one = attend_back(
        1, layer_ins[1], segs, packs, attn_saved, upstream, d_part, terms[::-1], (), dense_own, dense_other
    )
    upstream = lax.dynamic_index_in_dim(
        d_all.reshape(RING * RING, RING, quarter, width), lax.axis_index("expert"), 0, keepdims=False
    )
    input_grads = [None, upstream]
    attn_saved, mid, gates, rows_all, acts = saved[0]
    partial, *grads_zero, first_own, second_own, got_in_one, got_down_one = experts_back(
        0, rows_all, [d_all], acts, expert_own, expert_other, (factors_one, grads_one, dense_own)
    )
    d_part, *terms = moe_back(0, partial, mid, gates, packs, expert_count)
    input_grads[0], *factors_zero, smalls_zero, first_one, second_one, got_in_zero, got_down_zero = attend_back(
        0, layer_ins[0], segs, packs, attn_saved, upstream, d_part, terms[::-1],
        (first_own, second_own, *grads_zero), dense_own, dense_other,
    )
    expert_grads = ((*grads_zero, got_in_zero, got_down_zero), (*grads_one, got_in_one, got_down_one))
    first, second, small, outputs, d_inputs = finish(
        factors_zero, (smalls_zero, smalls_one), (first_one, second_one), outs, input_grads
    )
    inner = w_query.shape[2]
    projections = first.reshape(width, first.shape[-1]).astype(F32)[None]

    def total(index):
        mine, theirs = [
            jnp.where(lower, expert_grads[0][i], expert_grads[1][i]).astype(F32) for i in (index, index + 2)
        ]
        return mine + theirs

    grad_in, grad_down = total(0), total(1)
    units = w_gate.shape[3]
    grad_in = grad_in.reshape(2, 2, units, width)
    return (
        outputs.reshape(1, 2, group_rows, width),
        d_inputs.astype(F32).reshape(1, 2, group_rows, width),
        small[33:34],
        projections[:, :, :inner],
        projections[:, :, inner : inner + dim],
        projections[:, :, inner + dim :],
        small[34:35, :dim],
        small[34:35, dim : 2 * dim],
        second.reshape(inner, width).astype(F32)[None],
        small[32:33],
        small[:expert_count].T[None],
        jnp.swapaxes(grad_in[0], 1, 2)[None],
        jnp.swapaxes(grad_in[1], 1, 2)[None],
        grad_down.reshape(1, 2, units, width),
    )


def solution(mesh):
    placed = (
        P(None, "expert", None),
        P(None, "expert", None),
        P(None, "expert", None),
        P("section", None, "expert", None),
        P("section", None),
        P("section", None, "tensor"),
        P("section", None, "tensor"),
        P("section", None, "tensor"),
        P("section", None),
        P("section", None),
        P("section", "tensor", None),
        P("section", None),
        P("section", None, None),
        P("section", "expert", None, "tensor"),
        P("section", "expert", None, "tensor"),
        P("section", "expert", "tensor", None),
    )
    return jax.shard_map(
        body,
        mesh=mesh,
        in_specs=placed,
        out_specs=(
            P("section", None, "expert", None),
            P("section", None, "expert", None),
            P("section", None),
            P("section", None, "tensor"),
            P("section", None, "tensor"),
            P("section", None, "tensor"),
            P("section", None),
            P("section", None),
            P("section", "tensor", None),
            P("section", None),
            P("section", None, None),
            P("section", "expert", None, "tensor"),
            P("section", "expert", None, "tensor"),
            P("section", "expert", "tensor", None),
        ),
        check_vma=False,
    )
```

```python
import functools
import math

import jax
import jax.numpy as jnp
from jax import lax
from jax.experimental import pallas as pl
from jax.experimental.pallas import tpu as pltpu
from jax.sharding import PartitionSpec as P

RING = 4
BF16 = jnp.bfloat16
F32 = jnp.float32


def wrap(value):
    return lax.rem(value + 2 * RING, RING)


class Place:
    def __init__(self):
        self.section = lax.axis_index("section")
        expert = lax.axis_index("expert")
        self.x = lax.axis_index("tensor")
        self.z = lax.div(expert, RING)
        self.y = lax.rem(expert, RING)

    def index(self, axis):
        return getattr(self, axis)

    def device(self, axis, delta):
        at = {"x": self.x, "y": self.y, "z": self.z}
        at[axis] = wrap(at[axis] + delta)
        return (self.section, at["z"] * RING + at["y"], at["x"])

    def peer(self):
        return (1 - self.section, self.z * RING + self.y, self.x)


def greet(devices):
    barrier = pltpu.get_barrier_semaphore()
    for device in devices:
        pl.semaphore_signal(barrier, inc=1, device_id=device, device_id_type=pl.DeviceIdType.MESH)
    return lambda: pl.semaphore_wait(barrier, len(devices))


def meet(devices):
    greet(devices)()


class Copy:
    def __init__(self, sender, copy):
        self.sender, self.copy = sender, copy

    def wait_recv(self):
        self.sender.when(self.copy.wait_recv)


class Sender:
    def __init__(self, send_sems, recv_sems, flag=None):
        self.send_sems, self.recv_sems = send_sems, recv_sems
        self.flag = flag
        self.used = 0
        self.started = []

    def when(self, effect):
        if self.flag is None:
            effect()
        else:
            pl.when(self.flag)(effect)

    def make(self, source, target, device):
        copy = pltpu.make_async_remote_copy(
            src_ref=source,
            dst_ref=target,
            send_sem=self.send_sems.at[self.used],
            recv_sem=self.recv_sems.at[self.used],
            device_id=device,
            device_id_type=pl.DeviceIdType.MESH,
        )
        return copy

    def send(self, source, target, device):
        copy = self.make(source, target, device)
        self.used += 1
        self.when(copy.start)
        self.started.append(copy)
        return Copy(self, copy)

    def send_either(self, flag, source, otherwise, target, device):
        first, second = self.make(source, target, device), self.make(otherwise, target, device)
        self.used += 1
        pl.when(flag)(first.start)
        pl.when(jnp.logical_not(flag))(second.start)
        self.started.append(first)
        return Copy(self, first)

    def hand(self, flag, pairs, device):
        copies = []
        for source, target in pairs:
            copies.append(self.make(source, target, device))
            self.used += 1

        @pl.when(flag)
        def _():
            for copy in copies:
                copy.start()

        def settle():
            @pl.when(flag)
            def _():
                for copy in copies:
                    copy.wait_send()

            @pl.when(jnp.logical_not(flag))
            def _():
                for copy in copies:
                    copy.wait_recv()

        return settle

    def finish(self):
        def effect():
            for copy in self.started:
                copy.wait_send()

        self.when(effect)


def paced(job, points):
    count = iter(range(1000))

    def step():
        if next(count) in points:
            next(job, None)

    return step


def run(job):
    for _ in job:
        pass


def cut(width, count):
    tiles = width // 128
    edges = [tiles * i // count for i in range(count + 1)]
    return [(128 * a, 128 * (b - a)) for a, b in zip(edges[:-1], edges[1:])]


def region(place, order, phase, at, columns):
    spot = {}
    for i, axis in enumerate(order):
        spot[axis] = slice(None) if i < phase else (at if i == phase else place.index(axis))
    return (*[spot[axis] for axis in "zyx" if axis in spot], slice(None), pl.ds(*columns))


SENDS = 3 * (3 + 3 + 6)


def halves(columns):
    left, right = cut(columns[1], 2)
    return (columns[0] + left[0], left[1]), (columns[0] + right[0], right[1])


def thirds(buffer):
    return [(buffer, order, columns) for order, columns in zip(("xyz", "yzx", "zxy"), cut(buffer.shape[-1], 3))]


def gather(place, sender, plans, own=None, settle=None, beside=()):
    last_phase = len(plans[0][1]) - 1
    for phase in range(last_phase + 1):
        waits = []
        for buffer, order, columns in plans:
            axis = order[phase]
            me = place.index(axis)

            def push(delta, piece, buffer=buffer, order=order, axis=axis, me=me):
                here = buffer.at[region(place, order, phase, me, piece)]
                source = own.at[:, pl.ds(*piece)] if own is not None and phase == 0 else here
                return sender.send(source, here, place.device(axis, delta))

            if phase == last_phase:
                left, right = halves(columns)
                onward = (push(1, left), push(-1, right))
                waits += [push(1, right), push(-1, left)]
                waits.append((onward, buffer, order, axis, me, left, right))
            else:
                waits += [push(1, columns), push(-1, columns), push(2, columns)]
        if phase < len(beside):
            beside[phase]()
        yield
        last = []
        for wait in waits:
            if isinstance(wait, tuple):
                (up, down), buffer, order, axis, me, left, right = wait
                up.wait_recv()
                passing = buffer.at[region(place, order, phase, wrap(me - 1), left)]
                last.append(sender.send(passing, passing, place.device(axis, 1)))
                down.wait_recv()
                passing = buffer.at[region(place, order, phase, wrap(me + 1), right)]
                last.append(sender.send(passing, passing, place.device(axis, -1)))
            else:
                last.append(wait)
        if phase == last_phase:
            yield
        for copy in last:
            copy.wait_recv()
        if phase == 0 and settle is not None:
            settle()


def in_turn(jobs):
    jobs = list(jobs)
    while jobs:
        for job in list(jobs):
            try:
                next(job)
            except StopIteration:
                jobs.remove(job)
        if jobs:
            yield


def neighbours(place, axes="xyz"):
    return [place.device(axis, delta) for axis in axes for delta in (1, -1, 2)]


def reduce(place, sender, plans, slots, beside=()):
    last_phase = len(plans[0][1]) - 1
    for turn_number, phase in enumerate(range(last_phase, -1, -1)):
        waits = []
        for (buffer, order, columns), slot in zip(plans, slots):
            axis, slot = order[phase], slot[phase]
            me = place.index(axis)

            def push(delta, at, piece, target, buffer=buffer, order=order, axis=axis, me=me):
                source = buffer.at[region(place, order, phase, wrap(me + at), piece)]
                return sender.send(source, target, place.device(axis, delta))

            if phase == last_phase:
                left, right = halves(columns)
                up, down = push(1, 2, left, slot[0]), push(-1, 2, right, slot[1])
                near = push(1, 1, right, slot[2]), push(-1, -1, left, slot[3])
                waits.append((push, up, down, near))
            else:
                waits.append([push(delta, delta, columns, slot[i]) for i, delta in enumerate((1, -1, 2))])
        if turn_number < len(beside):
            beside[turn_number]()
        yield
        if phase == last_phase:
            later = []
            for (buffer, order, columns), slot, (push, up, down, near) in zip(plans, slots, waits):
                slot = slot[phase]
                me = place.index(order[phase])
                left, right = halves(columns)
                up.wait_recv()
                add_into(sender, buffer, region(place, order, phase, wrap(me + 1), left), slot[0])
                on_up = push(1, 1, left, slot[4])
                down.wait_recv()
                add_into(sender, buffer, region(place, order, phase, wrap(me - 1), right), slot[1])
                on_down = push(-1, -1, right, slot[5])
                later.append((*near, on_up, on_down))
            yield
            for (buffer, order, columns), slot, copies in zip(plans, slots, later):
                slot = slot[phase]
                me = place.index(order[phase])
                left, right = halves(columns)
                for copy in copies:
                    copy.wait_recv()
                add_into(sender, buffer, region(place, order, phase, me, left), slot[3], slot[4])
                add_into(sender, buffer, region(place, order, phase, me, right), slot[2], slot[5])
        else:
            for (buffer, order, columns), slot, copies in zip(plans, slots, waits):
                for copy in copies:
                    copy.wait_recv()
                add_into(sender, buffer, region(place, order, phase, place.index(order[phase]), columns), *slot[phase])


def slot_scratch(plans):
    scratch = []
    for rows, axes, columns in plans:
        left, right = halves(columns)
        for phase in range(axes):
            widths = (left, right, right, left, left, right) if phase == axes - 1 else (columns,) * 3
            scratch += [pltpu.VMEM((RING,) * phase + (rows, width), BF16) for _, width in widths]
    return scratch


def third_slots(rows, columns):
    return slot_scratch([(rows, 3, piece) for piece in cut(columns, 3)])


def sort_slots(refs, plans, axes):
    refs = list(refs)
    counts = [6 if phase == axes - 1 else 3 for phase in range(axes)]
    return [[[refs.pop(0) for _ in range(count)] for count in counts] for _ in range(plans)]


def add_into(sender, buffer, at, *terms):
    *spots, rows, columns = at
    free = [i for i, spot in enumerate(spots) if isinstance(spot, slice)]

    def some(first):
        spot = list(spots)
        picks = [slice(None)] * len(free)
        if first is not None:
            spot[free[0]] = first
            picks[0] = first
        here = (*spot, rows, columns)
        total = buffer[here].astype(F32)
        for term in terms:
            total = total + term[(*picks, slice(None), slice(None))].astype(F32)
        buffer[here] = total.astype(BF16)

    def all_blocks():
        if free:
            for i in range(RING):
                some(i)
        else:
            some(None)

    sender.when(all_blocks)


EPS = 1e-06
THETA = 1000000.0
MASKED = -1e30
GATED = 128
VMEM_LIMIT = 56 << 20


def params(number, vmem=VMEM_LIMIT):
    return pltpu.CompilerParams(collective_id=number, has_side_effects=True, vmem_limit_bytes=vmem)


IN_VMEM = pl.BlockSpec(memory_space=pltpu.VMEM)
ANYWHERE = pl.BlockSpec(memory_space=pl.ANY)


def copy_sems(count):
    return [pltpu.SemaphoreType.DMA((count,)), pltpu.SemaphoreType.DMA((count,))]


def dot_nn(left, right):
    return lax.dot_general(left, right, (((1,), (0,)), ((), ())), preferred_element_type=F32)


def dot_nt(left, right):
    return lax.dot_general(left, right, (((1,), (1,)), ((), ())), preferred_element_type=F32)


def dot_tn(left, right):
    return lax.dot_general(left, right, (((0,), (0,)), ((), ())), preferred_element_type=F32)


def inverse_rms(rows):
    return lax.rsqrt(jnp.mean(rows * rows, axis=-1, keepdims=True) + EPS)


def rms_back(rows, gain, grad):
    scale = inverse_rms(rows)
    unit = rows * scale
    lifted = grad * gain
    return scale * (lifted - unit * jnp.mean(lifted * unit, axis=-1, keepdims=True)), grad * unit


def send_x(place, sender, part, slots):
    return [
        sender.send(part.at[wrap(place.x + delta)], slots.at[i], place.device("x", delta))
        for i, delta in enumerate((1, -1, 2))
    ]


def sum_x(place, copies, part, slots):
    for copy in copies:
        copy.wait_recv()
    total = part[place.x].astype(F32)
    for i in range(3):
        total = total + slots[i].astype(F32)
    return total


def gather_x(place, sender, whole):
    mine = whole.at[place.x]
    copies = [sender.send(mine, mine, place.device("x", delta)) for delta in (1, -1, 2)]
    for copy in copies:
        copy.wait_recv()


def settle_job(place, sender, load, buffer, slots, mid, out):
    if load is not None:
        load.wait()
    yield from reduce(place, sender, thirds(buffer), sort_slots(slots, 3, 3))
    moe_rows = buffer[place.z, place.y, place.x].astype(F32)
    out[place.x] = (mid[...] + moe_rows).astype(BF16)
    mine = out.at[place.x]
    copies = [sender.send(mine, mine, place.device("x", delta)) for delta in (1, -1, 2)]
    yield
    for copy in copies:
        copy.wait_recv()


def part_columns(part, width):
    half = width // 2
    return pl.ds(part * half, half)


def settle_part(part, place, sems, partial, mid, out, scratch):
    sender = Sender(*sems)
    buffer, sem, *slots = scratch
    columns = part_columns(part, mid.shape[1])
    load = pltpu.make_async_copy(partial.at[:, :, :, :, columns], buffer, sem)
    load.start()
    return settle_job(place, sender, load, buffer, slots, mid.at[:, columns], out), sender


def settle_scratch(partial):
    *blocks, rows, width = partial.shape
    half = width // 2
    return [
        *copy_sems(3 + SENDS),
        pltpu.VMEM((*blocks, rows, half), BF16),
        pltpu.SemaphoreType.DMA,
        *third_slots(rows, half),
    ]


SETTLE_SCRATCH = 2 + 2 + 36


def moe_back_rows(layer, place, sender, buffer, mid, gates, pack0, pack1, d_part, gain_term, router_term):
    gain = of_layer(layer, pack0[PACK_ROUTER + 1 : PACK_ROUTER + 2], pack1[PACK_ROUTER + 1 : PACK_ROUTER + 2]).astype(F32)
    router = of_layer(layer, pack0[:PACK_ROUTER], pack1[:PACK_ROUTER])
    width = mid.shape[1]
    sums = buffer[place.z, place.y, place.x].astype(F32)
    weights = gates[...]
    d_gates = sums[:, width:]
    d_logits = (weights * (d_gates - jnp.sum(d_gates * weights, axis=-1, keepdims=True))).astype(BF16)
    d_moe_in = sums[:, :width] + dot_nn(d_logits, router)
    mid_rows = mid[...]
    d_mid, terms = rms_back(mid_rows, gain, d_moe_in)
    d_part[place.x] = d_mid.astype(BF16)
    gather_x(place, sender, d_part)
    gain_term[...] = jnp.sum(terms, axis=0, keepdims=True)
    moe_in = (mid_rows * inverse_rms(mid_rows) * gain).astype(BF16)
    router_term[...] = dot_tn(d_logits, moe_in)[: router_term.shape[0]]


def moe_back_kernel(
    layer, partial, mid, gates, pack0, pack1, d_part, gain_term, router_term, buffer, send, recv, local, *slots
):
    place = Place()
    load = pltpu.make_async_copy(partial, buffer, local)
    load.start()
    meet(neighbours(place))
    sender = Sender(send, recv)
    load.wait()
    run(reduce(place, sender, thirds(buffer), sort_slots(slots, 3, 3)))
    moe_back_rows(layer, place, sender, buffer, mid, gates, pack0, pack1, d_part, gain_term, router_term)
    sender.finish()


def moe_back(layer, partial, mid, gates, packs, expert_count):
    rows, width = mid.shape
    return pl.pallas_call(
        functools.partial(moe_back_kernel, layer),
        name="moe_back",
        out_shape=(
            jax.ShapeDtypeStruct((RING, rows, width), BF16),
            jax.ShapeDtypeStruct((1, width), F32),
            jax.ShapeDtypeStruct((expert_count, width), F32),
        ),
        in_specs=[ANYWHERE] + [IN_VMEM] * 4,
        out_specs=(IN_VMEM,) * 3,
        scratch_shapes=[
            pltpu.VMEM(partial.shape, BF16),
            *copy_sems(3 + SENDS),
            pltpu.SemaphoreType.DMA,
            *third_slots(rows, width + GATED),
        ],
        compiler_params=params(5 + layer),
    )(partial, mid, gates, *packs)


TILE = 256


def load_weights(layer, own, other, targets, sems):
    gate, up, down = targets
    half = gate.shape[0] // 2
    section = lax.axis_index("section")

    def pairs(source):
        return [
            (source[0].at[0], gate.at[pl.ds(0, half)]),
            (source[0].at[1], gate.at[pl.ds(half, half)]),
            (source[1].at[0], up.at[pl.ds(0, half)]),
            (source[1].at[1], up.at[pl.ds(half, half)]),
            (source[2].at[0], down.at[pl.ds(0, half)]),
            (source[2].at[1], down.at[pl.ds(half, half)]),
        ]

    @pl.when(section == layer)
    def _():
        for i, (source, target) in enumerate(pairs(own)):
            pltpu.make_async_copy(source, target, sems.at[i]).start()

    @pl.when(section != layer)
    def _():
        for i, (source, target) in enumerate(pairs(other)):
            pltpu.make_async_copy(source, target, sems.at[i]).start()

    return [pltpu.make_async_copy(source, target, sems.at[i]) for i, (source, target) in enumerate(pairs(own))]


def gate_columns(table, half):
    first = 2 * lax.axis_index("expert")
    lanes = lax.broadcasted_iota(jnp.int32, table.shape, 1)
    table = table.astype(F32)
    one = jnp.sum(jnp.where(lanes == first, table, 0.0), axis=1, keepdims=True)
    two = jnp.sum(jnp.where(lanes == first + 1, table, 0.0), axis=1, keepdims=True)
    units = lax.broadcasted_iota(jnp.int32, (table.shape[0], 2 * half), 1)
    return jnp.where(units < half, one, two)


class Stream:
    def __init__(self, hbm, slots, sems):
        self.hbm, self.slots, self.sems = hbm, slots, sems

    def copies(self, i, out):
        tile = self.slots.shape[1]
        rows = pl.ds(i * tile, tile)
        made = []
        at = 0
        for n, ref in enumerate(self.hbm):
            far, near = ref.at[rows], self.slots.at[i % 2, :, pl.ds(at, ref.shape[1])]
            at += ref.shape[1]
            pair = (near, far) if out else (far, near)
            made.append(pltpu.make_async_copy(*pair, self.sems.at[i % 2, n]))
        return made

    def fetch(self, i):
        for copy in self.copies(i, False):
            copy.start()

    def fetched(self, i):
        for copy in self.copies(i, False):
            copy.wait()
        return self.slots.at[i % 2]

    def store(self, i):
        for copy in self.copies(i, True):
            copy.start()

    def stored(self, i):
        for copy in self.copies(i, True):
            copy.wait()


def stream_scratch(widths, pieces=1, tile=TILE):
    scratch = []
    for width in widths:
        scratch += [pltpu.VMEM((2, tile, width), BF16), pltpu.SemaphoreType.DMA((2, pieces))]
    return scratch


SHARE_POINTS = (2, 5, 10)
BLOCKS = 8


def expert_kernel(layer, rows, shared, *refs):
    refs = list(refs)

    def take(count):
        taken = refs[:count]
        del refs[:count]
        return taken

    mid = take(0 if layer else 1)
    own, other, (out, acts, spread), (gate, up, down, sems) = take(3), take(3), take(3), take(4)
    row_slots, row_sems, act_slots, act_sems, send, recv, local = take(7)
    place = Place()
    met = greet(neighbours(place))
    sharer = Sender(send, recv)
    width = gate.shape[1]
    units = gate.shape[0]
    weights = load_weights(layer, own, other, (gate, up, down), sems)
    keep = pltpu.make_async_copy(shared.at[place.x], spread.at[place.z, place.y, place.x], local)
    keep.start()
    ins, kept = Stream([rows], row_slots, row_sems), Stream([acts], act_slots, act_sems)
    tile_rows = row_slots.shape[1]
    tiles = rows.shape[0] // tile_rows
    ins.fetch(0)
    if layer:
        out_slots, out_sems = refs
        outs = Stream([out], out_slots, out_sems)
    else:
        buffer, *slots = refs[2:]
        quarter = buffer.shape[3]
    met()
    sharing = gather(place, sharer, thirds(spread), shared.at[place.x], keep.wait)
    next(sharing)
    step = paced(sharing, SHARE_POINTS)
    for i in range(tiles):
        if i + 1 < tiles:
            ins.fetch(i + 1)
        tile = ins.fetched(i)
        if i == 0:
            for copy in weights:
                copy.wait()
        moe_in = tile[:, :width]
        gate_act = dot_nt(moe_in, gate[...])
        up_act = dot_nt(moe_in, up[...])
        hidden = gate_act / (1.0 + jnp.exp(-gate_act)) * up_act
        hidden = hidden * gate_columns(tile[:, width:], units // 2)
        step()
        if i >= 2:
            kept.stored(i - 2)
        act_slots[i % 2, :, :units] = gate_act.astype(BF16)
        act_slots[i % 2, :, units:] = up_act.astype(BF16)
        kept.store(i)
        made = dot_nn(hidden.astype(BF16), down[...])
        if layer:
            if i >= 2:
                outs.stored(i - 2)
            out_slots[i % 2] = made.astype(BF16)
            outs.store(i)
        else:
            for n in range(BLOCKS):
                block = i * BLOCKS + n
                here = (block // (RING * RING), block // RING % RING, block % RING)
                buffer[here] = made[n * quarter : (n + 1) * quarter].astype(BF16)
        step()
    if layer:
        run(sharing)
        for i in (tiles - 2, tiles - 1):
            outs.stored(i)
    else:
        sender = Sender(*refs[:2])
        run(in_turn([settle_job(place, sender, None, buffer, slots, mid[0], out), sharing]))
        sender.finish()
    for i in (tiles - 2, tiles - 1):
        kept.stored(i)
    sharer.finish()


def experts(layer, rows_all, shared, mid, own, other):
    quarter = rows_all.shape[3]
    count = RING**3 * quarter
    width = rows_all.shape[4] - GATED
    units = 2 * own[0].shape[1]
    rows = rows_all.reshape(count, width + GATED)
    tile = TILE if layer else BLOCKS * quarter
    if layer:
        mids, out_shape, out_spec = (), (count, width), ANYWHERE
        tail = stream_scratch((width,))
    else:
        mids, out_shape, out_spec = (mid,), (RING, quarter, width), IN_VMEM
        tail = [
            *copy_sems(3 + SENDS),
            pltpu.VMEM((*rows_all.shape[:4], width), BF16),
            *third_slots(quarter, width),
        ]
    out, acts, spread = pl.pallas_call(
        functools.partial(expert_kernel, layer),
        name="experts" if layer else "experts_settle",
        out_shape=(
            jax.ShapeDtypeStruct(out_shape, BF16),
            jax.ShapeDtypeStruct((count, 2 * units), BF16),
            jax.ShapeDtypeStruct((RING, RING, RING, quarter, shared.shape[2]), BF16),
        ),
        in_specs=[ANYWHERE, IN_VMEM] + [IN_VMEM] * len(mids) + [ANYWHERE] * 6,
        out_specs=(out_spec, ANYWHERE, ANYWHERE),
        scratch_shapes=[pltpu.VMEM((units, width), BF16)] * 3
        + [pltpu.SemaphoreType.DMA((6,))]
        + stream_scratch((width + GATED, 2 * units), tile=tile)
        + [*copy_sems(SENDS), pltpu.SemaphoreType.DMA]
        + tail,
        compiler_params=params(10 + layer),
    )(rows, shared, *mids, *own, *other)
    if layer:
        out = out.reshape(*rows_all.shape[:4], width)
    return out, acts, spread


SETTLE_POINTS = (3, 6)
SUM_POINTS = (4, 9)


def expert_back_kernel(layer, pieces, rows, *refs):
    refs = list(refs)

    def take(count):
        taken = refs[:count]
        del refs[:count]
        return taken

    grads, (acts,), own, other = take(pieces), take(1), take(3), take(3)
    extra = take(4)
    out, grad_in, grad_down = take(3)
    made = take(4)
    gate, up, down, sum_in, sum_down, sems = take(6)
    row_slots, row_sems, grad_slots, grad_sems, act_slots, act_sems, out_slots, out_sems, send, recv, local = take(11)
    place = Place()
    peer = place.peer()
    width = grad_in.shape[1]
    units = gate.shape[0]
    tiles = rows.shape[0] // TILE
    met = greet([peer, *neighbours(place, "yz")])
    upper = place.section == 1
    sender = Sender(send, recv, upper)
    first_own, second_own, got_in, got_down = made
    first, second, *slots = refs[:-2]
    loads = [pltpu.make_async_copy(*pair, local.at[i]) for i, pair in enumerate(zip(extra[:2], (first, second)))]
    for copy in loads:
        sender.when(copy.start)
    handing = Sender(refs[-2], refs[-1])

    def side():
        met()
        state["handed"] = handing.hand(place.section == 0, [(extra[2], got_in), (extra[3], got_down)], peer)
        for copy in loads:
            sender.when(copy.wait)
        yield from in_turn(gradient_reduces(place, sender, first, second, slots))
        first_own[...] = first[place.z, place.y]
        second_own[...] = second[place.z, place.y]

    state = {}
    job = side()

    weights = load_weights(layer, own, other, (gate, up, down), sems)
    ins, ups = Stream([rows], row_slots, row_sems), Stream(grads, grad_slots, grad_sems)
    kept, outs = Stream([acts], act_slots, act_sems), Stream([out], out_slots, out_sems)
    for stream in (ins, ups, kept):
        stream.fetch(0)
    next(job)
    step = paced(job, SUM_POINTS)
    first_expert = 2 * lax.axis_index("expert")
    for i in range(tiles):
        for stream in (ins, ups, kept):
            if i + 1 < tiles:
                stream.fetch(i + 1)
        tile, grad, act = ins.fetched(i), ups.fetched(i)[...], kept.fetched(i)
        if i == 0:
            for copy in weights:
                copy.wait()
        gates = gate_columns(tile[:, width:], units // 2)
        back = dot_nt(grad, down[...])
        gate_act = act[:, :units].astype(F32)
        up_act = act[:, units:].astype(F32)
        sigmoid = 1.0 / (1.0 + jnp.exp(-gate_act))
        silu = gate_act * sigmoid
        hidden = silu * up_act
        products = hidden * back
        in_one = lax.broadcasted_iota(jnp.int32, products.shape, 1) < units // 2
        one = jnp.sum(jnp.where(in_one, products, 0.0), axis=1, keepdims=True)
        two = jnp.sum(jnp.where(in_one, 0.0, products), axis=1, keepdims=True)
        lanes = lax.broadcasted_iota(jnp.int32, (products.shape[0], GATED), 1)
        d_gates = jnp.where(lanes == first_expert, one, jnp.where(lanes == first_expert + 1, two, 0.0))
        d_hidden = back * gates
        d_gate = (d_hidden * up_act * sigmoid * (1.0 + gate_act * (1.0 - sigmoid))).astype(BF16)
        d_up = (d_hidden * silu).astype(BF16)
        if i >= 2:
            outs.stored(i - 2)
        out_slots[i % 2, :, :width] = (dot_nn(d_gate, gate[...]) + dot_nn(d_up, up[...])).astype(BF16)
        out_slots[i % 2, :, width:] = d_gates.astype(BF16)
        outs.store(i)
        step()
        moe_in = tile[:, :width]
        terms = (
            (sum_in, slice(0, units), dot_tn(d_gate, moe_in)),
            (sum_in, slice(units, 2 * units), dot_tn(d_up, moe_in)),
            (sum_down, slice(0, units), dot_tn((hidden * gates).astype(BF16), grad)),
        )
        for total, at, term in terms:
            if i == 0:
                total[at] = term
            elif i < tiles - 1:
                total[at] += term
            else:
                low = grad_in if total is sum_in else grad_down
                low[at] = (total[at] + term).astype(BF16)
        step()
    run(job)
    for i in (tiles - 2, tiles - 1):
        outs.stored(i)
    sender.finish()
    state["handed"]()


def expert_back_sum_kernel(layer, pieces, rows, *refs):
    refs = list(refs)

    def take(count):
        taken = refs[:count]
        del refs[:count]
        return taken

    grads, (acts, mid, gates, pack0, pack1), own, other = take(pieces), take(5), take(3), take(3)
    above = take(1)[0]
    d_part, gain_term, router_term, grad_in, grad_down, *settled = take(7)
    gate, up, down, sems, row_all, grad_all, act_all, hiddens, load_sems = take(9)
    settle_refs = [take(SETTLE_SCRATCH) for _ in settled]
    send, recv, buffer, *slots = refs
    place = Place()
    met = greet(neighbours(place))
    sender = Sender(send, recv)
    parts = [
        settle_part(part, place, held[:2], above, mid, out, held[2:])
        for part, (out, held) in enumerate(zip(settled, settle_refs))
    ]
    settling = in_turn([job for job, _ in parts])
    weights = load_weights(layer, own, other, (gate, up, down), sems)
    quarter = buffer.shape[3]
    tile_rows = BLOCKS * quarter
    tiles = rows.shape[0] // tile_rows
    width = mid.shape[1]
    units = gate.shape[0]

    def loads(i):
        at = pl.ds(i * tile_rows, tile_rows)
        pairs = [(rows.at[at], row_all.at[at]), (acts.at[at], act_all.at[at])]
        start = 0
        for ref in grads:
            pairs.append((ref.at[at], grad_all.at[at, pl.ds(start, ref.shape[1])]))
            start += ref.shape[1]
        return [pltpu.make_async_copy(*pair, load_sems.at[i, n]) for n, pair in enumerate(pairs)]

    for i in range(tiles):
        for load in loads(i):
            load.start()
    for copy in weights:
        copy.wait()
    met()
    next(settling)
    first_expert = 2 * lax.axis_index("expert")
    for i in range(tiles):
        if i in SETTLE_POINTS:
            next(settling)
        for load in loads(i):
            load.wait()
        at = slice(i * tile_rows, (i + 1) * tile_rows)
        weight = gate_columns(row_all[at, width:], units // 2)
        back = dot_nt(grad_all[at], down[...])
        gate_act = act_all[at, :units].astype(F32)
        up_act = act_all[at, units:].astype(F32)
        sigmoid = 1.0 / (1.0 + jnp.exp(-gate_act))
        silu = gate_act * sigmoid
        hidden = silu * up_act
        products = hidden * back
        in_one = lax.broadcasted_iota(jnp.int32, products.shape, 1) < units // 2
        one = jnp.sum(jnp.where(in_one, products, 0.0), axis=1, keepdims=True)
        two = jnp.sum(jnp.where(in_one, 0.0, products), axis=1, keepdims=True)
        lanes = lax.broadcasted_iota(jnp.int32, (products.shape[0], GATED), 1)
        d_gates = jnp.where(lanes == first_expert, one, jnp.where(lanes == first_expert + 1, two, 0.0))
        d_hidden = back * weight
        d_gate = (d_hidden * up_act * sigmoid * (1.0 + gate_act * (1.0 - sigmoid))).astype(BF16)
        d_up = (d_hidden * silu).astype(BF16)
        act_all[at, :units] = d_gate
        act_all[at, units:] = d_up
        hiddens[at] = (hidden * weight).astype(BF16)
        d_rows = dot_nn(d_gate, gate[...]) + dot_nn(d_up, up[...])
        for n in range(BLOCKS):
            block = i * BLOCKS + n
            here = (block // (RING * RING), block // RING % RING, block % RING)
            piece = slice(n * quarter, (n + 1) * quarter)
            buffer[(*here, slice(None), slice(0, width))] = d_rows[piece].astype(BF16)
            buffer[(*here, slice(None), slice(width, None))] = d_gates[piece].astype(BF16)

    def products_job():
        step = 2 * LANES
        for target, source, inputs in ((grad_in, act_all, row_all), (grad_down, hiddens, grad_all)):
            for start in range(0, target.shape[0], step):
                size = min(step, target.shape[0] - start)
                term = dot_tn(source[:, start : start + size], inputs[:, :width])
                target[start : start + size] = term.astype(BF16)
                yield

    summing = reduce(place, sender, thirds(buffer), sort_slots(slots, 3, 3))
    making = products_job()
    for count in (2, 2, 1):
        next(summing)
        next(settling, None)
        for _ in range(count):
            next(making, None)
    run(in_turn([summing, settling]))
    run(making)
    moe_back_rows(layer, place, sender, buffer, mid, gates, pack0, pack1, d_part, gain_term, router_term)
    sender.finish()
    for _, settler in parts:
        settler.finish()


def experts_back_sum(layer, rows_all, grads_all, acts, mid, gates, packs, own, other, above, expert_count):
    quarter = rows_all.shape[3]
    count = RING**3 * quarter
    width = rows_all.shape[4] - GATED
    units = 2 * own[0].shape[1]
    grads = [g.reshape(count, g.shape[-1]) for g in grads_all]
    tiles = count // (BLOCKS * quarter)
    return pl.pallas_call(
        functools.partial(expert_back_sum_kernel, layer, len(grads)),
        name="experts_back_sum",
        out_shape=(
            jax.ShapeDtypeStruct((RING, quarter, width), BF16),
            jax.ShapeDtypeStruct((1, width), F32),
            jax.ShapeDtypeStruct((expert_count, width), F32),
            jax.ShapeDtypeStruct((2 * units, width), BF16),
            jax.ShapeDtypeStruct((units, width), BF16),
            *[jax.ShapeDtypeStruct((RING, quarter, width // 2), BF16)] * 2,
        ),
        in_specs=[ANYWHERE] * (2 + len(grads)) + [IN_VMEM] * 4 + [ANYWHERE] * 7,
        out_specs=(IN_VMEM,) * 7,
        scratch_shapes=[pltpu.VMEM((units, width), BF16)] * 3
        + [
            pltpu.SemaphoreType.DMA((6,)),
            pltpu.VMEM((count, width + GATED), BF16),
            pltpu.VMEM((count, width), BF16),
            pltpu.VMEM((count, 2 * units), BF16),
            pltpu.VMEM((count, units), BF16),
            pltpu.SemaphoreType.DMA((tiles, 2 + len(grads))),
            *settle_scratch(above),
            *settle_scratch(above),
            *copy_sems(3 + SENDS),
            pltpu.VMEM(rows_all.shape, BF16),
            *third_slots(quarter, width + GATED),
        ],
        compiler_params=params(14 + layer, 62 << 20),
    )(rows_all.reshape(count, width + GATED), *grads, acts, mid, gates, *packs, *own, *other, above)


def experts_back(layer, rows_all, grads_all, acts, own, other, extra):
    quarter = rows_all.shape[3]
    count = RING**3 * quarter
    width = rows_all.shape[4] - GATED
    units = 2 * own[0].shape[1]
    grads = [g.reshape(count, g.shape[-1]) for g in grads_all]
    products, grads_one, dense = extra
    first, second = gradient_shapes(dense)
    extra = (*products, *grads_one)
    extra_specs, made_specs = [ANYWHERE] * 4, (IN_VMEM, IN_VMEM, ANYWHERE, ANYWHERE)
    made = (
        jax.ShapeDtypeStruct(first[2:], BF16),
        jax.ShapeDtypeStruct(second[2:], BF16),
        jax.ShapeDtypeStruct(grads_one[0].shape, BF16),
        jax.ShapeDtypeStruct(grads_one[1].shape, BF16),
    )
    scratch = [
        *copy_sems(GRADIENT_SENDS),
        pltpu.SemaphoreType.DMA((2,)),
        pltpu.VMEM(first, BF16),
        pltpu.VMEM(second, BF16),
        *gradient_slots(first, second),
        *copy_sems(2),
    ]
    out, *rest = pl.pallas_call(
        functools.partial(expert_back_kernel, layer, len(grads)),
        name="experts_back",
        out_shape=(
            jax.ShapeDtypeStruct((count, width + GATED), BF16),
            jax.ShapeDtypeStruct((2 * units, width), BF16),
            jax.ShapeDtypeStruct((units, width), BF16),
            *made,
        ),
        in_specs=[ANYWHERE] * (1 + len(grads) + 1 + 6) + extra_specs,
        out_specs=(ANYWHERE, IN_VMEM, IN_VMEM, *made_specs),
        scratch_shapes=[pltpu.VMEM((units, width), BF16)] * 3
        + [pltpu.VMEM((2 * units, width), F32), pltpu.VMEM((units, width), F32), pltpu.SemaphoreType.DMA((6,))]
        + stream_scratch((width + GATED,))
        + stream_scratch((width,), len(grads))
        + stream_scratch((2 * units, width + GATED))
        + scratch,
        compiler_params=params(12 + layer),
    )(rows_all.reshape(count, width + GATED), *grads, acts, *own, *other, *extra)
    return (out.reshape(*rows_all.shape), *rest)


def pull(layer, own, other, targets, sems):
    section = lax.axis_index("section")

    @pl.when(section == layer)
    def _():
        for i, (source, target) in enumerate(zip(own, targets)):
            pltpu.make_async_copy(source, target, sems.at[i]).start()

    @pl.when(section != layer)
    def _():
        for i, (source, target) in enumerate(zip(other, targets)):
            pltpu.make_async_copy(source, target, sems.at[i]).start()

    return [pltpu.make_async_copy(source, target, sems.at[i]) for i, (source, target) in enumerate(zip(own, targets))]


def of_layer(layer, own, other):
    return jnp.where(lax.axis_index("section") == layer, own, other)


def tables(seg_column, seg_row, dim):
    rows = seg_column.shape[0]
    at_row = lax.broadcasted_iota(jnp.int32, (rows, rows), 0)
    at_column = lax.broadcasted_iota(jnp.int32, (rows, rows), 1)
    earlier = jnp.sum((seg_row < seg_column).astype(F32), axis=1, keepdims=True)
    position = lax.broadcasted_iota(jnp.int32, (rows, dim), 0).astype(F32) - earlier
    lane = lax.broadcasted_iota(jnp.int32, (rows, dim), 1)
    half = dim // 2
    place = jnp.where(lane < half, lane, lane - half).astype(F32)
    angle = position * jnp.exp(place * (-math.log(THETA) / half))
    sine = jnp.sin(angle)
    return jnp.cos(angle), jnp.where(lane < half, -sine, sine), (seg_row == seg_column) & (at_column <= at_row)


def turn(rows, cosine, sine):
    return rows * cosine + pltpu.roll(rows, rows.shape[1] // 2, 1) * sine


def turn_back(grad, cosine, sine):
    return grad * cosine + pltpu.roll(grad * sine, grad.shape[1] // 2, 1)


PACK_ROUTER = 128
PACK_ROWS = 144
HEADS_STEP = 2


def attend_mix_kernel(
    layer, rows, seg_column, seg_row, pack0, routes0, *refs
):
    refs = list(refs)

    def take(count):
        taken = refs[:count]
        del refs[:count]
        return taken

    if layer:
        (pack1, routes1), dense_own, dense_other = take(2), take(4), take(4)
        attended, query_raw, key_raw, value_low, mid, gates, rows_all = take(7)
    else:
        dense_own, expert_own = take(4), take(3)
        attended, query_raw, key_raw, value_low, mid, gates, rows_all, pack1, routes1 = take(9)
        dense_other, expert_other = take(4), take(3)
    wq, wk, wv, wo, total, part, own, slots, sems, send, recv, local = take(12)
    place = Place()
    section = place.section
    peer = place.peer()
    met = greet(neighbours(place) if layer else [peer, *neighbours(place)])
    dim = wk.shape[1]
    heads = wq.shape[1] // dim
    step = HEADS_STEP * dim
    steps = heads // HEADS_STEP

    def pieces(q, k, v, o):
        made = [k, v]
        for i in range(steps):
            made += [q.at[:, pl.ds(i * step, step)], o.at[pl.ds(i * step, step)]]
        return made

    targets = pieces(wq, wk, wv, wo)
    ours, theirs = pieces(*dense_own), pieces(*dense_other)
    if layer:
        loads = pull(layer, ours, theirs, targets, sems)

        def arrive(i):
            loads[i].wait()
    else:
        lower = section == 0
        loads = [pltpu.make_async_copy(*pair, sems.at[i]) for i, pair in enumerate(zip(ours, targets))]
        late = [pltpu.make_async_copy(*pair, sems.at[i]) for i, pair in enumerate(zip(theirs, targets))]

        @pl.when(lower)
        def _():
            for load in loads:
                load.start()

        met()
        pusher = Sender(*refs)
        first = [pusher.send(pack0, pack1, peer), pusher.send(routes0.at[1 - section], routes1, peer)]
        pushed = [pusher.send(*pair, peer) for pair in zip(ours, theirs)]
        for copy in first:
            copy.wait_recv()

        def prefetch(i):
            @pl.when(jnp.logical_not(lower))
            def _():
                pushed[i].wait_recv()
                late[i].start()

        def arrive(i):
            if i + 1 < len(pushed):
                prefetch(i + 1)
            loads[i].wait()

        prefetch(0)
    resid = rows[...].astype(F32)
    gain = of_layer(layer, pack0[PACK_ROUTER : PACK_ROUTER + 1], pack1[PACK_ROUTER : PACK_ROUTER + 1]).astype(F32)
    gains = of_layer(layer, pack0[PACK_ROUTER + 2 : PACK_ROUTER + 3], pack1[PACK_ROUTER + 2 : PACK_ROUTER + 3]).astype(F32)
    gain_query, gain_key = gains[:, :dim], gains[:, dim : 2 * dim]
    cosine, sine, allowed = tables(seg_column[...], seg_row[...], dim)
    normed = (resid * inverse_rms(resid) * gain).astype(BF16)
    arrive(0)
    raw = dot_nn(normed, wk[...])
    key_raw[...] = raw
    key = turn(raw * inverse_rms(raw) * gain_key, cosine, sine).astype(BF16)
    arrive(1)
    value = dot_nn(normed, wv[...]).astype(BF16)
    value_low[...] = value
    for i in range(steps):
        arrive(2 + 2 * i)
        raws = dot_nn(normed, wq[:, i * step : (i + 1) * step])
        query_raw[:, i * step : (i + 1) * step] = raws
        for h in range(HEADS_STEP):
            raw = raws[:, h * dim : (h + 1) * dim]
            query = turn(raw * inverse_rms(raw) * gain_query, cosine, sine).astype(BF16)
            scores = jnp.where(allowed, dot_nt(query, key) * (1.0 / math.sqrt(dim)), MASKED)
            raised = jnp.exp(scores - jnp.max(scores, axis=1, keepdims=True))
            probs = (raised / jnp.sum(raised, axis=1, keepdims=True)).astype(BF16)
            at = i * step + h * dim
            attended[:, at : at + dim] = dot_nn(probs, value).astype(BF16)
        arrive(3 + 2 * i)
        piece = dot_nn(attended[:, i * step : (i + 1) * step], wo[i * step : (i + 1) * step])
        if i == 0:
            total[...] = piece
        else:
            total[...] += piece
    quarter = part.shape[1]
    for i in range(part.shape[0]):
        part[i] = total[i * quarter : (i + 1) * quarter].astype(BF16)
        total[i * quarter : (i + 1) * quarter] = resid[i * quarter : (i + 1) * quarter]
    sender = Sender(send, recv)
    if layer:
        met()
    copies = send_x(place, sender, part, slots)
    if not layer:
        pushed_experts = [pusher.send(*pair, peer) for pair in zip(expert_own, expert_other)]
    chosen = of_layer(layer, routes0[section, place.x], routes1[place.x])
    lanes = lax.broadcasted_iota(jnp.int32, gates.shape, 1)
    named = chosen[:, 0:1] == lanes
    for i in range(1, chosen.shape[1]):
        named = named | (chosen[:, i : i + 1] == lanes)
    gain = of_layer(layer, pack0[PACK_ROUTER + 1 : PACK_ROUTER + 2], pack1[PACK_ROUTER + 1 : PACK_ROUTER + 2])
    router = of_layer(layer, pack0[:PACK_ROUTER], pack1[:PACK_ROUTER])
    mine = total[pl.ds(pl.multiple_of(place.x * quarter, 8), quarter)]
    mid_rows = mine + sum_x(place, copies, part, slots)
    mid[...] = mid_rows
    moe_in = (mid_rows * inverse_rms(mid_rows) * gain.astype(F32)).astype(BF16)
    logits = jnp.where(named, dot_nt(moe_in, router), MASKED)
    raised = jnp.where(named, jnp.exp(logits - jnp.max(logits, axis=-1, keepdims=True)), 0.0)
    weights = raised / jnp.sum(raised, axis=-1, keepdims=True)
    gates[...] = weights
    own[:, : moe_in.shape[1]] = moe_in
    own[:, moe_in.shape[1] :] = weights.astype(BF16)
    keep = pltpu.make_async_copy(own, rows_all.at[place.z, place.y, place.x], local)
    keep.start()
    run(gather(place, sender, thirds(rows_all), own, keep.wait))
    if not layer:

        @pl.when(lower)
        def _():
            for copy in pushed:
                copy.wait_recv()

        for copy in pushed_experts:
            copy.wait_recv()
        pusher.finish()
    sender.finish()


def weight_scratch(dense):
    return [pltpu.VMEM(w.shape, BF16) for w in dense]


def attend_mix(layer, rows, segs, pack, routes, own, other):
    count, width = rows.shape
    quarter = count // RING
    dim, inner = own[1].shape[1], own[0].shape[1]
    pieces = 2 + 2 * (inner // dim // HEADS_STEP)

    def like(array):
        return jax.ShapeDtypeStruct(array.shape, array.dtype)

    if layer:
        swapped, swapped_specs, push = (), (), ()
        inputs = (rows, *segs, pack[0], routes[0], pack[1], routes[1], *own, *other)
    else:
        swapped = (like(pack), jax.ShapeDtypeStruct(routes.shape[1:], routes.dtype), *map(like, own), *map(like, other))
        swapped_specs = (IN_VMEM, IN_VMEM) + (ANYWHERE,) * 7
        push = copy_sems(2 + pieces + 3)
        inputs = (rows, *segs, pack, routes, *own, *other)
    return pl.pallas_call(
        functools.partial(attend_mix_kernel, layer),
        name="attend_mix",
        out_shape=(
            jax.ShapeDtypeStruct((count, inner), BF16),
            jax.ShapeDtypeStruct((count, inner), F32),
            jax.ShapeDtypeStruct((count, dim), F32),
            jax.ShapeDtypeStruct((count, dim), BF16),
            jax.ShapeDtypeStruct((quarter, width), F32),
            jax.ShapeDtypeStruct((quarter, GATED), F32),
            jax.ShapeDtypeStruct((RING, RING, RING, quarter, width + GATED), BF16),
            *swapped,
        ),
        in_specs=[IN_VMEM] * (7 if layer else 5) + [ANYWHERE] * (8 if layer else 7),
        out_specs=(IN_VMEM,) * 6 + (ANYWHERE,) + swapped_specs,
        scratch_shapes=[
            *weight_scratch(own),
            pltpu.VMEM((count, width), F32),
            pltpu.VMEM((RING, quarter, width), BF16),
            pltpu.VMEM((quarter, width + GATED), BF16),
            pltpu.VMEM((3, quarter, width), BF16),
            pltpu.SemaphoreType.DMA((pieces,)),
            *copy_sems(3 + SENDS),
            pltpu.SemaphoreType.DMA,
            *push,
        ],
        compiler_params=params(1 + layer),
    )(*inputs)


SMALL = 48


def gradient_shapes(dense):
    width, inner = dense[0].shape
    proj = inner + 2 * dense[1].shape[1]
    blocks = RING * RING
    return (RING, RING, width // blocks, proj), (RING, RING, inner // blocks, width)


def gradient_plans(array):
    one, two = cut(array.shape[-1], 2)
    return [(array, "yz", one), (array, "zy", two)]


GRADIENT_SENDS = 2 * 18


def gradient_slots(first, second):
    scratch = []
    for shape in (first, second):
        one, two = cut(shape[3], 2)
        scratch += slot_scratch([(shape[2], 2, one), (shape[2], 2, two)])
    return scratch


def gradient_reduces(place, sender, first, second, slots, beside=()):
    return [
        reduce(place, sender, gradient_plans(first), sort_slots(slots[:18], 2, 2)),
        reduce(place, sender, gradient_plans(second), sort_slots(slots[18:], 2, 2), beside),
    ]


def gradient_gathers(place, sender, first, second, beside=()):
    return [
        gather(place, sender, gradient_plans(first)),
        gather(place, sender, gradient_plans(second), None, None, beside),
    ]


LANES = 128


def output_products(heads, mids, second):
    def blocks(i, _):
        pair = dot_tn(heads[:, pl.ds(pl.multiple_of(i * LANES, LANES), LANES)], mids[...]).astype(BF16)
        at = 2 * i
        second[lax.div(at, RING), lax.rem(at, RING)] = pair[: LANES // 2]
        second[lax.div(at, RING), lax.rem(at, RING) + 1] = pair[LANES // 2 :]
        return 0

    lax.fori_loop(0, heads.shape[1] // LANES, blocks, 0)


def input_products(normed, proj, first):
    def blocks(i, _):
        block = dot_tn(normed[:, pl.ds(pl.multiple_of(i * LANES, LANES), LANES)], proj[...])
        first[lax.div(i, RING), lax.rem(i, RING)] = block.astype(BF16)
        return 0

    lax.fori_loop(0, normed.shape[1] // LANES, blocks, 0)


def attend_back_kernel(
    layer, rows, seg_column, seg_row, pack0, pack1, attended, query_raw, key_raw, value_low, upstream, d_part,
    router_term, moe_gain_term, *refs
):
    last = layer == 0
    refs = list(refs)
    extra = [refs.pop(0) for _ in range(4 if last else 0)]
    q0, k0, v0, o0, q1, k1, v1, o1, d_input, normed_both, d_proj, heads_both, d_mid_low, smalls = refs[:14]
    refs = refs[14:]
    wide = [refs.pop(0) for _ in range(4 if last else 2)]
    wq, wk, wv, wo, total, d_mid, d_heads, part, own, slots, sems, send, recv, local, *side = refs
    place = Place()
    peer = place.peer()
    met = greet([peer, *neighbours(place)])
    count = rows.shape[0]
    job = iter(())
    if last:
        upper = place.section == 1
        first_own, second_own, grad_in, grad_down = extra
        first, second, got_in, got_down = wide
        side_sender = Sender(side[0], side[1], upper)
        handing = Sender(side[2], side[3])

        def widen():
            first[place.z, place.y] = first_own[...]
            second[place.z, place.y] = second_own[...]
            yield
            met()
            yield from in_turn(gradient_gathers(place, side_sender, first, second))

        job = widen()
    dim = wk.shape[1]
    heads = wq.shape[1] // dim
    inner = heads * dim
    step = HEADS_STEP * dim
    steps = heads // HEADS_STEP
    quarter = d_part.shape[1]

    def pieces(q, k, v, o):
        return [*[o.at[pl.ds(i * step, step)] for i in range(steps)],
                *[q.at[:, pl.ds(i * step, step)] for i in range(steps)], k, v]

    loads = pull(layer, pieces(q0, k0, v0, o0), pieces(q1, k1, v1, o1), pieces(wq, wk, wv, wo), sems)
    for i in range(RING):
        grad = upstream[i].astype(F32) + d_part[i].astype(F32)
        d_mid[i] = grad
        total[i * quarter : (i + 1) * quarter] = grad
    grad_low = total[...].astype(BF16)
    d_mid_low[:count] = grad_low
    heads_both[:count] = attended[...]
    resid = rows[...].astype(F32)
    gain = of_layer(layer, pack0[PACK_ROUTER : PACK_ROUTER + 1], pack1[PACK_ROUTER : PACK_ROUTER + 1]).astype(F32)
    gains = of_layer(layer, pack0[PACK_ROUTER + 2 : PACK_ROUTER + 3], pack1[PACK_ROUTER + 2 : PACK_ROUTER + 3]).astype(F32)
    gain_query, gain_key = gains[:, :dim], gains[:, dim : 2 * dim]
    cosine, sine, allowed = tables(seg_column[...], seg_row[...], dim)
    normed_both[:count] = (resid * inverse_rms(resid) * gain).astype(BF16)
    raw_key = key_raw[...]
    key = turn(raw_key * inverse_rms(raw_key) * gain_key, cosine, sine).astype(BF16)
    value = value_low[...]
    scale = 1.0 / math.sqrt(dim)
    d_key = jnp.zeros(key.shape, F32)
    d_value = jnp.zeros(key.shape, F32)
    gain_total = jnp.zeros(gain_query.shape, F32)
    handed_grads = None
    for i in range(steps):
        next(job, None)
        if last and i == 1:
            handed_grads = handing.hand(upper, [(grad_in, got_in), (grad_down, got_down)], peer)
        loads[i].wait()
        d_heads[...] = dot_nt(grad_low, wo[i * step : (i + 1) * step]).astype(BF16)
        for h in range(HEADS_STEP):
            at = i * step + h * dim
            raw = query_raw[:, at : at + dim]
            query = turn(raw * inverse_rms(raw) * gain_query, cosine, sine).astype(BF16)
            scores = jnp.where(allowed, dot_nt(query, key) * scale, MASKED)
            raised = jnp.exp(scores - jnp.max(scores, axis=1, keepdims=True))
            probs = raised / jnp.sum(raised, axis=1, keepdims=True)
            d_head = d_heads[:, h * dim : (h + 1) * dim]
            d_probs = dot_nt(d_head, value)
            d_value = d_value + dot_tn(probs.astype(BF16), d_head)
            d_scores = (probs * (d_probs - jnp.sum(d_probs * probs, axis=1, keepdims=True))).astype(BF16)
            d_query = turn_back(dot_nn(d_scores, key) * scale, cosine, sine)
            d_key = d_key + dot_tn(d_scores, query) * scale
            d_raw, terms = rms_back(raw, gain_query, d_query)
            gain_total = gain_total + jnp.sum(terms, axis=0, keepdims=True)
            d_proj[:count, at : at + dim] = d_raw.astype(BF16)
        loads[steps + i].wait()
        piece = dot_nt(d_proj[:count, i * step : (i + 1) * step], wq[:, i * step : (i + 1) * step])
        if i == 0:
            total[...] = piece
        else:
            total[...] += piece
    d_raw, terms = rms_back(raw_key, gain_key, turn_back(d_key, cosine, sine))
    d_proj[:count, inner : inner + dim] = d_raw.astype(BF16)
    d_proj[:count, inner + dim :] = d_value.astype(BF16)
    smalls[0, 32:] = jnp.zeros((SMALL - 32, smalls.shape[2]), F32)
    smalls[0, :32] = router_term[...]
    smalls[0, 32:33] = moe_gain_term[...]
    smalls[0, 34:35, :dim] = gain_total
    smalls[0, 34:35, dim : 2 * dim] = jnp.sum(terms, axis=0, keepdims=True)
    loads[2 * steps].wait()
    loads[2 * steps + 1].wait()
    total[...] += dot_nt(d_proj[:count, inner : inner + dim], wk[...]) + dot_nt(d_proj[:count, inner + dim :], wv[...])
    for i in range(RING):
        part[i] = total[i * quarter : (i + 1) * quarter].astype(BF16)
    sender = Sender(send, recv)
    if not last:
        met()
    copies = send_x(place, sender, part, slots)
    theirs = pl.ds(count, count)
    ours = pl.ds(0, count)
    handed = sender.hand(
        place.section != layer,
        [(ref.at[ours], ref.at[theirs]) for ref in (normed_both, d_proj, heads_both, d_mid_low)],
        peer,
    )
    mine = resid[:quarter]
    for i in range(1, RING):
        mine = jnp.where(place.x == i, resid[i * quarter : (i + 1) * quarter], mine)
    d_resid, terms = rms_back(mine, gain, sum_x(place, copies, part, slots))
    smalls[0, 33:34] = jnp.sum(terms, axis=0, keepdims=True)
    handed_small = sender.hand(place.section != layer, [(smalls.at[0], smalls.at[1])], peer)
    d_rows = (d_mid[place.x] + d_resid).astype(BF16)
    if last:
        d_input[place.x] = d_rows
        gather_x(place, sender, d_input)
    else:
        own[...] = d_rows
        keep = pltpu.make_async_copy(own, d_input.at[place.z, place.y, place.x], local)
        keep.start()
        spread = gather(place, sender, thirds(d_input), own, keep.wait)
        for _ in range(3):
            next(spread)
    handed()
    handed_small()
    if not last:
        owner = place.section == layer
        products, copy_out = side[:2], side[2]
        stores = [pltpu.make_async_copy(*pair, copy_out.at[i]) for i, pair in enumerate(zip(products, wide))]

        @pl.when(owner)
        def _():
            output_products(heads_both, d_mid_low, products[1])

        next(spread)

        @pl.when(owner)
        def _():
            stores[1].start()
            input_products(normed_both, d_proj, products[0])
            stores[0].start()

        run(spread)

        @pl.when(owner)
        def _():
            for store in stores:
                store.wait()

    sender.finish()
    if last:
        run(job)
        handed_grads()
        side_sender.finish()


def attend_back(layer, rows, segs, packs, saved, upstream, d_part, terms, extra, own, other):
    last = layer == 0
    first, second = gradient_shapes(own)
    wide = tuple(jax.ShapeDtypeStruct(shape, BF16) for shape in (first, second))
    side = (pltpu.VMEM(first, BF16), pltpu.VMEM(second, BF16), pltpu.SemaphoreType.DMA((2,)))
    if last:
        shapes = (first, second, extra[2].shape, extra[3].shape)
        wide = tuple(jax.ShapeDtypeStruct(shape, BF16) for shape in shapes)
        side = (
            *copy_sems(GRADIENT_SENDS),
            *copy_sems(2),
        )

    count, width = rows.shape
    quarter = count // RING
    dim, inner = own[1].shape[1], own[0].shape[1]
    out = (RING, quarter, width) if layer == 0 else (RING, RING, RING, quarter, width)
    return pl.pallas_call(
        functools.partial(attend_back_kernel, layer),
        name="attend_back_last" if layer == 0 else "attend_back",
        out_shape=(
            jax.ShapeDtypeStruct(out, BF16),
            jax.ShapeDtypeStruct((2 * count, width), BF16),
            jax.ShapeDtypeStruct((2 * count, inner + 2 * dim), BF16),
            jax.ShapeDtypeStruct((2 * count, inner), BF16),
            jax.ShapeDtypeStruct((2 * count, width), BF16),
            jax.ShapeDtypeStruct((2, SMALL, width), F32),
            *wide,
        ),
        in_specs=[IN_VMEM] * 13 + ([IN_VMEM] * 2 + [ANYWHERE] * 2 if last else []) + [ANYWHERE] * 8,
        out_specs=(IN_VMEM if last else ANYWHERE,) + (IN_VMEM,) * (7 if last else 5) + (ANYWHERE,) * 2,
        scratch_shapes=[
            *weight_scratch(own),
            pltpu.VMEM((count, width), F32),
            pltpu.VMEM((RING, quarter, width), F32),
            pltpu.VMEM((count, HEADS_STEP * dim), BF16),
            pltpu.VMEM((RING, quarter, width), BF16),
            pltpu.VMEM((quarter, width), BF16),
            pltpu.VMEM((3, quarter, width), BF16),
            pltpu.SemaphoreType.DMA((2 + 2 * (inner // dim // HEADS_STEP),)),
            *copy_sems(3 + 5 + (3 if layer == 0 else SENDS)),
            pltpu.SemaphoreType.DMA,
            *side,
        ],
        compiler_params=params(7 + layer),
    )(rows, *segs, *packs, *saved, upstream, d_part, *terms, *extra, *own, *other)


def finish_kernel(
    normed0, proj0, heads0, mids0, small0, small1, first_one, second_one, out0, out1a, out1b, ig0, ig1,
    first, second, small_out, outputs, input_grads,
    first_sums, second_sums, normed, proj, heads, mids, terms, passing, small_slots, send, recv, flagged_send,
    flagged_recv, local, *slots
):
    place = Place()
    lower = place.section == 0
    upper = place.section == 1
    peer = place.peer()
    met = greet([peer, *neighbours(place)])
    sender = Sender(send, recv)
    reducer = Sender(flagged_send, flagged_recv, lower)

    def keep(index, source, otherwise, target):
        one, two = (pltpu.make_async_copy(origin, target, local.at[index]) for origin in (source, otherwise))
        pl.when(lower)(one.start)
        pl.when(upper)(two.start)
        return one

    half = out1a.shape[2]
    pairs = [(small0, small1, terms), (ig0, ig1, input_grads.at[place.section])]
    halves_of = []
    for part, above in enumerate((out1a, out1b)):
        columns = pl.ds(part * half, half)
        halves_of.append((out0.at[:, :, columns], above, outputs.at[place.section, :, :, columns]))
    pairs += halves_of
    loads = ((normed0, normed), (proj0, proj), (heads0, heads), (mids0, mids))
    loads = [pltpu.make_async_copy(*pair, local.at[4 + i]) for i, pair in enumerate(loads)]
    ready = [
        pltpu.make_async_copy(*pair, local.at[8 + i]) for i, pair in enumerate(((first_one, first), (second_one, second)))
    ]

    @pl.when(upper)
    def _():
        for copy in ready:
            copy.start()

    @pl.when(lower)
    def _():
        for copy in loads:
            copy.start()
        for copy in loads:
            copy.wait()
        output_products(heads, mids, second_sums)

    kept = [keep(i, *pair) for i, pair in enumerate(pairs)]
    kept[0].wait()
    met()
    state = {}

    def exchange(step, total):
        passing[...] = total
        buffer = small_slots.at[step, 3]
        buffer[...] = total.astype(BF16)
        state["copies"] = [
            sender.send(buffer, small_slots.at[step, i], place.device("xyz"[step], delta))
            for i, delta in enumerate((1, -1, 2))
        ]

    def collect(step):
        for copy in state["copies"]:
            copy.wait_recv()
        total = passing[...]
        for i in range(3):
            total = total + small_slots[step, i].astype(F32)
        return total

    def small_last():
        small_out[...] = collect(2)

    def swap_rows():
        state["late"] = [
            *[sender.send_either(lower, high, low, target, peer) for low, high, target in halves_of],
            sender.send_either(lower, ig1, ig0, input_grads.at[place.section], peer),
        ]
        exchange(0, terms[0] + terms[1])

    def second_step():
        exchange(1, collect(0))

    first_job, second_job = gradient_reduces(place, reducer, first_sums, second_sums, slots, (swap_rows, second_step))
    next(second_job)
    pl.when(lower)(lambda: input_products(normed, proj, first_sums))
    run(in_turn([first_job, second_job]))

    @pl.when(lower)
    def _():
        first[place.z, place.y] = first_sums[place.z, place.y]
        second[place.z, place.y] = second_sums[place.z, place.y]

    beside = (lambda: exchange(2, collect(1)), small_last)
    run(in_turn(gradient_gathers(place, reducer, first, second, beside)))
    for copy in state["late"]:
        copy.wait_recv()
    for copy in kept[1:]:
        copy.wait()

    @pl.when(upper)
    def _():
        for copy in ready:
            copy.wait()

    sender.finish()
    reducer.finish()


def finish(factors, smalls, ready, outs, input_grads):
    rows, width = factors[0].shape
    first, second = ready[0].shape, ready[1].shape
    both = (2, *outs[0].shape)
    return pl.pallas_call(
        finish_kernel,
        name="finish",
        out_shape=(
            jax.ShapeDtypeStruct(first, BF16),
            jax.ShapeDtypeStruct(second, BF16),
            jax.ShapeDtypeStruct(smalls[0].shape[1:], F32),
            jax.ShapeDtypeStruct(both, BF16),
            jax.ShapeDtypeStruct(both, BF16),
        ),
        in_specs=[ANYWHERE] * 13,
        out_specs=(IN_VMEM,) * 3 + (ANYWHERE,) * 2,
        scratch_shapes=[
            pltpu.VMEM(first, BF16),
            pltpu.VMEM(second, BF16),
            *[pltpu.VMEM(f.shape, BF16) for f in factors],
            pltpu.VMEM(smalls[0].shape, F32),
            pltpu.VMEM(smalls[0].shape[1:], F32),
            pltpu.VMEM((3, 4, *smalls[0].shape[1:]), BF16),
            *copy_sems(3 + 9),
            *copy_sems(2 * GRADIENT_SENDS),
            pltpu.SemaphoreType.DMA((10,)),
            *gradient_slots(first, second),
        ],
        compiler_params=params(9),
    )(*factors, *smalls, *ready, *outs, *input_grads)


STEPS = 8


def widen_kernel(
    section, first, second, gate_own0, gate_own1, up_own0, up_own1, gate_got0, gate_got1, up_got0, up_got1,
    down_own0, down_own1, down_got0, down_got1, small, outputs_in, d_inputs_in,
    query, key, value, output, gate, up, down, router, gain_moe, gain_attn, gain_query, gain_key, outputs, d_inputs
):
    inner, dim = query.shape[1], key.shape[1]
    query[...] = first[:, :inner].astype(F32)
    key[...] = first[:, inner : inner + dim].astype(F32)
    value[...] = first[:, inner + dim :].astype(F32)
    output[...] = second[...].astype(F32)
    lower = section[0] == 0

    def either(low, high):
        return jnp.where(lower, low[...].astype(F32), high[...].astype(F32))

    gate[...] = either(gate_own0, gate_own1) + either(gate_got0, gate_got1)
    up[...] = either(up_own0, up_own1) + either(up_got0, up_got1)
    down[...] = either(down_own0, down_own1) + either(down_got0, down_got1)
    outputs[...] = outputs_in[...]
    d_inputs[...] = d_inputs_in[...].astype(F32)

    @pl.when(pl.program_id(0) == 0)
    def _():
        count = router.shape[0]
        router[...] = small[:count]
        gain_moe[...] = small[count : count + 1]
        gain_attn[...] = small[count + 1 : count + 2]
        gain_query[...] = small[count + 2 : count + 3, :dim]
        gain_key[...] = small[count + 2 : count + 3, dim : 2 * dim]


def widen(section, first, second, expert_grads, small, outputs, d_inputs, dim, expert_count):
    (in0, down0, got_in0, got_down0), (in1, down1, got_in1, got_down1) = expert_grads
    width = second.shape[1]
    inner = first.shape[1] - 2 * dim
    units = down0.shape[0]

    def rows(count, columns):
        return pl.BlockSpec((count // STEPS, columns), lambda i, section: (i, 0))

    def either(ahead=0):
        block = (units // STEPS, width)
        return [
            pl.BlockSpec(block, lambda i, section: (jnp.where(section[0] == 0, ahead + i, ahead), 0)),
            pl.BlockSpec(block, lambda i, section: (jnp.where(section[0] == 1, ahead + i, ahead), 0)),
        ]

    def whole(*shape):
        return pl.BlockSpec(shape, lambda i, section: (0,) * len(shape))

    def slab(array):
        return pl.BlockSpec((*array.shape[:-1], width // STEPS), lambda i, section: (0, 0, 0, i))

    def shape(*dims):
        return jax.ShapeDtypeStruct(dims, F32)

    return pl.pallas_call(
        widen_kernel,
        name="widen",
        out_shape=(
            shape(width, inner),
            shape(width, dim),
            shape(width, dim),
            shape(*second.shape),
            shape(units, width),
            shape(units, width),
            shape(units, width),
            shape(expert_count, width),
            shape(1, width),
            shape(1, width),
            shape(1, dim),
            shape(1, dim),
            jax.ShapeDtypeStruct(outputs.shape, BF16),
            shape(*d_inputs.shape),
        ),
        grid_spec=pltpu.PrefetchScalarGridSpec(
            num_scalar_prefetch=1,
            grid=(STEPS,),
            in_specs=[
                rows(width, first.shape[1]),
                rows(second.shape[0], width),
                *either(),
                *either(STEPS),
                *either(),
                *either(STEPS),
                *either(),
                *either(),
                whole(*small.shape),
                slab(outputs),
                slab(d_inputs),
            ],
            out_specs=(
                rows(width, inner),
                rows(width, dim),
                rows(width, dim),
                rows(second.shape[0], width),
                rows(units, width),
                rows(units, width),
                rows(units, width),
                whole(expert_count, width),
                whole(1, width),
                whole(1, width),
                whole(1, dim),
                whole(1, dim),
                slab(outputs),
                slab(d_inputs),
            ),
        ),
        compiler_params=pltpu.CompilerParams(vmem_limit_bytes=VMEM_LIMIT),
    )(
        section[None], first, second, in0, in1, in0, in1, got_in0, got_in1, got_in0, got_in1,
        down0, down1, got_down0, got_down1, small, outputs, d_inputs,
    )


def body(
    block_input,
    cotangent,
    segments,
    routes,
    norm_attn,
    w_query,
    key_matrix,
    value_matrix,
    norm_query,
    norm_key,
    w_output,
    norm_moe,
    w_router,
    w_gate,
    w_up,
    w_down,
):
    section = lax.axis_index("section")
    _, group_rows, width = block_input.shape
    expert_count = w_router.shape[2]
    quarter = group_rows // RING
    dim = norm_query.shape[1]

    dense_own = (w_query[0], key_matrix[0], value_matrix[0], w_output[0])
    expert_own = (jnp.swapaxes(w_gate[0], 1, 2), jnp.swapaxes(w_up[0], 1, 2), w_down[0])
    pack_own = jnp.concatenate(
        [
            jnp.pad(w_router[0].T, ((0, PACK_ROUTER - expert_count), (0, 0))),
            norm_attn,
            norm_moe,
            jnp.pad(jnp.concatenate([norm_query, norm_key], axis=1), ((0, PACK_ROWS - PACK_ROUTER - 3), (0, width - 2 * dim))),
        ],
        axis=0,
    )
    def pick(array):
        return lax.dynamic_index_in_dim(array, section, 0, keepdims=False)

    def quarters(array):
        return array.reshape(RING, quarter, array.shape[-1])

    segment = pick(segments)
    segs = (segment.reshape(group_rows, 1), segment.reshape(1, group_rows))

    routes = routes[0].reshape(2, RING, quarter, routes.shape[-1])
    rows_in = pick(block_input)
    upstream = quarters(pick(cotangent))
    shared = (upstream[:, :, : width // 2], upstream[:, :, width // 2 :])
    saved, layer_ins, outs, grads_all = [], [], [], []
    for layer in range(2):
        layer_ins.append(rows_in)
        if layer == 0:
            made = attend_mix(layer, rows_in, segs, pack_own, routes, dense_own, expert_own)
            packs, routes_other = (pack_own, made[7]), made[8]
            dense_other, expert_other = made[9:13], made[13:]
        else:
            made = attend_mix(layer, rows_in, segs, packs, (routes, routes_other), dense_own, dense_other)
        attn_saved, (mid, gates, rows_all) = made[:4], made[4:7]
        made, acts, spread = experts(layer, rows_all, shared[layer], mid, expert_own, expert_other)
        grads_all.append(spread)
        saved.append((attn_saved, mid, gates, rows_all, acts))
        if layer == 0:
            rows_in = made.reshape(group_rows, width)
            outs.append(made)

    attn_saved, mid, gates, rows_all, acts = saved[1]
    d_part, *terms, grad_in, grad_down, out_low, out_high = experts_back_sum(
        1, rows_all, grads_all, acts, mid, gates, packs, expert_own, expert_other, made, expert_count
    )
    outs += [out_low, out_high]
    grads_one = (grad_in, grad_down)
    d_all, *_, smalls_one, products_first, products_second = attend_back(
        1, layer_ins[1], segs, packs, attn_saved, upstream, d_part, terms[::-1], (), dense_own, dense_other
    )
    upstream = lax.dynamic_index_in_dim(
        d_all.reshape(RING * RING, RING, quarter, width), lax.axis_index("expert"), 0, keepdims=False
    )
    input_grads = [None, upstream]
    attn_saved, mid, gates, rows_all, acts = saved[0]
    partial, *grads_zero, first_own, second_own, got_in_one, got_down_one = experts_back(
        0, rows_all, [d_all], acts, expert_own, expert_other, ((products_first, products_second), grads_one, dense_own)
    )
    d_part, *terms = moe_back(0, partial, mid, gates, packs, expert_count)
    input_grads[0], *factors_zero, smalls_zero, first_one, second_one, got_in_zero, got_down_zero = attend_back(
        0, layer_ins[0], segs, packs, attn_saved, upstream, d_part, terms[::-1],
        (first_own, second_own, *grads_zero), dense_own, dense_other,
    )
    expert_grads = ((*grads_zero, got_in_zero, got_down_zero), (*grads_one, got_in_one, got_down_one))
    first, second, small, outputs, d_inputs = finish(
        factors_zero, (smalls_zero, smalls_one), (first_one, second_one), outs, input_grads
    )
    query, key, value, output, gate, up, down, router, gain_moe, gain_attn, gain_query, gain_key, outputs, d_inputs = widen(
        section, first.reshape(width, first.shape[-1]), second.reshape(-1, width), expert_grads, small, outputs, d_inputs,
        dim, expert_count,
    )
    units = w_gate.shape[3]

    def by_expert(array):
        return array.reshape(1, 2, units, width)

    return (
        outputs.reshape(1, 2, group_rows, width),
        d_inputs.reshape(1, 2, group_rows, width),
        gain_attn,
        query[None],
        key[None],
        value[None],
        gain_query,
        gain_key,
        output[None],
        gain_moe,
        router.T[None],
        jnp.swapaxes(by_expert(gate), 2, 3),
        jnp.swapaxes(by_expert(up), 2, 3),
        by_expert(down),
    )


def solution(mesh):
    placed = (
        P(None, "expert", None),
        P(None, "expert", None),
        P(None, "expert", None),
        P("section", None, "expert", None),
        P("section", None),
        P("section", None, "tensor"),
        P("section", None, "tensor"),
        P("section", None, "tensor"),
        P("section", None),
        P("section", None),
        P("section", "tensor", None),
        P("section", None),
        P("section", None, None),
        P("section", "expert", None, "tensor"),
        P("section", "expert", None, "tensor"),
        P("section", "expert", "tensor", None),
    )
    return jax.shard_map(
        body,
        mesh=mesh,
        in_specs=placed,
        out_specs=(
            P("section", None, "expert", None),
            P("section", None, "expert", None),
            P("section", None),
            P("section", None, "tensor"),
            P("section", None, "tensor"),
            P("section", None, "tensor"),
            P("section", None),
            P("section", None),
            P("section", "tensor", None),
            P("section", None),
            P("section", None, None),
            P("section", "expert", None, "tensor"),
            P("section", "expert", None, "tensor"),
            P("section", "expert", "tensor", None),
        ),
        check_vma=False,
    )
```

```python
import functools
import math

import jax
import jax.numpy as jnp
from jax import lax
from jax.experimental import pallas as pl
from jax.experimental.pallas import tpu as pltpu
from jax.sharding import PartitionSpec as P

RING = 4
BF16 = jnp.bfloat16
F32 = jnp.float32


def wrap(value):
    return lax.rem(value + 2 * RING, RING)


class Place:
    def __init__(self):
        self.section = lax.axis_index("section")
        expert = lax.axis_index("expert")
        self.x = lax.axis_index("tensor")
        self.z = lax.div(expert, RING)
        self.y = lax.rem(expert, RING)

    def index(self, axis):
        return getattr(self, axis)

    def device(self, axis, delta):
        at = {"x": self.x, "y": self.y, "z": self.z}
        at[axis] = wrap(at[axis] + delta)
        return (self.section, at["z"] * RING + at["y"], at["x"])

    def peer(self):
        return (1 - self.section, self.z * RING + self.y, self.x)


def greet(devices):
    barrier = pltpu.get_barrier_semaphore()
    for device in devices:
        pl.semaphore_signal(barrier, inc=1, device_id=device, device_id_type=pl.DeviceIdType.MESH)
    return lambda: pl.semaphore_wait(barrier, len(devices))


def meet(devices):
    greet(devices)()


class Copy:
    def __init__(self, sender, copy):
        self.sender, self.copy = sender, copy

    def wait_recv(self):
        self.sender.when(self.copy.wait_recv)


class Sender:
    def __init__(self, send_sems, recv_sems, flag=None):
        self.send_sems, self.recv_sems = send_sems, recv_sems
        self.flag = flag
        self.used = 0
        self.started = []

    def when(self, effect):
        if self.flag is None:
            effect()
        else:
            pl.when(self.flag)(effect)

    def make(self, source, target, device):
        copy = pltpu.make_async_remote_copy(
            src_ref=source,
            dst_ref=target,
            send_sem=self.send_sems.at[self.used],
            recv_sem=self.recv_sems.at[self.used],
            device_id=device,
            device_id_type=pl.DeviceIdType.MESH,
        )
        return copy

    def send(self, source, target, device):
        copy = self.make(source, target, device)
        self.used += 1
        self.when(copy.start)
        self.started.append(copy)
        return Copy(self, copy)

    def send_either(self, flag, source, otherwise, target, device):
        first, second = self.make(source, target, device), self.make(otherwise, target, device)
        self.used += 1
        pl.when(flag)(first.start)
        pl.when(jnp.logical_not(flag))(second.start)
        self.started.append(first)
        return Copy(self, first)

    def hand(self, flag, pairs, device):
        copies = []
        for source, target in pairs:
            copies.append(self.make(source, target, device))
            self.used += 1

        @pl.when(flag)
        def _():
            for copy in copies:
                copy.start()

        def settle():
            @pl.when(flag)
            def _():
                for copy in copies:
                    copy.wait_send()

            @pl.when(jnp.logical_not(flag))
            def _():
                for copy in copies:
                    copy.wait_recv()

        return settle

    def finish(self):
        def effect():
            for copy in self.started:
                copy.wait_send()

        self.when(effect)


def paced(job, points):
    count = iter(range(1000))

    def step():
        if next(count) in points:
            next(job, None)

    return step


def run(job):
    for _ in job:
        pass


def cut(width, count):
    tiles = width // 128
    edges = [tiles * i // count for i in range(count + 1)]
    return [(128 * a, 128 * (b - a)) for a, b in zip(edges[:-1], edges[1:])]


def region(place, order, phase, at, columns):
    spot = {}
    for i, axis in enumerate(order):
        spot[axis] = slice(None) if i < phase else (at if i == phase else place.index(axis))
    return (*[spot[axis] for axis in "zyx" if axis in spot], slice(None), pl.ds(*columns))


SENDS = 3 * (3 + 3 + 6)


def halves(columns):
    left, right = cut(columns[1], 2)
    return (columns[0] + left[0], left[1]), (columns[0] + right[0], right[1])


def thirds(buffer):
    return [(buffer, order, columns) for order, columns in zip(("xyz", "yzx", "zxy"), cut(buffer.shape[-1], 3))]


def gather(place, sender, plans, own=None, settle=None, beside=()):
    last_phase = len(plans[0][1]) - 1
    for phase in range(last_phase + 1):
        waits = []
        for buffer, order, columns in plans:
            axis = order[phase]
            me = place.index(axis)

            def push(delta, piece, buffer=buffer, order=order, axis=axis, me=me):
                here = buffer.at[region(place, order, phase, me, piece)]
                source = own.at[:, pl.ds(*piece)] if own is not None and phase == 0 else here
                return sender.send(source, here, place.device(axis, delta))

            if phase == last_phase:
                left, right = halves(columns)
                onward = (push(1, left), push(-1, right))
                waits += [push(1, right), push(-1, left)]
                waits.append((onward, buffer, order, axis, me, left, right))
            else:
                waits += [push(1, columns), push(-1, columns), push(2, columns)]
        if phase < len(beside):
            beside[phase]()
        yield
        last = []
        for wait in waits:
            if isinstance(wait, tuple):
                (up, down), buffer, order, axis, me, left, right = wait
                up.wait_recv()
                passing = buffer.at[region(place, order, phase, wrap(me - 1), left)]
                last.append(sender.send(passing, passing, place.device(axis, 1)))
                down.wait_recv()
                passing = buffer.at[region(place, order, phase, wrap(me + 1), right)]
                last.append(sender.send(passing, passing, place.device(axis, -1)))
            else:
                last.append(wait)
        if phase == last_phase:
            yield
        for copy in last:
            copy.wait_recv()
        if phase == 0 and settle is not None:
            settle()


def in_turn(jobs):
    jobs = list(jobs)
    while jobs:
        for job in list(jobs):
            try:
                next(job)
            except StopIteration:
                jobs.remove(job)
        if jobs:
            yield


def neighbours(place, axes="xyz"):
    return [place.device(axis, delta) for axis in axes for delta in (1, -1, 2)]


def reduce(place, sender, plans, slots, beside=()):
    last_phase = len(plans[0][1]) - 1
    for turn_number, phase in enumerate(range(last_phase, -1, -1)):
        waits = []
        for (buffer, order, columns), slot in zip(plans, slots):
            axis, slot = order[phase], slot[phase]
            me = place.index(axis)

            def push(delta, at, piece, target, buffer=buffer, order=order, axis=axis, me=me):
                source = buffer.at[region(place, order, phase, wrap(me + at), piece)]
                return sender.send(source, target, place.device(axis, delta))

            if phase == last_phase:
                left, right = halves(columns)
                up, down = push(1, 2, left, slot[0]), push(-1, 2, right, slot[1])
                near = push(1, 1, right, slot[2]), push(-1, -1, left, slot[3])
                waits.append((push, up, down, near))
            else:
                waits.append([push(delta, delta, columns, slot[i]) for i, delta in enumerate((1, -1, 2))])
        if turn_number < len(beside):
            beside[turn_number]()
        yield
        if phase == last_phase:
            later = []
            for (buffer, order, columns), slot, (push, up, down, near) in zip(plans, slots, waits):
                slot = slot[phase]
                me = place.index(order[phase])
                left, right = halves(columns)
                up.wait_recv()
                add_into(sender, buffer, region(place, order, phase, wrap(me + 1), left), slot[0])
                on_up = push(1, 1, left, slot[4])
                down.wait_recv()
                add_into(sender, buffer, region(place, order, phase, wrap(me - 1), right), slot[1])
                on_down = push(-1, -1, right, slot[5])
                later.append((*near, on_up, on_down))
            yield
            for (buffer, order, columns), slot, copies in zip(plans, slots, later):
                slot = slot[phase]
                me = place.index(order[phase])
                left, right = halves(columns)
                for copy in copies:
                    copy.wait_recv()
                add_into(sender, buffer, region(place, order, phase, me, left), slot[3], slot[4])
                add_into(sender, buffer, region(place, order, phase, me, right), slot[2], slot[5])
        else:
            for (buffer, order, columns), slot, copies in zip(plans, slots, waits):
                for copy in copies:
                    copy.wait_recv()
                add_into(sender, buffer, region(place, order, phase, place.index(order[phase]), columns), *slot[phase])


def slot_scratch(plans):
    scratch = []
    for rows, axes, columns in plans:
        left, right = halves(columns)
        for phase in range(axes):
            widths = (left, right, right, left, left, right) if phase == axes - 1 else (columns,) * 3
            scratch += [pltpu.VMEM((RING,) * phase + (rows, width), BF16) for _, width in widths]
    return scratch


def third_slots(rows, columns):
    return slot_scratch([(rows, 3, piece) for piece in cut(columns, 3)])


def sort_slots(refs, plans, axes):
    refs = list(refs)
    counts = [6 if phase == axes - 1 else 3 for phase in range(axes)]
    return [[[refs.pop(0) for _ in range(count)] for count in counts] for _ in range(plans)]


def add_into(sender, buffer, at, *terms):
    *spots, rows, columns = at
    free = [i for i, spot in enumerate(spots) if isinstance(spot, slice)]

    def some(first):
        spot = list(spots)
        picks = [slice(None)] * len(free)
        if first is not None:
            spot[free[0]] = first
            picks[0] = first
        here = (*spot, rows, columns)
        total = buffer[here].astype(F32)
        for term in terms:
            total = total + term[(*picks, slice(None), slice(None))].astype(F32)
        buffer[here] = total.astype(BF16)

    def all_blocks():
        if free:
            for i in range(RING):
                some(i)
        else:
            some(None)

    sender.when(all_blocks)


EPS = 1e-06
THETA = 1000000.0
MASKED = -1e30
GATED = 128
VMEM_LIMIT = 56 << 20


def params(number, vmem=VMEM_LIMIT):
    return pltpu.CompilerParams(collective_id=number, has_side_effects=True, vmem_limit_bytes=vmem)


IN_VMEM = pl.BlockSpec(memory_space=pltpu.VMEM)
ANYWHERE = pl.BlockSpec(memory_space=pl.ANY)


def copy_sems(count):
    return [pltpu.SemaphoreType.DMA((count,)), pltpu.SemaphoreType.DMA((count,))]


def dot_nn(left, right):
    return lax.dot_general(left, right, (((1,), (0,)), ((), ())), preferred_element_type=F32)


def dot_nt(left, right):
    return lax.dot_general(left, right, (((1,), (1,)), ((), ())), preferred_element_type=F32)


def dot_tn(left, right):
    return lax.dot_general(left, right, (((0,), (0,)), ((), ())), preferred_element_type=F32)


def inverse_rms(rows):
    return lax.rsqrt(jnp.mean(rows * rows, axis=-1, keepdims=True) + EPS)


def rms_back(rows, gain, grad):
    scale = inverse_rms(rows)
    unit = rows * scale
    lifted = grad * gain
    return scale * (lifted - unit * jnp.mean(lifted * unit, axis=-1, keepdims=True)), grad * unit


def send_x(place, sender, part, slots):
    return [
        sender.send(part.at[wrap(place.x + delta)], slots.at[i], place.device("x", delta))
        for i, delta in enumerate((1, -1, 2))
    ]


def sum_x(place, copies, part, slots):
    for copy in copies:
        copy.wait_recv()
    total = part[place.x].astype(F32)
    for i in range(3):
        total = total + slots[i].astype(F32)
    return total


def gather_x(place, sender, whole):
    mine = whole.at[place.x]
    copies = [sender.send(mine, mine, place.device("x", delta)) for delta in (1, -1, 2)]
    for copy in copies:
        copy.wait_recv()


def settle_job(place, sender, load, buffer, slots, mid, out):
    if load is not None:
        load.wait()
    yield from reduce(place, sender, thirds(buffer), sort_slots(slots, 3, 3))
    moe_rows = buffer[place.z, place.y, place.x].astype(F32)
    out[place.x] = (mid[...] + moe_rows).astype(BF16)
    mine = out.at[place.x]
    copies = [sender.send(mine, mine, place.device("x", delta)) for delta in (1, -1, 2)]
    yield
    for copy in copies:
        copy.wait_recv()


def part_columns(part, width):
    half = width // 2
    return pl.ds(part * half, half)


def settle_part(part, place, sems, partial, mid, out, scratch):
    sender = Sender(*sems)
    buffer, sem, *slots = scratch
    columns = part_columns(part, mid.shape[1])
    load = pltpu.make_async_copy(partial.at[:, :, :, :, columns], buffer, sem)
    load.start()
    return settle_job(place, sender, load, buffer, slots, mid.at[:, columns], out), sender


def settle_scratch(partial):
    *blocks, rows, width = partial.shape
    half = width // 2
    return [
        *copy_sems(3 + SENDS),
        pltpu.VMEM((*blocks, rows, half), BF16),
        pltpu.SemaphoreType.DMA,
        *third_slots(rows, half),
    ]


SETTLE_SCRATCH = 2 + 2 + 36


def moe_back_rows(layer, place, sender, buffer, mid, gates, pack0, pack1, d_part, gain_term, router_term):
    gain = of_layer(layer, pack0[PACK_ROUTER + 1 : PACK_ROUTER + 2], pack1[PACK_ROUTER + 1 : PACK_ROUTER + 2]).astype(F32)
    router = of_layer(layer, pack0[:PACK_ROUTER], pack1[:PACK_ROUTER])
    width = mid.shape[1]
    sums = buffer[place.z, place.y, place.x].astype(F32)
    weights = gates[...]
    d_gates = sums[:, width:]
    d_logits = (weights * (d_gates - jnp.sum(d_gates * weights, axis=-1, keepdims=True))).astype(BF16)
    d_moe_in = sums[:, :width] + dot_nn(d_logits, router)
    mid_rows = mid[...]
    d_mid, terms = rms_back(mid_rows, gain, d_moe_in)
    d_part[place.x] = d_mid.astype(BF16)
    gather_x(place, sender, d_part)
    gain_term[...] = jnp.sum(terms, axis=0, keepdims=True)
    moe_in = (mid_rows * inverse_rms(mid_rows) * gain).astype(BF16)
    router_term[...] = dot_tn(d_logits, moe_in)[: router_term.shape[0]]


def moe_back_kernel(
    layer, partial, mid, gates, pack0, pack1, d_part, gain_term, router_term, buffer, send, recv, local, *slots
):
    place = Place()
    load = pltpu.make_async_copy(partial, buffer, local)
    load.start()
    meet(neighbours(place))
    sender = Sender(send, recv)
    load.wait()
    run(reduce(place, sender, thirds(buffer), sort_slots(slots, 3, 3)))
    moe_back_rows(layer, place, sender, buffer, mid, gates, pack0, pack1, d_part, gain_term, router_term)
    sender.finish()


def moe_back(layer, partial, mid, gates, packs, expert_count):
    rows, width = mid.shape
    return pl.pallas_call(
        functools.partial(moe_back_kernel, layer),
        name="moe_back",
        out_shape=(
            jax.ShapeDtypeStruct((RING, rows, width), BF16),
            jax.ShapeDtypeStruct((1, width), F32),
            jax.ShapeDtypeStruct((expert_count, width), F32),
        ),
        in_specs=[ANYWHERE] + [IN_VMEM] * 4,
        out_specs=(IN_VMEM,) * 3,
        scratch_shapes=[
            pltpu.VMEM(partial.shape, BF16),
            *copy_sems(3 + SENDS),
            pltpu.SemaphoreType.DMA,
            *third_slots(rows, width + GATED),
        ],
        compiler_params=params(5 + layer),
    )(partial, mid, gates, *packs)


TILE = 256


def load_weights(layer, own, other, targets, sems):
    gate, up, down = targets
    half = gate.shape[0] // 2
    section = lax.axis_index("section")

    def pairs(source):
        return [
            (source[0].at[0], gate.at[pl.ds(0, half)]),
            (source[0].at[1], gate.at[pl.ds(half, half)]),
            (source[1].at[0], up.at[pl.ds(0, half)]),
            (source[1].at[1], up.at[pl.ds(half, half)]),
            (source[2].at[0], down.at[pl.ds(0, half)]),
            (source[2].at[1], down.at[pl.ds(half, half)]),
        ]

    @pl.when(section == layer)
    def _():
        for i, (source, target) in enumerate(pairs(own)):
            pltpu.make_async_copy(source, target, sems.at[i]).start()

    @pl.when(section != layer)
    def _():
        for i, (source, target) in enumerate(pairs(other)):
            pltpu.make_async_copy(source, target, sems.at[i]).start()

    return [pltpu.make_async_copy(source, target, sems.at[i]) for i, (source, target) in enumerate(pairs(own))]


def gate_columns(table, half):
    first = 2 * lax.axis_index("expert")
    lanes = lax.broadcasted_iota(jnp.int32, table.shape, 1)
    table = table.astype(F32)
    one = jnp.sum(jnp.where(lanes == first, table, 0.0), axis=1, keepdims=True)
    two = jnp.sum(jnp.where(lanes == first + 1, table, 0.0), axis=1, keepdims=True)
    units = lax.broadcasted_iota(jnp.int32, (table.shape[0], 2 * half), 1)
    return jnp.where(units < half, one, two)


class Stream:
    def __init__(self, hbm, slots, sems):
        self.hbm, self.slots, self.sems = hbm, slots, sems

    def copies(self, i, out):
        tile = self.slots.shape[1]
        rows = pl.ds(i * tile, tile)
        made = []
        at = 0
        for n, ref in enumerate(self.hbm):
            far, near = ref.at[rows], self.slots.at[i % 2, :, pl.ds(at, ref.shape[1])]
            at += ref.shape[1]
            pair = (near, far) if out else (far, near)
            made.append(pltpu.make_async_copy(*pair, self.sems.at[i % 2, n]))
        return made

    def fetch(self, i):
        for copy in self.copies(i, False):
            copy.start()

    def fetched(self, i):
        for copy in self.copies(i, False):
            copy.wait()
        return self.slots.at[i % 2]

    def store(self, i):
        for copy in self.copies(i, True):
            copy.start()

    def stored(self, i):
        for copy in self.copies(i, True):
            copy.wait()


def stream_scratch(widths, pieces=1, tile=TILE):
    scratch = []
    for width in widths:
        scratch += [pltpu.VMEM((2, tile, width), BF16), pltpu.SemaphoreType.DMA((2, pieces))]
    return scratch


BLOCKS = 8
SETTLE_POINTS = (3, 6)
SUM_POINTS = (4, 9)


def expert_back_kernel(layer, pieces, rows, *refs):
    refs = list(refs)

    def take(count):
        taken = refs[:count]
        del refs[:count]
        return taken

    grads, (acts,), own, other = take(pieces), take(1), take(3), take(3)
    extra = take(4)
    out, grad_in, grad_down = take(3)
    made = take(4)
    gate, up, down, sum_in, sum_down, sems = take(6)
    row_slots, row_sems, grad_slots, grad_sems, act_slots, act_sems, out_slots, out_sems, send, recv, local = take(11)
    place = Place()
    peer = place.peer()
    width = grad_in.shape[1]
    units = gate.shape[0]
    tiles = rows.shape[0] // TILE
    met = greet([peer, *neighbours(place, "yz")])
    upper = place.section == 1
    sender = Sender(send, recv, upper)
    first_own, second_own, got_in, got_down = made
    first, second, *slots = refs[:-2]
    loads = [pltpu.make_async_copy(*pair, local.at[i]) for i, pair in enumerate(zip(extra[:2], (first, second)))]
    for copy in loads:
        sender.when(copy.start)
    handing = Sender(refs[-2], refs[-1])

    def side():
        met()
        state["handed"] = handing.hand(place.section == 0, [(extra[2], got_in), (extra[3], got_down)], peer)
        for copy in loads:
            sender.when(copy.wait)
        yield from in_turn(gradient_reduces(place, sender, first, second, slots))
        first_own[...] = first[place.z, place.y]
        second_own[...] = second[place.z, place.y]

    state = {}
    job = side()

    weights = load_weights(layer, own, other, (gate, up, down), sems)
    ins, ups = Stream([rows], row_slots, row_sems), Stream(grads, grad_slots, grad_sems)
    kept, outs = Stream([acts], act_slots, act_sems), Stream([out], out_slots, out_sems)
    for stream in (ins, ups, kept):
        stream.fetch(0)
    next(job)
    step = paced(job, SUM_POINTS)
    first_expert = 2 * lax.axis_index("expert")
    for i in range(tiles):
        for stream in (ins, ups, kept):
            if i + 1 < tiles:
                stream.fetch(i + 1)
        tile, grad, act = ins.fetched(i), ups.fetched(i)[...], kept.fetched(i)
        if i == 0:
            for copy in weights:
                copy.wait()
        gates = gate_columns(tile[:, width:], units // 2)
        back = dot_nt(grad, down[...])
        gate_act = act[:, :units].astype(F32)
        up_act = act[:, units:].astype(F32)
        sigmoid = 1.0 / (1.0 + jnp.exp(-gate_act))
        silu = gate_act * sigmoid
        hidden = silu * up_act
        products = hidden * back
        in_one = lax.broadcasted_iota(jnp.int32, products.shape, 1) < units // 2
        one = jnp.sum(jnp.where(in_one, products, 0.0), axis=1, keepdims=True)
        two = jnp.sum(jnp.where(in_one, 0.0, products), axis=1, keepdims=True)
        lanes = lax.broadcasted_iota(jnp.int32, (products.shape[0], GATED), 1)
        d_gates = jnp.where(lanes == first_expert, one, jnp.where(lanes == first_expert + 1, two, 0.0))
        d_hidden = back * gates
        d_gate = (d_hidden * up_act * sigmoid * (1.0 + gate_act * (1.0 - sigmoid))).astype(BF16)
        d_up = (d_hidden * silu).astype(BF16)
        if i >= 2:
            outs.stored(i - 2)
        out_slots[i % 2, :, :width] = (dot_nn(d_gate, gate[...]) + dot_nn(d_up, up[...])).astype(BF16)
        out_slots[i % 2, :, width:] = d_gates.astype(BF16)
        outs.store(i)
        step()
        moe_in = tile[:, :width]
        terms = (
            (sum_in, slice(0, units), dot_tn(d_gate, moe_in)),
            (sum_in, slice(units, 2 * units), dot_tn(d_up, moe_in)),
            (sum_down, slice(0, units), dot_tn((hidden * gates).astype(BF16), grad)),
        )
        for total, at, term in terms:
            if i == 0:
                total[at] = term
            elif i < tiles - 1:
                total[at] += term
            else:
                low = grad_in if total is sum_in else grad_down
                low[at] = (total[at] + term).astype(BF16)
        step()
    run(job)
    for i in (tiles - 2, tiles - 1):
        outs.stored(i)
    sender.finish()
    state["handed"]()


def expert_back_sum_kernel(layer, pieces, rows, *refs):
    refs = list(refs)

    def take(count):
        taken = refs[:count]
        del refs[:count]
        return taken

    grads, (acts, mid, gates, pack0, pack1), own, other = take(pieces), take(5), take(3), take(3)
    above = take(1)[0]
    d_part, gain_term, router_term, grad_in, grad_down, *settled = take(6)
    gate, up, down, sems, row_all, grad_all, act_all, hiddens, load_sems = take(9)
    settle_refs = [take(SETTLE_SCRATCH) for _ in settled]
    send, recv, buffer, *slots = refs
    place = Place()
    met = greet(neighbours(place))
    sender = Sender(send, recv)
    parts = [
        settle_part(part, place, held[:2], above, mid, out, held[2:])
        for part, (out, held) in enumerate(zip(settled, settle_refs))
    ]
    settling = in_turn([job for job, _ in parts])
    weights = load_weights(layer, own, other, (gate, up, down), sems)
    quarter = buffer.shape[3]
    tile_rows = BLOCKS * quarter
    tiles = rows.shape[0] // tile_rows
    width = mid.shape[1]
    units = gate.shape[0]

    def loads(i):
        at = pl.ds(i * tile_rows, tile_rows)
        pairs = [(rows.at[at], row_all.at[at]), (acts.at[at], act_all.at[at])]
        start = 0
        for ref in grads:
            pairs.append((ref.at[at], grad_all.at[at, pl.ds(start, ref.shape[1])]))
            start += ref.shape[1]
        return [pltpu.make_async_copy(*pair, load_sems.at[i, n]) for n, pair in enumerate(pairs)]

    for i in range(tiles):
        for load in loads(i):
            load.start()
    for copy in weights:
        copy.wait()
    met()
    next(settling)
    first_expert = 2 * lax.axis_index("expert")
    for i in range(tiles):
        if i in SETTLE_POINTS:
            next(settling)
        for load in loads(i):
            load.wait()
        at = slice(i * tile_rows, (i + 1) * tile_rows)
        weight = gate_columns(row_all[at, width:], units // 2)
        back = dot_nt(grad_all[at], down[...])
        gate_act = act_all[at, :units].astype(F32)
        up_act = act_all[at, units:].astype(F32)
        sigmoid = 1.0 / (1.0 + jnp.exp(-gate_act))
        silu = gate_act * sigmoid
        hidden = silu * up_act
        products = hidden * back
        in_one = lax.broadcasted_iota(jnp.int32, products.shape, 1) < units // 2
        one = jnp.sum(jnp.where(in_one, products, 0.0), axis=1, keepdims=True)
        two = jnp.sum(jnp.where(in_one, 0.0, products), axis=1, keepdims=True)
        lanes = lax.broadcasted_iota(jnp.int32, (products.shape[0], GATED), 1)
        d_gates = jnp.where(lanes == first_expert, one, jnp.where(lanes == first_expert + 1, two, 0.0))
        d_hidden = back * weight
        d_gate = (d_hidden * up_act * sigmoid * (1.0 + gate_act * (1.0 - sigmoid))).astype(BF16)
        d_up = (d_hidden * silu).astype(BF16)
        act_all[at, :units] = d_gate
        act_all[at, units:] = d_up
        hiddens[at] = (hidden * weight).astype(BF16)
        d_rows = dot_nn(d_gate, gate[...]) + dot_nn(d_up, up[...])
        for n in range(BLOCKS):
            block = i * BLOCKS + n
            here = (block // (RING * RING), block // RING % RING, block % RING)
            piece = slice(n * quarter, (n + 1) * quarter)
            buffer[(*here, slice(None), slice(0, width))] = d_rows[piece].astype(BF16)
            buffer[(*here, slice(None), slice(width, None))] = d_gates[piece].astype(BF16)

    def products_job():
        step = 2 * LANES
        for target, source, inputs in ((grad_in, act_all, row_all), (grad_down, hiddens, grad_all)):
            for start in range(0, target.shape[0], step):
                size = min(step, target.shape[0] - start)
                term = dot_tn(source[:, start : start + size], inputs[:, :width])
                target[start : start + size] = term.astype(BF16)
                yield

    summing = reduce(place, sender, thirds(buffer), sort_slots(slots, 3, 3))
    making = products_job()
    for count in (2, 2, 1):
        next(summing)
        next(settling, None)
        for _ in range(count):
            next(making, None)
    run(in_turn([summing, settling]))
    run(making)
    moe_back_rows(layer, place, sender, buffer, mid, gates, pack0, pack1, d_part, gain_term, router_term)
    sender.finish()
    for _, settler in parts:
        settler.finish()


def experts_back_sum(layer, rows_all, grads_all, acts, mid, gates, packs, own, other, above, expert_count):
    quarter = rows_all.shape[3]
    count = RING**3 * quarter
    width = rows_all.shape[4] - GATED
    units = 2 * own[0].shape[1]
    grads = [g.reshape(count, g.shape[-1]) for g in grads_all]
    tiles = count // (BLOCKS * quarter)
    return pl.pallas_call(
        functools.partial(expert_back_sum_kernel, layer, len(grads)),
        name="experts_back_sum",
        out_shape=(
            jax.ShapeDtypeStruct((RING, quarter, width), BF16),
            jax.ShapeDtypeStruct((1, width), F32),
            jax.ShapeDtypeStruct((expert_count, width), F32),
            jax.ShapeDtypeStruct((2 * units, width), BF16),
            jax.ShapeDtypeStruct((units, width), BF16),
            jax.ShapeDtypeStruct((RING, quarter, width // 2), BF16),
        ),
        in_specs=[ANYWHERE] * (2 + len(grads)) + [IN_VMEM] * 4 + [ANYWHERE] * 7,
        out_specs=(IN_VMEM,) * 6,
        scratch_shapes=[pltpu.VMEM((units, width), BF16)] * 3
        + [
            pltpu.SemaphoreType.DMA((6,)),
            pltpu.VMEM((count, width + GATED), BF16),
            pltpu.VMEM((count, width), BF16),
            pltpu.VMEM((count, 2 * units), BF16),
            pltpu.VMEM((count, units), BF16),
            pltpu.SemaphoreType.DMA((tiles, 2 + len(grads))),
            *settle_scratch(above),
            *copy_sems(3 + SENDS),
            pltpu.VMEM(rows_all.shape, BF16),
            *third_slots(quarter, width + GATED),
        ],
        compiler_params=params(14 + layer),
    )(rows_all.reshape(count, width + GATED), *grads, acts, mid, gates, *packs, *own, *other, above)


def experts_back(layer, rows_all, grads_all, acts, own, other, extra):
    quarter = rows_all.shape[3]
    count = RING**3 * quarter
    width = rows_all.shape[4] - GATED
    units = 2 * own[0].shape[1]
    grads = [g.reshape(count, g.shape[-1]) for g in grads_all]
    products, grads_one, dense = extra
    first, second = gradient_shapes(dense)
    extra = (*products, *grads_one)
    extra_specs, made_specs = [ANYWHERE] * 4, (IN_VMEM, IN_VMEM, ANYWHERE, ANYWHERE)
    made = (
        jax.ShapeDtypeStruct(first[2:], BF16),
        jax.ShapeDtypeStruct(second[2:], BF16),
        jax.ShapeDtypeStruct(grads_one[0].shape, BF16),
        jax.ShapeDtypeStruct(grads_one[1].shape, BF16),
    )
    scratch = [
        *copy_sems(GRADIENT_SENDS),
        pltpu.SemaphoreType.DMA((2,)),
        pltpu.VMEM(first, BF16),
        pltpu.VMEM(second, BF16),
        *gradient_slots(first, second),
        *copy_sems(2),
    ]
    out, *rest = pl.pallas_call(
        functools.partial(expert_back_kernel, layer, len(grads)),
        name="experts_back",
        out_shape=(
            jax.ShapeDtypeStruct((count, width + GATED), BF16),
            jax.ShapeDtypeStruct((2 * units, width), BF16),
            jax.ShapeDtypeStruct((units, width), BF16),
            *made,
        ),
        in_specs=[ANYWHERE] * (1 + len(grads) + 1 + 6) + extra_specs,
        out_specs=(ANYWHERE, IN_VMEM, IN_VMEM, *made_specs),
        scratch_shapes=[pltpu.VMEM((units, width), BF16)] * 3
        + [pltpu.VMEM((2 * units, width), F32), pltpu.VMEM((units, width), F32), pltpu.SemaphoreType.DMA((6,))]
        + stream_scratch((width + GATED,))
        + stream_scratch((width,), len(grads))
        + stream_scratch((2 * units, width + GATED))
        + scratch,
        compiler_params=params(12 + layer),
    )(rows_all.reshape(count, width + GATED), *grads, acts, *own, *other, *extra)
    return (out.reshape(*rows_all.shape), *rest)


def pull(layer, own, other, targets, sems):
    section = lax.axis_index("section")

    @pl.when(section == layer)
    def _():
        for i, (source, target) in enumerate(zip(own, targets)):
            pltpu.make_async_copy(source, target, sems.at[i]).start()

    @pl.when(section != layer)
    def _():
        for i, (source, target) in enumerate(zip(other, targets)):
            pltpu.make_async_copy(source, target, sems.at[i]).start()

    return [pltpu.make_async_copy(source, target, sems.at[i]) for i, (source, target) in enumerate(zip(own, targets))]


def of_layer(layer, own, other):
    return jnp.where(lax.axis_index("section") == layer, own, other)


def tables(seg_row, dim):
    rows = seg_row.shape[1]
    at_row = lax.broadcasted_iota(jnp.int32, (rows, rows), 0)
    at_column = lax.broadcasted_iota(jnp.int32, (rows, rows), 1)
    seg_row = seg_row.astype(F32)
    seg_column = jnp.sum(jnp.where(at_row == at_column, seg_row, 0.0), axis=1, keepdims=True)
    earlier = jnp.sum((seg_row < seg_column).astype(F32), axis=1, keepdims=True)
    position = lax.broadcasted_iota(jnp.int32, (rows, dim), 0).astype(F32) - earlier
    lane = lax.broadcasted_iota(jnp.int32, (rows, dim), 1)
    half = dim // 2
    place = jnp.where(lane < half, lane, lane - half).astype(F32)
    angle = position * jnp.exp(place * (-math.log(THETA) / half))
    sine = jnp.sin(angle)
    return jnp.cos(angle), jnp.where(lane < half, -sine, sine), (seg_row == seg_column) & (at_column <= at_row)


def turn(rows, cosine, sine):
    return rows * cosine + pltpu.roll(rows, rows.shape[1] // 2, 1) * sine


def turn_back(grad, cosine, sine):
    return grad * cosine + pltpu.roll(grad * sine, grad.shape[1] // 2, 1)


PACK_ROUTER = 128
PACK_ROWS = 144
HEADS_STEP = 2
SETTLE_BESIDE = (0, 3)
WIDEN_POINTS = (0, 1, 3)


def fill_pack(pack, router, norm_attn, norm_moe, norm_query, norm_key):
    count, width = router.shape
    pack[:count] = router[...]
    pack[count:PACK_ROUTER] = jnp.zeros((PACK_ROUTER - count, width), BF16)
    heads = [norm_query[...].astype(F32), norm_key[...].astype(F32)]
    rest = width - sum(h.shape[1] for h in heads)
    heads = jnp.concatenate([*heads, jnp.zeros((1, rest), F32)], axis=1)
    row = lax.broadcasted_iota(jnp.int32, (PACK_ROWS - PACK_ROUTER, width), 0)
    gains = jnp.where(row == 2, heads, 0.0)
    gains = jnp.where(row == 1, norm_moe[...].astype(F32), gains)
    pack[PACK_ROUTER:] = jnp.where(row == 0, norm_attn[...].astype(F32), gains).astype(BF16)


def forward_kernel(
    layer, rows, segments, routes0, upstream, *refs
):
    refs = list(refs)

    def take(count):
        taken = refs[:count]
        del refs[:count]
        return taken

    if layer:
        (pack0, pack1, routes1), dense_own, dense_other, expert_own, expert_other = take(3), take(4), take(4), take(3), take(3)
        attended, query_raw, key_raw, value_low, mid, gates, rows_all, spread, acts, out = take(10)
    else:
        (router_own, norm_attn, norm_moe, norm_query, norm_key), dense_own, expert_own = take(5), take(4), take(3)
        attended, query_raw, key_raw, value_low, mid, gates, rows_all, spread, acts, out = take(10)
        (pack0, pack1, routes1), dense_other, expert_other = take(3), take(4), take(3)
    wq, wk, wv, wo, total, part, own, slots, sems, send, recv, local = take(12)
    share_send, share_recv, gate, up, down, expert_sems, all_in, act_slots, act_sems, named_all = take(10)
    place = Place()
    section = place.section
    if not layer:
        rows = rows.at[section]
    part_width = rows.shape[1] // 2
    shared = upstream.at[section, :, :, pl.ds(layer * part_width, part_width)]
    peer = place.peer()
    met = greet(neighbours(place) if layer else [peer, *neighbours(place)])
    keep_shared = pltpu.make_async_copy(shared.at[place.x], spread.at[place.z, place.y, place.x], local.at[1])
    keep_shared.start()
    sharer = Sender(share_send, share_recv)
    sharing = gather(place, sharer, thirds(spread), shared.at[place.x], keep_shared.wait)
    dim = wk.shape[1]
    heads = wq.shape[1] // dim
    step = HEADS_STEP * dim
    steps = heads // HEADS_STEP

    def pieces(q, k, v, o):
        made = [k, v]
        for i in range(steps):
            made += [q.at[:, pl.ds(i * step, step)], o.at[pl.ds(i * step, step)]]
        return made

    targets = pieces(wq, wk, wv, wo)
    ours, theirs = pieces(*dense_own), pieces(*dense_other)
    if layer:
        loads = pull(layer, ours, theirs, targets, sems)

        def arrive(i):
            loads[i].wait()

        fetching = load_weights(layer, expert_own, expert_other, (gate, up, down), expert_sems)
        met()
    else:
        lower = section == 0
        loads = [pltpu.make_async_copy(*pair, sems.at[i]) for i, pair in enumerate(zip(ours, targets))]
        late = [pltpu.make_async_copy(*pair, sems.at[i]) for i, pair in enumerate(zip(theirs, targets))]

        @pl.when(lower)
        def _():
            for load in loads:
                load.start()

        fill_pack(pack0, router_own, norm_attn, norm_moe, norm_query, norm_key)
        met()
        pusher = Sender(*take(2))
        first = [pusher.send(pack0, pack1, peer), pusher.send(routes0.at[1 - section], routes1, peer)]
        pushed = [pusher.send(*pair, peer) for pair in zip(ours, theirs)]
        for copy in first:
            copy.wait_recv()

        def prefetch(i):
            @pl.when(jnp.logical_not(lower))
            def _():
                pushed[i].wait_recv()
                late[i].start()

        def arrive(i):
            if i + 1 < len(pushed):
                prefetch(i + 1)
            loads[i].wait()

        prefetch(0)
    next(sharing)
    resid = rows[...].astype(F32)
    gain = of_layer(layer, pack0[PACK_ROUTER : PACK_ROUTER + 1], pack1[PACK_ROUTER : PACK_ROUTER + 1]).astype(F32)
    gains = of_layer(layer, pack0[PACK_ROUTER + 2 : PACK_ROUTER + 3], pack1[PACK_ROUTER + 2 : PACK_ROUTER + 3]).astype(F32)
    gain_query, gain_key = gains[:, :dim], gains[:, dim : 2 * dim]
    cosine, sine, allowed = tables(segments[place.section], dim)
    normed = (resid * inverse_rms(resid) * gain).astype(BF16)
    arrive(0)
    raw = dot_nn(normed, wk[...])
    key_raw[...] = raw
    key = turn(raw * inverse_rms(raw) * gain_key, cosine, sine).astype(BF16)
    arrive(1)
    value = dot_nn(normed, wv[...]).astype(BF16)
    value_low[...] = value
    for i in range(steps):
        if i == steps // 2:
            next(sharing)
        arrive(2 + 2 * i)
        raws = dot_nn(normed, wq[:, i * step : (i + 1) * step])
        query_raw[:, i * step : (i + 1) * step] = raws
        for h in range(HEADS_STEP):
            raw = raws[:, h * dim : (h + 1) * dim]
            query = turn(raw * inverse_rms(raw) * gain_query, cosine, sine).astype(BF16)
            scores = jnp.where(allowed, dot_nt(query, key) * (1.0 / math.sqrt(dim)), MASKED)
            raised = jnp.exp(scores - jnp.max(scores, axis=1, keepdims=True))
            probs = (raised / jnp.sum(raised, axis=1, keepdims=True)).astype(BF16)
            at = i * step + h * dim
            attended[:, at : at + dim] = dot_nn(probs, value).astype(BF16)
        arrive(3 + 2 * i)
        piece = dot_nn(attended[:, i * step : (i + 1) * step], wo[i * step : (i + 1) * step])
        if i == 0:
            total[...] = piece
        else:
            total[...] += piece
    quarter = part.shape[1]
    for i in range(part.shape[0]):
        part[i] = total[i * quarter : (i + 1) * quarter].astype(BF16)
        total[i * quarter : (i + 1) * quarter] = resid[i * quarter : (i + 1) * quarter]
    sender = Sender(send, recv)
    copies = send_x(place, sender, part, slots)
    if not layer:
        pushed_experts = [pusher.send(*pair, peer) for pair in zip(expert_own, expert_other)]
    chosen = of_layer(layer, routes0[section], routes1[...])
    number = lax.broadcasted_iota(jnp.int32, (GATED, chosen.shape[1]), 0)
    named = chosen[0:1] == number
    for i in range(1, chosen.shape[0]):
        named = named | (chosen[i : i + 1] == number)
    across = lax.broadcasted_iota(jnp.int32, (GATED, GATED), 0) == lax.broadcasted_iota(jnp.int32, (GATED, GATED), 1)
    named_all[...] = dot_tn(named.astype(F32).astype(BF16), across.astype(F32).astype(BF16))
    named = named_all[pl.ds(pl.multiple_of(place.x * quarter, 8), quarter)] > 0.5
    gain = of_layer(layer, pack0[PACK_ROUTER + 1 : PACK_ROUTER + 2], pack1[PACK_ROUTER + 1 : PACK_ROUTER + 2])
    router = of_layer(layer, pack0[:PACK_ROUTER], pack1[:PACK_ROUTER])
    mine = total[pl.ds(pl.multiple_of(place.x * quarter, 8), quarter)]
    mid_rows = mine + sum_x(place, copies, part, slots)
    mid[...] = mid_rows
    moe_in = (mid_rows * inverse_rms(mid_rows) * gain.astype(F32)).astype(BF16)
    logits = jnp.where(named, dot_nt(moe_in, router), MASKED)
    raised = jnp.where(named, jnp.exp(logits - jnp.max(logits, axis=-1, keepdims=True)), 0.0)
    weights = raised / jnp.sum(raised, axis=-1, keepdims=True)
    gates[...] = weights
    own[:, : moe_in.shape[1]] = moe_in
    own[:, moe_in.shape[1] :] = weights.astype(BF16)
    keep = pltpu.make_async_copy(own, all_in.at[place.z, place.y, place.x], local.at[0])
    keep.start()
    gathering = gather(place, sender, thirds(all_in), own, keep.wait)
    for _ in range(3):
        next(gathering)
    if not layer:
        for copy in pushed_experts:
            copy.wait_recv()
        fetching = load_weights(layer, expert_own, expert_other, (gate, up, down), expert_sems)
    run(gathering)
    store = pltpu.make_async_copy(all_in, rows_all, local.at[2])
    store.start()
    next(sharing)
    for copy in fetching:
        copy.wait()
    kept = Stream([acts], act_slots, act_sems)
    if layer:
        out_slots, out_sems = refs
        outs = Stream([out], out_slots, out_sems)
    else:
        settle_send, settle_recv, buffer, *settle_slots = refs
    width = gate.shape[1]
    units = gate.shape[0]
    tile_rows = BLOCKS * quarter
    tiles = acts.shape[0] // tile_rows
    half = BLOCKS // RING
    for i in range(tiles):
        at = i * half
        tile = all_in[at // RING, at % RING : at % RING + half].astype(F32).reshape(tile_rows, width + GATED)
        moe_in = tile[:, :width].astype(BF16)
        gate_act = dot_nt(moe_in, gate[...])
        up_act = dot_nt(moe_in, up[...])
        hidden = gate_act / (1.0 + jnp.exp(-gate_act)) * up_act
        hidden = hidden * gate_columns(tile[:, width:], units // 2)
        if i >= 2:
            kept.stored(i - 2)
        act_slots[i % 2, :, :units] = gate_act.astype(BF16)
        act_slots[i % 2, :, units:] = up_act.astype(BF16)
        kept.store(i)
        made = dot_nn(hidden.astype(BF16), down[...])
        if layer:
            if i >= 2:
                outs.stored(i - 2)
            out_slots[i % 2] = made.astype(BF16)
            outs.store(i)
        else:
            for n in range(BLOCKS):
                block = i * BLOCKS + n
                here = (block // (RING * RING), block // RING % RING, block % RING)
                buffer[here] = made[n * quarter : (n + 1) * quarter].astype(BF16)
        if i == SHARE_TILE:
            next(sharing)
    if layer:
        run(sharing)
        for i in (tiles - 2, tiles - 1):
            outs.stored(i)
    else:
        settler = Sender(settle_send, settle_recv)
        run(in_turn([settle_job(place, settler, None, buffer, settle_slots, mid, out), sharing]))
        settler.finish()

        @pl.when(lower)
        def _():
            for copy in pushed:
                copy.wait_recv()

        pusher.finish()
    for i in (tiles - 2, tiles - 1):
        kept.stored(i)
    store.wait()
    sharer.finish()
    sender.finish()


def weight_scratch(dense):
    return [pltpu.VMEM(w.shape, BF16) for w in dense]


SHARE_TILE = 4


def forward(layer, rows, segments, packs, routes, upstream, own, other, expert_own, expert_other):
    count, width = rows.shape[-2:]
    quarter = count // RING
    dim, inner = own[1].shape[1], own[0].shape[1]
    pieces = 2 + 2 * (inner // dim // HEADS_STEP)
    units = 2 * expert_own[0].shape[1]
    everyone = (RING, RING, RING, quarter)
    total = RING**3 * quarter
    tile = BLOCKS * quarter

    def like(array):
        return jax.ShapeDtypeStruct(array.shape, array.dtype)

    if layer:
        out, out_spec = (total, width), ANYWHERE
        swapped, swapped_specs, push = (), (), ()
        tail = stream_scratch((width,), tile=tile)
        inputs = (rows, segments, routes[0], upstream, *packs, routes[1], *own, *other, *expert_own, *expert_other)
    else:
        out, out_spec = (RING, quarter, width), IN_VMEM
        pack = jax.ShapeDtypeStruct((PACK_ROWS, width), BF16)
        swapped = (pack, pack, jax.ShapeDtypeStruct(routes.shape[1:], routes.dtype), *map(like, own), *map(like, expert_own))
        swapped_specs = (IN_VMEM,) * 3 + (ANYWHERE,) * 7
        push = copy_sems(2 + pieces + 3)
        tail = [*copy_sems(3 + SENDS), pltpu.VMEM((*everyone, width), BF16), *third_slots(quarter, width)]
        inputs = (rows, segments, routes, upstream, *packs, *own, *expert_own)
    return pl.pallas_call(
        functools.partial(forward_kernel, layer),
        name="forward",
        out_shape=(
            jax.ShapeDtypeStruct((count, inner), BF16),
            jax.ShapeDtypeStruct((count, inner), F32),
            jax.ShapeDtypeStruct((count, dim), F32),
            jax.ShapeDtypeStruct((count, dim), BF16),
            jax.ShapeDtypeStruct((quarter, width), F32),
            jax.ShapeDtypeStruct((quarter, GATED), F32),
            jax.ShapeDtypeStruct((*everyone, width + GATED), BF16),
            jax.ShapeDtypeStruct((*everyone, width // 2), BF16),
            jax.ShapeDtypeStruct((total, 2 * units), BF16),
            jax.ShapeDtypeStruct(out, BF16),
            *swapped,
        ),
        in_specs=[IN_VMEM] * (7 if layer else 9) + [ANYWHERE] * (14 if layer else 7),
        out_specs=(IN_VMEM,) * 6 + (ANYWHERE,) * 3 + (out_spec,) + swapped_specs,
        scratch_shapes=[
            *weight_scratch(own),
            pltpu.VMEM((count, width), F32),
            pltpu.VMEM((RING, quarter, width), BF16),
            pltpu.VMEM((quarter, width + GATED), BF16),
            pltpu.VMEM((3, quarter, width), BF16),
            pltpu.SemaphoreType.DMA((pieces,)),
            *copy_sems(3 + SENDS),
            pltpu.SemaphoreType.DMA((3,)),
            *copy_sems(SENDS),
            *[pltpu.VMEM((units, width), BF16)] * 3,
            pltpu.SemaphoreType.DMA((6,)),
            pltpu.VMEM((*everyone, width + GATED), BF16),
            *stream_scratch((2 * units,), tile=tile),
            pltpu.VMEM((count, GATED), F32),
            *push,
            *tail,
        ],
        compiler_params=params(1 + layer),
    )(*inputs)


SMALL = 48


def gradient_shapes(dense):
    width, inner = dense[0].shape
    proj = inner + 2 * dense[1].shape[1]
    blocks = RING * RING
    return (RING, RING, width // blocks, proj), (RING, RING, inner // blocks, width)


def gradient_plans(array):
    one, two = cut(array.shape[-1], 2)
    return [(array, "yz", one), (array, "zy", two)]


GRADIENT_SENDS = 2 * 18


def gradient_slots(first, second):
    scratch = []
    for shape in (first, second):
        one, two = cut(shape[3], 2)
        scratch += slot_scratch([(shape[2], 2, one), (shape[2], 2, two)])
    return scratch


def gradient_reduces(place, sender, first, second, slots, beside=()):
    return [
        reduce(place, sender, gradient_plans(first), sort_slots(slots[:18], 2, 2)),
        reduce(place, sender, gradient_plans(second), sort_slots(slots[18:], 2, 2), beside),
    ]


def gradient_gathers(place, sender, first, second, beside=()):
    return [
        gather(place, sender, gradient_plans(first)),
        gather(place, sender, gradient_plans(second), None, None, beside),
    ]


LANES = 128


def output_products(heads, mids, second):
    def blocks(i, _):
        pair = dot_tn(heads[:, pl.ds(pl.multiple_of(i * LANES, LANES), LANES)], mids[...]).astype(BF16)
        at = 2 * i
        second[lax.div(at, RING), lax.rem(at, RING)] = pair[: LANES // 2]
        second[lax.div(at, RING), lax.rem(at, RING) + 1] = pair[LANES // 2 :]
        return 0

    lax.fori_loop(0, heads.shape[1] // LANES, blocks, 0)


def input_products(normed, proj, first):
    def blocks(i, _):
        block = dot_tn(normed[:, pl.ds(pl.multiple_of(i * LANES, LANES), LANES)], proj[...])
        first[lax.div(i, RING), lax.rem(i, RING)] = block.astype(BF16)
        return 0

    lax.fori_loop(0, normed.shape[1] // LANES, blocks, 0)


def attend_back_kernel(
    layer, rows, segments, pack0, pack1, attended, query_raw, key_raw, value_low, upstream, d_part,
    router_term, moe_gain_term, *refs
):
    last = layer == 0
    refs = list(refs)
    extra = [refs.pop(0) for _ in range(8 if last else 2)]
    q0, k0, v0, o0, q1, k1, v1, o1, d_input, normed_both, d_proj, heads_both, d_mid_low, smalls = refs[:14]
    refs = refs[14:]
    wide = [refs.pop(0) for _ in range(7 if last else 4)]
    wq, wk, wv, wo, total, d_mid, d_heads, part, own, slots, sems, send, recv, local, *side = refs
    place = Place()
    peer = place.peer()
    met = greet([peer, *neighbours(place)])
    if last:
        rows = rows.at[place.section]
    else:
        upstream = upstream.at[place.section]
    count = rows.shape[0]
    job = iter(())
    theirs, ours = pl.ds(count, count), pl.ds(0, count)
    if last:
        upper = place.section == 1
        first_own, second_own, grad_in, grad_down, out_zero, out_low, out_high, grad_one = extra
        first, second, got_in, got_down, outputs, input_grads, second_sum = wide
        lower = place.section == 0
        swapper = Sender(side[4], side[5])
        half = out_low.shape[2]
        my_rows, my_grads = outputs.at[place.section], input_grads.at[place.section]
        row_pairs = []
        for piece, above in enumerate((out_low, out_high)):
            columns = pl.ds(piece * half, half)
            row_pairs.append((out_zero.at[:, :, columns], above, my_rows.at[:, :, columns]))

        def keep_rows(index, low, high, target):
            one, two = (pltpu.make_async_copy(origin, target, side[6].at[index]) for origin in (low, high))
            pl.when(lower)(one.start)
            pl.when(upper)(two.start)
            return one

        kept_rows = [keep_rows(i, *pair) for i, pair in enumerate(row_pairs)]
        side_sender = Sender(side[0], side[1], upper)
        handing = Sender(side[2], side[3])

        def widen():
            first[place.z, place.y] = first_own[...]
            second[place.z, place.y] = second_own[...]
            yield
            met()
            yield from in_turn(gradient_gathers(place, side_sender, first, second))

        job = widen()
        summer = Sender(side[7], side[8], lower)
        second_parts, *second_slots = side[9:]

        def sum_second():
            handed_early()
            pl.when(lower)(lambda: output_products(heads_both, d_mid_low, second_parts))
            yield from reduce(place, summer, gradient_plans(second_parts), sort_slots(second_slots, 2, 2))
            second_sum[...] = second_parts[place.z, place.y]

        summing = sum_second()
    else:
        settling, settler = settle_part(1, place, side[3:5], extra[1], extra[0], wide[2], side[5:])
    dim = wk.shape[1]
    heads = wq.shape[1] // dim
    inner = heads * dim
    step = HEADS_STEP * dim
    steps = heads // HEADS_STEP
    quarter = d_part.shape[1]

    def pieces(q, k, v, o):
        return [*[o.at[pl.ds(i * step, step)] for i in range(steps)],
                *[q.at[:, pl.ds(i * step, step)] for i in range(steps)], k, v]

    loads = pull(layer, pieces(q0, k0, v0, o0), pieces(q1, k1, v1, o1), pieces(wq, wk, wv, wo), sems)
    for i in range(RING):
        grad = upstream[i].astype(F32) + d_part[i].astype(F32)
        d_mid[i] = grad
        total[i * quarter : (i + 1) * quarter] = grad
    grad_low = total[...].astype(BF16)
    d_mid_low[:count] = grad_low
    heads_both[:count] = attended[...]
    resid = rows[...].astype(F32)
    gain = of_layer(layer, pack0[PACK_ROUTER : PACK_ROUTER + 1], pack1[PACK_ROUTER : PACK_ROUTER + 1]).astype(F32)
    gains = of_layer(layer, pack0[PACK_ROUTER + 2 : PACK_ROUTER + 3], pack1[PACK_ROUTER + 2 : PACK_ROUTER + 3]).astype(F32)
    gain_query, gain_key = gains[:, :dim], gains[:, dim : 2 * dim]
    cosine, sine, allowed = tables(segments[place.section], dim)
    normed_both[:count] = (resid * inverse_rms(resid) * gain).astype(BF16)
    raw_key = key_raw[...]
    key = turn(raw_key * inverse_rms(raw_key) * gain_key, cosine, sine).astype(BF16)
    value = value_low[...]
    scale = 1.0 / math.sqrt(dim)
    d_key = jnp.zeros(key.shape, F32)
    d_value = jnp.zeros(key.shape, F32)
    gain_total = jnp.zeros(gain_query.shape, F32)
    handed_grads = None
    for i in range(steps):
        if i in WIDEN_POINTS:
            next(job, None)
        if not last and i in SETTLE_BESIDE:
            if i == 0:
                met()
            next(settling)
        if last and i == 1:
            handed_grads = handing.hand(upper, [(grad_in, got_in), (grad_down, got_down)], peer)
            handed_early = handing.hand(
                upper, [(ref.at[ours], ref.at[theirs]) for ref in (heads_both, d_mid_low, normed_both)], peer
            )
            swaps = [swapper.send_either(lower, high, low, target, peer) for low, high, target in row_pairs]
        if last and i == steps - 1:
            next(summing)
        loads[i].wait()
        d_heads[...] = dot_nt(grad_low, wo[i * step : (i + 1) * step]).astype(BF16)
        for h in range(HEADS_STEP):
            at = i * step + h * dim
            raw = query_raw[:, at : at + dim]
            query = turn(raw * inverse_rms(raw) * gain_query, cosine, sine).astype(BF16)
            scores = jnp.where(allowed, dot_nt(query, key) * scale, MASKED)
            raised = jnp.exp(scores - jnp.max(scores, axis=1, keepdims=True))
            probs = raised / jnp.sum(raised, axis=1, keepdims=True)
            d_head = d_heads[:, h * dim : (h + 1) * dim]
            d_probs = dot_nt(d_head, value)
            d_value = d_value + dot_tn(probs.astype(BF16), d_head)
            d_scores = (probs * (d_probs - jnp.sum(d_probs * probs, axis=1, keepdims=True))).astype(BF16)
            d_query = turn_back(dot_nn(d_scores, key) * scale, cosine, sine)
            d_key = d_key + dot_tn(d_scores, query) * scale
            d_raw, terms = rms_back(raw, gain_query, d_query)
            gain_total = gain_total + jnp.sum(terms, axis=0, keepdims=True)
            d_proj[:count, at : at + dim] = d_raw.astype(BF16)
        loads[steps + i].wait()
        piece = dot_nt(d_proj[:count, i * step : (i + 1) * step], wq[:, i * step : (i + 1) * step])
        if i == 0:
            total[...] = piece
        else:
            total[...] += piece
    d_raw, terms = rms_back(raw_key, gain_key, turn_back(d_key, cosine, sine))
    d_proj[:count, inner : inner + dim] = d_raw.astype(BF16)
    d_proj[:count, inner + dim :] = d_value.astype(BF16)
    smalls[0, 32:] = jnp.zeros((SMALL - 32, smalls.shape[2]), F32)
    smalls[0, :32] = router_term[...]
    smalls[0, 32:33] = moe_gain_term[...]
    smalls[0, 34:35, :dim] = gain_total
    smalls[0, 34:35, dim : 2 * dim] = jnp.sum(terms, axis=0, keepdims=True)
    loads[2 * steps].wait()
    loads[2 * steps + 1].wait()
    total[...] += dot_nt(d_proj[:count, inner : inner + dim], wk[...]) + dot_nt(d_proj[:count, inner + dim :], wv[...])
    for i in range(RING):
        part[i] = total[i * quarter : (i + 1) * quarter].astype(BF16)
    sender = Sender(send, recv)
    copies = send_x(place, sender, part, slots)
    handed = sender.hand(
        place.section != layer,
        [(ref.at[ours], ref.at[theirs]) for ref in ((d_proj,) if last else (normed_both, d_proj, heads_both, d_mid_low))],
        peer,
    )
    if last:
        next(summing, None)
    mine = resid[:quarter]
    for i in range(1, RING):
        mine = jnp.where(place.x == i, resid[i * quarter : (i + 1) * quarter], mine)
    d_resid, terms = rms_back(mine, gain, sum_x(place, copies, part, slots))
    smalls[0, 33:34] = jnp.sum(terms, axis=0, keepdims=True)
    handed_small = sender.hand(place.section != layer, [(smalls.at[0], smalls.at[1])], peer)
    d_rows = (d_mid[place.x] + d_resid).astype(BF16)
    if last:
        d_input[place.x] = d_rows
        gather_x(place, sender, d_input)
        swaps.append(swapper.send_either(lower, grad_one, d_input, my_grads, peer))
        kept_rows.append(keep_rows(2, d_input, grad_one, my_grads))
    else:
        own[...] = d_rows
        keep = pltpu.make_async_copy(own, d_input.at[place.z, place.y, place.x], local)
        keep.start()
        spread = gather(place, sender, thirds(d_input), own, keep.wait)
        for _ in range(3):
            next(spread)
            next(settling, None)
    handed()
    handed_small()
    if not last:
        owner = place.section == layer
        products, copy_out = side[:2], side[2]
        stores = [pltpu.make_async_copy(*pair, copy_out.at[i]) for i, pair in enumerate(zip(products, wide))]

        @pl.when(owner)
        def _():
            output_products(heads_both, d_mid_low, products[1])

        next(spread)

        @pl.when(owner)
        def _():
            stores[1].start()
            input_products(normed_both, d_proj, products[0])
            stores[0].start()

        run(in_turn([spread, settling]))
        settler.finish()
        fetch = pltpu.make_async_copy(d_input.at[place.z, place.y], wide[3], local)
        fetch.start()
        fetch.wait()

        @pl.when(owner)
        def _():
            for store in stores:
                store.wait()

    sender.finish()
    if last:
        handed_grads()
        for copy in swaps:
            copy.wait_recv()
        for copy in kept_rows:
            copy.wait()
        run(in_turn([job, summing]))
        summer.finish()
        swapper.finish()
        side_sender.finish()


def attend_back(layer, rows, segments, packs, saved, upstream, d_part, terms, extra, own, other):
    last = layer == 0
    first, second = gradient_shapes(own)
    wide = tuple(jax.ShapeDtypeStruct(shape, BF16) for shape in (first, second))
    side = (pltpu.VMEM(first, BF16), pltpu.VMEM(second, BF16), pltpu.SemaphoreType.DMA((2,)))
    if last:
        both = (2, *d_part.shape)
        shapes = (first, second, extra[2].shape, extra[3].shape, both, both, second[2:])
        wide = tuple(jax.ShapeDtypeStruct(shape, BF16) for shape in shapes)
        side = (
            *copy_sems(GRADIENT_SENDS),
            *copy_sems(2 + 3),
            *copy_sems(3),
            pltpu.SemaphoreType.DMA((3,)),
            *copy_sems(18),
            pltpu.VMEM(second, BF16),
            *slot_scratch([(second[2], 2, piece) for piece in cut(second[3], 2)]),
        )
    else:
        wide += (jax.ShapeDtypeStruct((*d_part.shape[:2], d_part.shape[2] // 2), BF16), jax.ShapeDtypeStruct(d_part.shape, BF16))
        side += tuple(settle_scratch(extra[1]))

    count, width = rows.shape[-2:]
    quarter = count // RING
    dim, inner = own[1].shape[1], own[0].shape[1]
    out = (RING, quarter, width) if layer == 0 else (RING, RING, RING, quarter, width)
    return pl.pallas_call(
        functools.partial(attend_back_kernel, layer),
        name="attend_back_last" if layer == 0 else "attend_back",
        out_shape=(
            jax.ShapeDtypeStruct(out, BF16),
            jax.ShapeDtypeStruct((2 * count, width), BF16),
            jax.ShapeDtypeStruct((2 * count, inner + 2 * dim), BF16),
            jax.ShapeDtypeStruct((2 * count, inner), BF16),
            jax.ShapeDtypeStruct((2 * count, width), BF16),
            jax.ShapeDtypeStruct((2, SMALL, width), F32),
            *wide,
        ),
        in_specs=[IN_VMEM] * 12 + ([IN_VMEM] * 2 + [ANYWHERE] * 2 + [IN_VMEM] * 4 if last else [IN_VMEM, ANYWHERE]) + [ANYWHERE] * 8,
        out_specs=(IN_VMEM if last else ANYWHERE,) + (IN_VMEM,) * (7 if last else 5) + (ANYWHERE,) * (4 if last else 2) + (IN_VMEM,) * (1 if last else 2),
        scratch_shapes=[
            *weight_scratch(own),
            pltpu.VMEM((count, width), F32),
            pltpu.VMEM((RING, quarter, width), F32),
            pltpu.VMEM((count, HEADS_STEP * dim), BF16),
            pltpu.VMEM((RING, quarter, width), BF16),
            pltpu.VMEM((quarter, width), BF16),
            pltpu.VMEM((3, quarter, width), BF16),
            pltpu.SemaphoreType.DMA((2 + 2 * (inner // dim // HEADS_STEP),)),
            *copy_sems(3 + 5 + (3 if layer == 0 else SENDS)),
            pltpu.SemaphoreType.DMA,
            *side,
        ],
        compiler_params=params(7 + layer),
    )(rows, segments, *packs, *saved, upstream, d_part, *terms, *extra, *own, *other)


def finish_kernel(
    normed0, proj0, second_sum, small0, small1, first_one, second_one,
    first, second, small_out,
    first_sums, normed, proj, terms, passing, small_slots, send, recv, flagged_send,
    flagged_recv, local, *slots
):
    place = Place()
    lower = place.section == 0
    upper = place.section == 1
    met = greet(neighbours(place))
    sender = Sender(send, recv)
    reducer = Sender(flagged_send, flagged_recv, lower)

    def keep(index, source, otherwise, target):
        one, two = (pltpu.make_async_copy(origin, target, local.at[index]) for origin in (source, otherwise))
        pl.when(lower)(one.start)
        pl.when(upper)(two.start)
        return one

    pairs = [(small0, small1, terms)]
    loads = ((normed0, normed), (proj0, proj))
    loads = [pltpu.make_async_copy(*pair, local.at[1 + i]) for i, pair in enumerate(loads)]
    ready = [
        pltpu.make_async_copy(*pair, local.at[3 + i]) for i, pair in enumerate(((first_one, first), (second_one, second)))
    ]

    @pl.when(upper)
    def _():
        for copy in ready:
            copy.start()

    @pl.when(lower)
    def _():
        for copy in loads:
            copy.start()
        for copy in loads:
            copy.wait()
        input_products(normed, proj, first_sums)

    kept = [keep(i, *pair) for i, pair in enumerate(pairs)]
    kept[0].wait()
    met()
    state = {}

    def exchange(step, total):
        passing[...] = total
        buffer = small_slots.at[step, 3]
        buffer[...] = total.astype(BF16)
        state["copies"] = [
            sender.send(buffer, small_slots.at[step, i], place.device("xyz"[step], delta))
            for i, delta in enumerate((1, -1, 2))
        ]

    def collect(step):
        for copy in state["copies"]:
            copy.wait_recv()
        total = passing[...]
        for i in range(3):
            total = total + small_slots[step, i].astype(F32)
        return total

    def small_last():
        small_out[...] = collect(2)

    def first_step():
        exchange(0, terms[0] + terms[1])

    def second_step():
        exchange(1, collect(0))

    run(reduce(place, reducer, gradient_plans(first_sums), sort_slots(slots, 2, 2), (first_step, second_step)))

    @pl.when(lower)
    def _():
        first[place.z, place.y] = first_sums[place.z, place.y]
        second[place.z, place.y] = second_sum[...]

    beside = (lambda: exchange(2, collect(1)), small_last)
    run(in_turn(gradient_gathers(place, reducer, first, second, beside)))

    @pl.when(upper)
    def _():
        for copy in ready:
            copy.wait()

    sender.finish()
    reducer.finish()


def finish(factors, smalls, ready):
    first, second = ready[0].shape, ready[1].shape
    return pl.pallas_call(
        finish_kernel,
        name="finish",
        out_shape=(
            jax.ShapeDtypeStruct(first, BF16),
            jax.ShapeDtypeStruct(second, BF16),
            jax.ShapeDtypeStruct(smalls[0].shape[1:], F32),
        ),
        in_specs=[ANYWHERE] * 2 + [IN_VMEM] + [ANYWHERE] * 4,
        out_specs=(IN_VMEM,) * 3,
        scratch_shapes=[
            pltpu.VMEM(first, BF16),
            *[pltpu.VMEM(f.shape, BF16) for f in factors[:2]],
            pltpu.VMEM(smalls[0].shape, F32),
            pltpu.VMEM(smalls[0].shape[1:], F32),
            pltpu.VMEM((3, 4, *smalls[0].shape[1:]), BF16),
            *copy_sems(9),
            *copy_sems(18 + GRADIENT_SENDS),
            pltpu.SemaphoreType.DMA((5,)),
            *slot_scratch([(first[2], 2, piece) for piece in cut(first[3], 2)]),
        ],
        compiler_params=params(9),
    )(*factors, *smalls, *ready)


STEPS = 8


def widen_kernel(
    section, first, second, gate_own0, gate_own1, up_own0, up_own1, gate_got0, gate_got1, up_got0, up_got1,
    down_own0, down_own1, down_got0, down_got1, small, outputs_in, d_inputs_in,
    query, key, value, output, gate, up, down, router, gain_moe, gain_attn, gain_query, gain_key, outputs, d_inputs
):
    inner, dim = query.shape[1], key.shape[1]
    query[...] = first[:, :inner].astype(F32)
    key[...] = first[:, inner : inner + dim].astype(F32)
    value[...] = first[:, inner + dim :].astype(F32)
    output[...] = second[...].astype(F32)
    lower = section[0] == 0

    def either(low, high):
        return jnp.where(lower, low[...].astype(F32), high[...].astype(F32))

    gate[...] = either(gate_own0, gate_own1) + either(gate_got0, gate_got1)
    up[...] = either(up_own0, up_own1) + either(up_got0, up_got1)
    down[...] = either(down_own0, down_own1) + either(down_got0, down_got1)
    outputs[...] = outputs_in[...]
    d_inputs[...] = d_inputs_in[...].astype(F32)

    @pl.when(pl.program_id(0) == 0)
    def _():
        count = router.shape[0]
        router[...] = small[:count]
        gain_moe[...] = small[count : count + 1]
        gain_attn[...] = small[count + 1 : count + 2]
        gain_query[...] = small[count + 2 : count + 3, :dim]
        gain_key[...] = small[count + 2 : count + 3, dim : 2 * dim]


def widen(section, first, second, expert_grads, small, outputs, d_inputs, dim, expert_count):
    (in0, down0, got_in0, got_down0), (in1, down1, got_in1, got_down1) = expert_grads
    width = second.shape[1]
    inner = first.shape[1] - 2 * dim
    units = down0.shape[0]

    def rows(count, columns):
        return pl.BlockSpec((count // STEPS, columns), lambda i, section: (i, 0))

    def either(ahead=0):
        block = (units // STEPS, width)
        return [
            pl.BlockSpec(block, lambda i, section: (jnp.where(section[0] == 0, ahead + i, ahead), 0)),
            pl.BlockSpec(block, lambda i, section: (jnp.where(section[0] == 1, ahead + i, ahead), 0)),
        ]

    def whole(*shape):
        return pl.BlockSpec(shape, lambda i, section: (0,) * len(shape))

    def slab(array):
        return pl.BlockSpec((*array.shape[:-1], width // STEPS), lambda i, section: (0, 0, 0, i))

    def shape(*dims):
        return jax.ShapeDtypeStruct(dims, F32)

    return pl.pallas_call(
        widen_kernel,
        name="widen",
        out_shape=(
            shape(width, inner),
            shape(width, dim),
            shape(width, dim),
            shape(*second.shape),
            shape(units, width),
            shape(units, width),
            shape(units, width),
            shape(expert_count, width),
            shape(1, width),
            shape(1, width),
            shape(1, dim),
            shape(1, dim),
            jax.ShapeDtypeStruct(outputs.shape, BF16),
            shape(*d_inputs.shape),
        ),
        grid_spec=pltpu.PrefetchScalarGridSpec(
            num_scalar_prefetch=1,
            grid=(STEPS,),
            in_specs=[
                rows(width, first.shape[1]),
                rows(second.shape[0], width),
                *either(),
                *either(STEPS),
                *either(),
                *either(STEPS),
                *either(),
                *either(),
                whole(*small.shape),
                slab(outputs),
                slab(d_inputs),
            ],
            out_specs=(
                rows(width, inner),
                rows(width, dim),
                rows(width, dim),
                rows(second.shape[0], width),
                rows(units, width),
                rows(units, width),
                rows(units, width),
                whole(expert_count, width),
                whole(1, width),
                whole(1, width),
                whole(1, dim),
                whole(1, dim),
                slab(outputs),
                slab(d_inputs),
            ),
        ),
        compiler_params=pltpu.CompilerParams(vmem_limit_bytes=VMEM_LIMIT),
    )(
        section[None], first, second, in0, in1, in0, in1, got_in0, got_in1, got_in0, got_in1,
        down0, down1, got_down0, got_down1, small, outputs, d_inputs,
    )


def body(
    block_input,
    cotangent,
    segments,
    routes,
    norm_attn,
    w_query,
    key_matrix,
    value_matrix,
    norm_query,
    norm_key,
    w_output,
    norm_moe,
    w_router,
    w_gate,
    w_up,
    w_down,
):
    section = lax.axis_index("section")
    _, group_rows, width = block_input.shape
    expert_count = w_router.shape[2]
    quarter = group_rows // RING
    dim = norm_query.shape[1]

    dense_own = (w_query[0], key_matrix[0], value_matrix[0], w_output[0])
    expert_own = (jnp.swapaxes(w_gate[0], 1, 2), jnp.swapaxes(w_up[0], 1, 2), w_down[0])
    layer_gains = (w_router[0].T, norm_attn, norm_moe, norm_query, norm_key)
    routes = jnp.swapaxes(routes[0], 1, 2)
    upstream = cotangent.reshape(2, RING, quarter, width)
    rows_in = block_input
    saved, layer_ins, outs, grads_all = [], [], [], []
    for layer in range(2):
        layer_ins.append(rows_in)
        if layer == 0:
            made = forward(layer, rows_in, segments, layer_gains, routes, upstream, dense_own, None, expert_own, None)
            packs, routes_other = made[10:12], made[12]
            dense_other, expert_other = made[13:17], made[17:]
        else:
            made = forward(
                layer, rows_in, segments, packs, (routes, routes_other), upstream, dense_own, dense_other,
                expert_own, expert_other,
            )
        attn_saved, (mid, gates, rows_all, spread, acts, made) = made[:4], made[4:10]
        grads_all.append(spread)
        saved.append((attn_saved, mid, gates, rows_all, acts))
        if layer == 0:
            rows_in = made.reshape(group_rows, width)
            outs.append(made)
    made = made.reshape(RING, RING, RING, quarter, width)

    attn_saved, mid, gates, rows_all, acts = saved[1]
    d_part, *terms, grad_in, grad_down, out_low = experts_back_sum(
        1, rows_all, grads_all, acts, mid, gates, packs, expert_own, expert_other, made, expert_count
    )
    grads_one = (grad_in, grad_down)
    d_all, *_, smalls_one, products_first, products_second, out_high, upstream = attend_back(
        1, layer_ins[1], segments, packs, attn_saved, upstream, d_part, terms[::-1], (mid, made), dense_own, dense_other
    )
    outs += [out_low, out_high]
    attn_saved, mid, gates, rows_all, acts = saved[0]
    partial, *grads_zero, first_own, second_own, got_in_one, got_down_one = experts_back(
        0, rows_all, [d_all], acts, expert_own, expert_other, ((products_first, products_second), grads_one, dense_own)
    )
    d_part, *terms = moe_back(0, partial, mid, gates, packs, expert_count)
    _, *factors_zero, smalls_zero, first_one, second_one, got_in_zero, got_down_zero, outputs, d_inputs, second_sum = attend_back(
        0, layer_ins[0], segments, packs, attn_saved, upstream, d_part, terms[::-1],
        (first_own, second_own, *grads_zero, *outs, upstream), dense_own, dense_other,
    )
    expert_grads = ((*grads_zero, got_in_zero, got_down_zero), (*grads_one, got_in_one, got_down_one))
    first, second, small = finish((*factors_zero[:2], second_sum), (smalls_zero, smalls_one), (first_one, second_one))
    query, key, value, output, gate, up, down, router, gain_moe, gain_attn, gain_query, gain_key, outputs, d_inputs = widen(
        section, first.reshape(width, first.shape[-1]), second.reshape(-1, width), expert_grads, small, outputs, d_inputs,
        dim, expert_count,
    )
    units = w_gate.shape[3]

    def by_expert(array):
        return array.reshape(1, 2, units, width)

    return (
        outputs.reshape(1, 2, group_rows, width),
        d_inputs.reshape(1, 2, group_rows, width),
        gain_attn,
        query[None],
        key[None],
        value[None],
        gain_query,
        gain_key,
        output[None],
        gain_moe,
        router.T[None],
        jnp.swapaxes(by_expert(gate), 2, 3),
        jnp.swapaxes(by_expert(up), 2, 3),
        by_expert(down),
    )


def solution(mesh):
    placed = (
        P(None, "expert", None),
        P(None, "expert", None),
        P(None, "expert", None),
        P("section", None, "expert", None),
        P("section", None),
        P("section", None, "tensor"),
        P("section", None, "tensor"),
        P("section", None, "tensor"),
        P("section", None),
        P("section", None),
        P("section", "tensor", None),
        P("section", None),
        P("section", None, None),
        P("section", "expert", None, "tensor"),
        P("section", "expert", None, "tensor"),
        P("section", "expert", "tensor", None),
    )
    return jax.shard_map(
        body,
        mesh=mesh,
        in_specs=placed,
        out_specs=(
            P("section", None, "expert", None),
            P("section", None, "expert", None),
            P("section", None),
            P("section", None, "tensor"),
            P("section", None, "tensor"),
            P("section", None, "tensor"),
            P("section", None),
            P("section", None),
            P("section", "tensor", None),
            P("section", None),
            P("section", None, None),
            P("section", "expert", None, "tensor"),
            P("section", "expert", None, "tensor"),
            P("section", "expert", "tensor", None),
        ),
        check_vma=False,
    )
```

```python
import functools
import math

import jax
import jax.numpy as jnp
from jax import lax
from jax.experimental import pallas as pl
from jax.experimental.pallas import tpu as pltpu
from jax.sharding import PartitionSpec as P

RING = 4
BF16 = jnp.bfloat16
F32 = jnp.float32


def wrap(value):
    return lax.rem(value + 2 * RING, RING)


class Place:
    def __init__(self):
        self.section = lax.axis_index("section")
        expert = lax.axis_index("expert")
        self.x = lax.axis_index("tensor")
        self.z = lax.div(expert, RING)
        self.y = lax.rem(expert, RING)

    def index(self, axis):
        return getattr(self, axis)

    def device(self, axis, delta):
        at = {"x": self.x, "y": self.y, "z": self.z}
        at[axis] = wrap(at[axis] + delta)
        return (self.section, at["z"] * RING + at["y"], at["x"])

    def peer(self):
        return (1 - self.section, self.z * RING + self.y, self.x)


def greet(devices):
    barrier = pltpu.get_barrier_semaphore()
    for device in devices:
        pl.semaphore_signal(barrier, inc=1, device_id=device, device_id_type=pl.DeviceIdType.MESH)
    return lambda: pl.semaphore_wait(barrier, len(devices))


def meet(devices):
    greet(devices)()


class Copy:
    def __init__(self, sender, copy):
        self.sender, self.copy = sender, copy

    def wait_recv(self):
        self.sender.when(self.copy.wait_recv)


class Sender:
    def __init__(self, send_sems, recv_sems, flag=None):
        self.send_sems, self.recv_sems = send_sems, recv_sems
        self.flag = flag
        self.used = 0
        self.started = []

    def when(self, effect):
        if self.flag is None:
            effect()
        else:
            pl.when(self.flag)(effect)

    def make(self, source, target, device):
        copy = pltpu.make_async_remote_copy(
            src_ref=source,
            dst_ref=target,
            send_sem=self.send_sems.at[self.used],
            recv_sem=self.recv_sems.at[self.used],
            device_id=device,
            device_id_type=pl.DeviceIdType.MESH,
        )
        return copy

    def send(self, source, target, device):
        copy = self.make(source, target, device)
        self.used += 1
        self.when(copy.start)
        self.started.append(copy)
        return Copy(self, copy)

    def send_either(self, flag, source, otherwise, target, device):
        first, second = self.make(source, target, device), self.make(otherwise, target, device)
        self.used += 1
        pl.when(flag)(first.start)
        pl.when(jnp.logical_not(flag))(second.start)
        self.started.append(first)
        return Copy(self, first)

    def hand(self, flag, pairs, device):
        copies = []
        for source, target in pairs:
            copies.append(self.make(source, target, device))
            self.used += 1

        @pl.when(flag)
        def _():
            for copy in copies:
                copy.start()

        def settle():
            @pl.when(flag)
            def _():
                for copy in copies:
                    copy.wait_send()

            @pl.when(jnp.logical_not(flag))
            def _():
                for copy in copies:
                    copy.wait_recv()

        return settle

    def finish(self):
        def effect():
            for copy in self.started:
                copy.wait_send()

        self.when(effect)


def paced(job, points):
    count = iter(range(1000))

    def step():
        if next(count) in points:
            next(job, None)

    return step


def run(job):
    for _ in job:
        pass


def cut(width, count):
    tiles = width // 128
    edges = [tiles * i // count for i in range(count + 1)]
    return [(128 * a, 128 * (b - a)) for a, b in zip(edges[:-1], edges[1:])]


def region(place, order, phase, at, columns):
    spot = {}
    for i, axis in enumerate(order):
        spot[axis] = slice(None) if i < phase else (at if i == phase else place.index(axis))
    return (*[spot[axis] for axis in "zyx" if axis in spot], slice(None), pl.ds(*columns))


SENDS = 3 * (3 + 3 + 6)


def halves(columns):
    left, right = cut(columns[1], 2)
    return (columns[0] + left[0], left[1]), (columns[0] + right[0], right[1])


def thirds(buffer):
    return [(buffer, order, columns) for order, columns in zip(("xyz", "yzx", "zxy"), cut(buffer.shape[-1], 3))]


def gather(place, sender, plans, own=None, settle=None, beside=()):
    last_phase = len(plans[0][1]) - 1
    for phase in range(last_phase + 1):
        waits = []
        for buffer, order, columns in plans:
            axis = order[phase]
            me = place.index(axis)

            def push(delta, piece, buffer=buffer, order=order, axis=axis, me=me):
                here = buffer.at[region(place, order, phase, me, piece)]
                source = own.at[:, pl.ds(*piece)] if own is not None and phase == 0 else here
                return sender.send(source, here, place.device(axis, delta))

            if phase == last_phase:
                left, right = halves(columns)
                onward = (push(1, left), push(-1, right))
                waits += [push(1, right), push(-1, left)]
                waits.append((onward, buffer, order, axis, me, left, right))
            else:
                waits += [push(1, columns), push(-1, columns), push(2, columns)]
        if phase < len(beside):
            beside[phase]()
        yield
        last = []
        for wait in waits:
            if isinstance(wait, tuple):
                (up, down), buffer, order, axis, me, left, right = wait
                up.wait_recv()
                passing = buffer.at[region(place, order, phase, wrap(me - 1), left)]
                last.append(sender.send(passing, passing, place.device(axis, 1)))
                down.wait_recv()
                passing = buffer.at[region(place, order, phase, wrap(me + 1), right)]
                last.append(sender.send(passing, passing, place.device(axis, -1)))
            else:
                last.append(wait)
        if phase == last_phase:
            yield
        for copy in last:
            copy.wait_recv()
        if phase == 0 and settle is not None:
            settle()


def in_turn(jobs):
    jobs = list(jobs)
    while jobs:
        for job in list(jobs):
            try:
                next(job)
            except StopIteration:
                jobs.remove(job)
        if jobs:
            yield


def neighbours(place, axes="xyz"):
    return [place.device(axis, delta) for axis in axes for delta in (1, -1, 2)]


def reduce(place, sender, plans, slots, beside=()):
    last_phase = len(plans[0][1]) - 1
    for turn_number, phase in enumerate(range(last_phase, -1, -1)):
        waits = []
        for (buffer, order, columns), slot in zip(plans, slots):
            axis, slot = order[phase], slot[phase]
            me = place.index(axis)

            def push(delta, at, piece, target, buffer=buffer, order=order, axis=axis, me=me):
                source = buffer.at[region(place, order, phase, wrap(me + at), piece)]
                return sender.send(source, target, place.device(axis, delta))

            if phase == last_phase:
                left, right = halves(columns)
                up, down = push(1, 2, left, slot[0]), push(-1, 2, right, slot[1])
                near = push(1, 1, right, slot[2]), push(-1, -1, left, slot[3])
                waits.append((push, up, down, near))
            else:
                waits.append([push(delta, delta, columns, slot[i]) for i, delta in enumerate((1, -1, 2))])
        if turn_number < len(beside):
            beside[turn_number]()
        yield
        if phase == last_phase:
            later = []
            for (buffer, order, columns), slot, (push, up, down, near) in zip(plans, slots, waits):
                slot = slot[phase]
                me = place.index(order[phase])
                left, right = halves(columns)
                up.wait_recv()
                add_into(sender, buffer, region(place, order, phase, wrap(me + 1), left), slot[0])
                on_up = push(1, 1, left, slot[4])
                down.wait_recv()
                add_into(sender, buffer, region(place, order, phase, wrap(me - 1), right), slot[1])
                on_down = push(-1, -1, right, slot[5])
                later.append((*near, on_up, on_down))
            yield
            for (buffer, order, columns), slot, copies in zip(plans, slots, later):
                slot = slot[phase]
                me = place.index(order[phase])
                left, right = halves(columns)
                for copy in copies:
                    copy.wait_recv()
                add_into(sender, buffer, region(place, order, phase, me, left), slot[3], slot[4])
                add_into(sender, buffer, region(place, order, phase, me, right), slot[2], slot[5])
        else:
            for (buffer, order, columns), slot, copies in zip(plans, slots, waits):
                for copy in copies:
                    copy.wait_recv()
                add_into(sender, buffer, region(place, order, phase, place.index(order[phase]), columns), *slot[phase])


def slot_scratch(plans):
    scratch = []
    for rows, axes, columns in plans:
        left, right = halves(columns)
        for phase in range(axes):
            widths = (left, right, right, left, left, right) if phase == axes - 1 else (columns,) * 3
            scratch += [pltpu.VMEM((RING,) * phase + (rows, width), BF16) for _, width in widths]
    return scratch


def third_slots(rows, columns):
    return slot_scratch([(rows, 3, piece) for piece in cut(columns, 3)])


def sort_slots(refs, plans, axes):
    refs = list(refs)
    counts = [6 if phase == axes - 1 else 3 for phase in range(axes)]
    return [[[refs.pop(0) for _ in range(count)] for count in counts] for _ in range(plans)]


def add_into(sender, buffer, at, *terms):
    *spots, rows, columns = at
    free = [i for i, spot in enumerate(spots) if isinstance(spot, slice)]

    def some(first):
        spot = list(spots)
        picks = [slice(None)] * len(free)
        if first is not None:
            spot[free[0]] = first
            picks[0] = first
        here = (*spot, rows, columns)
        total = buffer[here].astype(F32)
        for term in terms:
            total = total + term[(*picks, slice(None), slice(None))].astype(F32)
        buffer[here] = total.astype(BF16)

    def all_blocks():
        if free:
            for i in range(RING):
                some(i)
        else:
            some(None)

    sender.when(all_blocks)


EPS = 1e-06
THETA = 1000000.0
MASKED = -1e30
GATED = 128
VMEM_LIMIT = 56 << 20


def params(number, vmem=VMEM_LIMIT):
    return pltpu.CompilerParams(collective_id=number, has_side_effects=True, vmem_limit_bytes=vmem)


IN_VMEM = pl.BlockSpec(memory_space=pltpu.VMEM)
ANYWHERE = pl.BlockSpec(memory_space=pl.ANY)


def copy_sems(count):
    return [pltpu.SemaphoreType.DMA((count,)), pltpu.SemaphoreType.DMA((count,))]


def dot_nn(left, right):
    return lax.dot_general(left, right, (((1,), (0,)), ((), ())), preferred_element_type=F32)


def dot_nt(left, right):
    return lax.dot_general(left, right, (((1,), (1,)), ((), ())), preferred_element_type=F32)


def dot_tn(left, right):
    return lax.dot_general(left, right, (((0,), (0,)), ((), ())), preferred_element_type=F32)


def inverse_rms(rows):
    return lax.rsqrt(jnp.mean(rows * rows, axis=-1, keepdims=True) + EPS)


def rms_back(rows, gain, grad):
    scale = inverse_rms(rows)
    unit = rows * scale
    lifted = grad * gain
    return scale * (lifted - unit * jnp.mean(lifted * unit, axis=-1, keepdims=True)), grad * unit


def send_x(place, sender, part, slots):
    return [
        sender.send(part.at[wrap(place.x + delta)], slots.at[i], place.device("x", delta))
        for i, delta in enumerate((1, -1, 2))
    ]


def sum_x(place, copies, part, slots):
    for copy in copies:
        copy.wait_recv()
    total = part[place.x].astype(F32)
    for i in range(3):
        total = total + slots[i].astype(F32)
    return total


def gather_x(place, sender, whole):
    mine = whole.at[place.x]
    copies = [sender.send(mine, mine, place.device("x", delta)) for delta in (1, -1, 2)]
    for copy in copies:
        copy.wait_recv()


def settle_job(place, sender, load, buffer, slots, mid, out):
    if load is not None:
        load.wait()
    yield from reduce(place, sender, thirds(buffer), sort_slots(slots, 3, 3))
    moe_rows = buffer[place.z, place.y, place.x].astype(F32)
    out[place.x] = (mid[...] + moe_rows).astype(BF16)
    mine = out.at[place.x]
    copies = [sender.send(mine, mine, place.device("x", delta)) for delta in (1, -1, 2)]
    yield
    for copy in copies:
        copy.wait_recv()


def part_columns(part, width):
    half = width // 2
    return pl.ds(part * half, half)


def settle_part(part, place, sems, partial, mid, out, scratch):
    sender = Sender(*sems)
    buffer, sem, *slots = scratch
    columns = part_columns(part, mid.shape[1])
    load = pltpu.make_async_copy(partial.at[:, :, :, :, columns], buffer, sem)
    load.start()
    return settle_job(place, sender, load, buffer, slots, mid.at[:, columns], out), sender


def settle_scratch(partial):
    *blocks, rows, width = partial.shape
    half = width // 2
    return [
        *copy_sems(3 + SENDS),
        pltpu.VMEM((*blocks, rows, half), BF16),
        pltpu.SemaphoreType.DMA,
        *third_slots(rows, half),
    ]


SETTLE_SCRATCH = 2 + 2 + 36


def moe_back_rows(layer, place, sender, buffer, mid, gates, pack0, pack1, d_part, gain_term, router_term):
    gain = of_layer(layer, pack0[PACK_ROUTER + 1 : PACK_ROUTER + 2], pack1[PACK_ROUTER + 1 : PACK_ROUTER + 2]).astype(F32)
    router = of_layer(layer, pack0[:PACK_ROUTER], pack1[:PACK_ROUTER])
    width = mid.shape[1]
    sums = buffer[place.z, place.y, place.x].astype(F32)
    weights = gates[...]
    d_gates = sums[:, width:]
    d_logits = (weights * (d_gates - jnp.sum(d_gates * weights, axis=-1, keepdims=True))).astype(BF16)
    d_moe_in = sums[:, :width] + dot_nn(d_logits, router)
    mid_rows = mid[...]
    d_mid, terms = rms_back(mid_rows, gain, d_moe_in)
    d_part[place.x] = d_mid.astype(BF16)
    gather_x(place, sender, d_part)
    gain_term[...] = jnp.sum(terms, axis=0, keepdims=True)
    moe_in = (mid_rows * inverse_rms(mid_rows) * gain).astype(BF16)
    router_term[...] = dot_tn(d_logits, moe_in)[: router_term.shape[0]]


def moe_back_kernel(
    layer, partial, mid, gates, pack0, pack1, d_part, gain_term, router_term, buffer, send, recv, local, *slots
):
    place = Place()
    load = pltpu.make_async_copy(partial, buffer, local)
    load.start()
    meet(neighbours(place))
    sender = Sender(send, recv)
    load.wait()
    run(reduce(place, sender, thirds(buffer), sort_slots(slots, 3, 3)))
    moe_back_rows(layer, place, sender, buffer, mid, gates, pack0, pack1, d_part, gain_term, router_term)
    sender.finish()


def moe_back(layer, partial, mid, gates, packs, expert_count):
    rows, width = mid.shape
    return pl.pallas_call(
        functools.partial(moe_back_kernel, layer),
        name="moe_back",
        out_shape=(
            jax.ShapeDtypeStruct((RING, rows, width), BF16),
            jax.ShapeDtypeStruct((1, width), F32),
            jax.ShapeDtypeStruct((expert_count, width), F32),
        ),
        in_specs=[ANYWHERE] + [IN_VMEM] * 4,
        out_specs=(IN_VMEM,) * 3,
        scratch_shapes=[
            pltpu.VMEM(partial.shape, BF16),
            *copy_sems(3 + SENDS),
            pltpu.SemaphoreType.DMA,
            *third_slots(rows, width + GATED),
        ],
        compiler_params=params(5 + layer),
    )(partial, mid, gates, *packs)


TILE = 256


def load_weights(layer, own, other, targets, sems):
    gate, up, down = targets
    half = gate.shape[0] // 2
    section = lax.axis_index("section")

    def pairs(source):
        return [
            (source[0].at[0], gate.at[pl.ds(0, half)]),
            (source[0].at[1], gate.at[pl.ds(half, half)]),
            (source[1].at[0], up.at[pl.ds(0, half)]),
            (source[1].at[1], up.at[pl.ds(half, half)]),
            (source[2].at[0], down.at[pl.ds(0, half)]),
            (source[2].at[1], down.at[pl.ds(half, half)]),
        ]

    @pl.when(section == layer)
    def _():
        for i, (source, target) in enumerate(pairs(own)):
            pltpu.make_async_copy(source, target, sems.at[i]).start()

    @pl.when(section != layer)
    def _():
        for i, (source, target) in enumerate(pairs(other)):
            pltpu.make_async_copy(source, target, sems.at[i]).start()

    return [pltpu.make_async_copy(source, target, sems.at[i]) for i, (source, target) in enumerate(pairs(own))]


def gate_columns(table, half):
    first = 2 * lax.axis_index("expert")
    lanes = lax.broadcasted_iota(jnp.int32, table.shape, 1)
    table = table.astype(F32)
    one = jnp.sum(jnp.where(lanes == first, table, 0.0), axis=1, keepdims=True)
    two = jnp.sum(jnp.where(lanes == first + 1, table, 0.0), axis=1, keepdims=True)
    units = lax.broadcasted_iota(jnp.int32, (table.shape[0], 2 * half), 1)
    return jnp.where(units < half, one, two)


class Stream:
    def __init__(self, hbm, slots, sems):
        self.hbm, self.slots, self.sems = hbm, slots, sems

    def copies(self, i, out):
        tile = self.slots.shape[1]
        rows = pl.ds(i * tile, tile)
        made = []
        at = 0
        for n, ref in enumerate(self.hbm):
            far, near = ref.at[rows], self.slots.at[i % 2, :, pl.ds(at, ref.shape[1])]
            at += ref.shape[1]
            pair = (near, far) if out else (far, near)
            made.append(pltpu.make_async_copy(*pair, self.sems.at[i % 2, n]))
        return made

    def fetch(self, i):
        for copy in self.copies(i, False):
            copy.start()

    def fetched(self, i):
        for copy in self.copies(i, False):
            copy.wait()
        return self.slots.at[i % 2]

    def store(self, i):
        for copy in self.copies(i, True):
            copy.start()

    def stored(self, i):
        for copy in self.copies(i, True):
            copy.wait()


def stream_scratch(widths, pieces=1, tile=TILE):
    scratch = []
    for width in widths:
        scratch += [pltpu.VMEM((2, tile, width), BF16), pltpu.SemaphoreType.DMA((2, pieces))]
    return scratch


BLOCKS = 8
SETTLE_POINTS = (3, 6)
SUM_POINTS = (4, 9)


def expert_back_kernel(layer, pieces, rows, *refs):
    refs = list(refs)

    def take(count):
        taken = refs[:count]
        del refs[:count]
        return taken

    grads, (acts,), own, other = take(pieces), take(1), take(3), take(3)
    extra = take(4)
    out, grad_in, grad_down = take(3)
    made = take(4)
    gate, up, down, sum_in, sum_down, sems = take(6)
    row_slots, row_sems, grad_slots, grad_sems, act_slots, act_sems, out_slots, out_sems, send, recv, local = take(11)
    place = Place()
    peer = place.peer()
    width = grad_in.shape[1]
    units = gate.shape[0]
    tiles = rows.shape[0] // TILE
    met = greet([peer, *neighbours(place, "yz")])
    upper = place.section == 1
    sender = Sender(send, recv, upper)
    first_own, second_own, got_in, got_down = made
    first, second, *slots = refs[:-2]
    loads = [pltpu.make_async_copy(*pair, local.at[i]) for i, pair in enumerate(zip(extra[:2], (first, second)))]
    for copy in loads:
        sender.when(copy.start)
    handing = Sender(refs[-2], refs[-1])

    def side():
        met()
        state["handed"] = handing.hand(place.section == 0, [(extra[2], got_in), (extra[3], got_down)], peer)
        for copy in loads:
            sender.when(copy.wait)
        yield from in_turn(gradient_reduces(place, sender, first, second, slots))
        first_own[...] = first[place.z, place.y]
        second_own[...] = second[place.z, place.y]

    state = {}
    job = side()

    weights = load_weights(layer, own, other, (gate, up, down), sems)
    ins, ups = Stream([rows], row_slots, row_sems), Stream(grads, grad_slots, grad_sems)
    kept, outs = Stream([acts], act_slots, act_sems), Stream([out], out_slots, out_sems)
    for stream in (ins, ups, kept):
        stream.fetch(0)
    next(job)
    step = paced(job, SUM_POINTS)
    first_expert = 2 * lax.axis_index("expert")
    for i in range(tiles):
        for stream in (ins, ups, kept):
            if i + 1 < tiles:
                stream.fetch(i + 1)
        tile, grad, act = ins.fetched(i), ups.fetched(i)[...], kept.fetched(i)
        if i == 0:
            for copy in weights:
                copy.wait()
        gates = gate_columns(tile[:, width:], units // 2)
        back = dot_nt(grad, down[...])
        gate_act = act[:, :units].astype(F32)
        up_act = act[:, units:].astype(F32)
        sigmoid = 1.0 / (1.0 + jnp.exp(-gate_act))
        silu = gate_act * sigmoid
        hidden = silu * up_act
        products = hidden * back
        in_one = lax.broadcasted_iota(jnp.int32, products.shape, 1) < units // 2
        one = jnp.sum(jnp.where(in_one, products, 0.0), axis=1, keepdims=True)
        two = jnp.sum(jnp.where(in_one, 0.0, products), axis=1, keepdims=True)
        lanes = lax.broadcasted_iota(jnp.int32, (products.shape[0], GATED), 1)
        d_gates = jnp.where(lanes == first_expert, one, jnp.where(lanes == first_expert + 1, two, 0.0))
        d_hidden = back * gates
        d_gate = (d_hidden * up_act * sigmoid * (1.0 + gate_act * (1.0 - sigmoid))).astype(BF16)
        d_up = (d_hidden * silu).astype(BF16)
        if i >= 2:
            outs.stored(i - 2)
        out_slots[i % 2, :, :width] = (dot_nn(d_gate, gate[...]) + dot_nn(d_up, up[...])).astype(BF16)
        out_slots[i % 2, :, width:] = d_gates.astype(BF16)
        outs.store(i)
        step()
        moe_in = tile[:, :width]
        terms = (
            (sum_in, slice(0, units), dot_tn(d_gate, moe_in)),
            (sum_in, slice(units, 2 * units), dot_tn(d_up, moe_in)),
            (sum_down, slice(0, units), dot_tn((hidden * gates).astype(BF16), grad)),
        )
        for total, at, term in terms:
            if i == 0:
                total[at] = term
            elif i < tiles - 1:
                total[at] += term
            else:
                low = grad_in if total is sum_in else grad_down
                low[at] = (total[at] + term).astype(BF16)
        step()
    run(job)
    for i in (tiles - 2, tiles - 1):
        outs.stored(i)
    sender.finish()
    state["handed"]()


def expert_back_sum_kernel(layer, pieces, rows, *refs):
    refs = list(refs)

    def take(count):
        taken = refs[:count]
        del refs[:count]
        return taken

    grads, (acts, mid, gates, pack0, pack1), own, other = take(pieces), take(5), take(3), take(3)
    above = take(1)[0]
    d_part, gain_term, router_term, grad_in, grad_down, *settled = take(6)
    gate, up, down, sems, row_all, grad_all, act_all, hiddens, load_sems = take(9)
    settle_refs = [take(SETTLE_SCRATCH) for _ in settled]
    send, recv, buffer, *slots = refs
    place = Place()
    met = greet(neighbours(place))
    sender = Sender(send, recv)
    parts = [
        settle_part(part, place, held[:2], above, mid, out, held[2:])
        for part, (out, held) in enumerate(zip(settled, settle_refs))
    ]
    settling = in_turn([job for job, _ in parts])
    weights = load_weights(layer, own, other, (gate, up, down), sems)
    quarter = buffer.shape[3]
    tile_rows = BLOCKS * quarter
    tiles = rows.shape[0] // tile_rows
    width = mid.shape[1]
    units = gate.shape[0]

    def loads(i):
        at = pl.ds(i * tile_rows, tile_rows)
        pairs = [(rows.at[at], row_all.at[at]), (acts.at[at], act_all.at[at])]
        start = 0
        for ref in grads:
            pairs.append((ref.at[at], grad_all.at[at, pl.ds(start, ref.shape[1])]))
            start += ref.shape[1]
        return [pltpu.make_async_copy(*pair, load_sems.at[i, n]) for n, pair in enumerate(pairs)]

    for i in range(tiles):
        for load in loads(i):
            load.start()
    for copy in weights:
        copy.wait()
    met()
    next(settling)
    first_expert = 2 * lax.axis_index("expert")
    for i in range(tiles):
        if i in SETTLE_POINTS:
            next(settling)
        for load in loads(i):
            load.wait()
        at = slice(i * tile_rows, (i + 1) * tile_rows)
        weight = gate_columns(row_all[at, width:], units // 2)
        back = dot_nt(grad_all[at], down[...])
        gate_act = act_all[at, :units].astype(F32)
        up_act = act_all[at, units:].astype(F32)
        sigmoid = 1.0 / (1.0 + jnp.exp(-gate_act))
        silu = gate_act * sigmoid
        hidden = silu * up_act
        products = hidden * back
        in_one = lax.broadcasted_iota(jnp.int32, products.shape, 1) < units // 2
        one = jnp.sum(jnp.where(in_one, products, 0.0), axis=1, keepdims=True)
        two = jnp.sum(jnp.where(in_one, 0.0, products), axis=1, keepdims=True)
        lanes = lax.broadcasted_iota(jnp.int32, (products.shape[0], GATED), 1)
        d_gates = jnp.where(lanes == first_expert, one, jnp.where(lanes == first_expert + 1, two, 0.0))
        d_hidden = back * weight
        d_gate = (d_hidden * up_act * sigmoid * (1.0 + gate_act * (1.0 - sigmoid))).astype(BF16)
        d_up = (d_hidden * silu).astype(BF16)
        act_all[at, :units] = d_gate
        act_all[at, units:] = d_up
        hiddens[at] = (hidden * weight).astype(BF16)
        d_rows = dot_nn(d_gate, gate[...]) + dot_nn(d_up, up[...])
        for n in range(BLOCKS):
            block = i * BLOCKS + n
            here = (block // (RING * RING), block // RING % RING, block % RING)
            piece = slice(n * quarter, (n + 1) * quarter)
            buffer[(*here, slice(None), slice(0, width))] = d_rows[piece].astype(BF16)
            buffer[(*here, slice(None), slice(width, None))] = d_gates[piece].astype(BF16)

    def products_job():
        step = 2 * LANES
        for target, source, inputs in ((grad_in, act_all, row_all), (grad_down, hiddens, grad_all)):
            for start in range(0, target.shape[0], step):
                size = min(step, target.shape[0] - start)
                term = dot_tn(source[:, start : start + size], inputs[:, :width])
                target[start : start + size] = term.astype(BF16)
                yield

    summing = reduce(place, sender, thirds(buffer), sort_slots(slots, 3, 3))
    making = products_job()
    for count in (2, 2, 1):
        next(summing)
        next(settling, None)
        for _ in range(count):
            next(making, None)
    run(in_turn([summing, settling]))
    run(making)
    moe_back_rows(layer, place, sender, buffer, mid, gates, pack0, pack1, d_part, gain_term, router_term)
    sender.finish()
    for _, settler in parts:
        settler.finish()


def experts_back_sum(layer, rows_all, grads_all, acts, mid, gates, packs, own, other, above, expert_count):
    quarter = rows_all.shape[3]
    count = RING**3 * quarter
    width = rows_all.shape[4] - GATED
    units = 2 * own[0].shape[1]
    grads = [g.reshape(count, g.shape[-1]) for g in grads_all]
    tiles = count // (BLOCKS * quarter)
    return pl.pallas_call(
        functools.partial(expert_back_sum_kernel, layer, len(grads)),
        name="experts_back_sum",
        out_shape=(
            jax.ShapeDtypeStruct((RING, quarter, width), BF16),
            jax.ShapeDtypeStruct((1, width), F32),
            jax.ShapeDtypeStruct((expert_count, width), F32),
            jax.ShapeDtypeStruct((2 * units, width), BF16),
            jax.ShapeDtypeStruct((units, width), BF16),
            jax.ShapeDtypeStruct((RING, quarter, width // 2), BF16),
        ),
        in_specs=[ANYWHERE] * (2 + len(grads)) + [IN_VMEM] * 4 + [ANYWHERE] * 7,
        out_specs=(IN_VMEM,) * 6,
        scratch_shapes=[pltpu.VMEM((units, width), BF16)] * 3
        + [
            pltpu.SemaphoreType.DMA((6,)),
            pltpu.VMEM((count, width + GATED), BF16),
            pltpu.VMEM((count, width), BF16),
            pltpu.VMEM((count, 2 * units), BF16),
            pltpu.VMEM((count, units), BF16),
            pltpu.SemaphoreType.DMA((tiles, 2 + len(grads))),
            *settle_scratch(above),
            *copy_sems(3 + SENDS),
            pltpu.VMEM(rows_all.shape, BF16),
            *third_slots(quarter, width + GATED),
        ],
        compiler_params=params(14 + layer),
    )(rows_all.reshape(count, width + GATED), *grads, acts, mid, gates, *packs, *own, *other, above)


def experts_back(layer, rows_all, grads_all, acts, own, other, extra):
    quarter = rows_all.shape[3]
    count = RING**3 * quarter
    width = rows_all.shape[4] - GATED
    units = 2 * own[0].shape[1]
    grads = [g.reshape(count, g.shape[-1]) for g in grads_all]
    products, grads_one, dense = extra
    first, second = gradient_shapes(dense)
    extra = (*products, *grads_one)
    extra_specs, made_specs = [ANYWHERE] * 4, (IN_VMEM, IN_VMEM, ANYWHERE, ANYWHERE)
    made = (
        jax.ShapeDtypeStruct(first[2:], BF16),
        jax.ShapeDtypeStruct(second[2:], BF16),
        jax.ShapeDtypeStruct(grads_one[0].shape, BF16),
        jax.ShapeDtypeStruct(grads_one[1].shape, BF16),
    )
    scratch = [
        *copy_sems(GRADIENT_SENDS),
        pltpu.SemaphoreType.DMA((2,)),
        pltpu.VMEM(first, BF16),
        pltpu.VMEM(second, BF16),
        *gradient_slots(first, second),
        *copy_sems(2),
    ]
    out, *rest = pl.pallas_call(
        functools.partial(expert_back_kernel, layer, len(grads)),
        name="experts_back",
        out_shape=(
            jax.ShapeDtypeStruct((count, width + GATED), BF16),
            jax.ShapeDtypeStruct((2 * units, width), BF16),
            jax.ShapeDtypeStruct((units, width), BF16),
            *made,
        ),
        in_specs=[ANYWHERE] * (1 + len(grads) + 1 + 6) + extra_specs,
        out_specs=(ANYWHERE, IN_VMEM, IN_VMEM, *made_specs),
        scratch_shapes=[pltpu.VMEM((units, width), BF16)] * 3
        + [pltpu.VMEM((2 * units, width), F32), pltpu.VMEM((units, width), F32), pltpu.SemaphoreType.DMA((6,))]
        + stream_scratch((width + GATED,))
        + stream_scratch((width,), len(grads))
        + stream_scratch((2 * units, width + GATED))
        + scratch,
        compiler_params=params(12 + layer),
    )(rows_all.reshape(count, width + GATED), *grads, acts, *own, *other, *extra)
    return (out.reshape(*rows_all.shape), *rest)


def pull(layer, own, other, targets, sems):
    section = lax.axis_index("section")

    @pl.when(section == layer)
    def _():
        for i, (source, target) in enumerate(zip(own, targets)):
            pltpu.make_async_copy(source, target, sems.at[i]).start()

    @pl.when(section != layer)
    def _():
        for i, (source, target) in enumerate(zip(other, targets)):
            pltpu.make_async_copy(source, target, sems.at[i]).start()

    return [pltpu.make_async_copy(source, target, sems.at[i]) for i, (source, target) in enumerate(zip(own, targets))]


def of_layer(layer, own, other):
    return jnp.where(lax.axis_index("section") == layer, own, other)


def tables(seg_row, dim):
    rows = seg_row.shape[1]
    at_row = lax.broadcasted_iota(jnp.int32, (rows, rows), 0)
    at_column = lax.broadcasted_iota(jnp.int32, (rows, rows), 1)
    seg_row = seg_row.astype(F32)
    seg_column = jnp.sum(jnp.where(at_row == at_column, seg_row, 0.0), axis=1, keepdims=True)
    earlier = jnp.sum((seg_row < seg_column).astype(F32), axis=1, keepdims=True)
    position = lax.broadcasted_iota(jnp.int32, (rows, dim), 0).astype(F32) - earlier
    lane = lax.broadcasted_iota(jnp.int32, (rows, dim), 1)
    half = dim // 2
    place = jnp.where(lane < half, lane, lane - half).astype(F32)
    angle = position * jnp.exp(place * (-math.log(THETA) / half))
    sine = jnp.sin(angle)
    return jnp.cos(angle), jnp.where(lane < half, -sine, sine), (seg_row == seg_column) & (at_column <= at_row)


def turn(rows, cosine, sine):
    return rows * cosine + pltpu.roll(rows, rows.shape[1] // 2, 1) * sine


def turn_back(grad, cosine, sine):
    return grad * cosine + pltpu.roll(grad * sine, grad.shape[1] // 2, 1)


PACK_ROUTER = 128
PACK_ROWS = 144
HEADS_STEP = 2
SETTLE_BESIDE = (0, 3)
WIDEN_POINTS = (0, 1, 3)


def fill_pack(pack, router, norm_attn, norm_moe, norm_query, norm_key):
    count, width = router.shape
    pack[:count] = router[...]
    pack[count:PACK_ROUTER] = jnp.zeros((PACK_ROUTER - count, width), BF16)
    heads = [norm_query[...].astype(F32), norm_key[...].astype(F32)]
    rest = width - sum(h.shape[1] for h in heads)
    heads = jnp.concatenate([*heads, jnp.zeros((1, rest), F32)], axis=1)
    row = lax.broadcasted_iota(jnp.int32, (PACK_ROWS - PACK_ROUTER, width), 0)
    gains = jnp.where(row == 2, heads, 0.0)
    gains = jnp.where(row == 1, norm_moe[...].astype(F32), gains)
    pack[PACK_ROUTER:] = jnp.where(row == 0, norm_attn[...].astype(F32), gains).astype(BF16)


def forward_kernel(
    layer, rows, segments, routes0, upstream, *refs
):
    refs = list(refs)

    def take(count):
        taken = refs[:count]
        del refs[:count]
        return taken

    if layer:
        (pack0, pack1, routes1), dense_own, dense_other, expert_own, expert_other = take(3), take(4), take(4), take(3), take(3)
        attended, query_raw, key_raw, value_low, mid, gates, rows_all, spread, acts, out = take(10)
    else:
        (router_own, norm_attn, norm_moe, norm_query, norm_key), dense_own, expert_own = take(5), take(4), take(3)
        attended, query_raw, key_raw, value_low, mid, gates, rows_all, spread, acts, out = take(10)
        (pack0, pack1, routes1), dense_other, expert_other = take(3), take(4), take(3)
    wq, wk, wv, wo, total, part, own, slots, sems, send, recv, local = take(12)
    share_send, share_recv, gate, up, down, expert_sems, all_in, act_slots, act_sems, named_all = take(10)
    place = Place()
    section = place.section
    if not layer:
        rows = rows.at[section]
    part_width = rows.shape[1] // 2
    shared = upstream.at[section, :, :, pl.ds(layer * part_width, part_width)]
    peer = place.peer()
    met = greet(neighbours(place) if layer else [peer, *neighbours(place)])
    keep_shared = pltpu.make_async_copy(shared.at[place.x], spread.at[place.z, place.y, place.x], local.at[1])
    keep_shared.start()
    sharer = Sender(share_send, share_recv)
    sharing = gather(place, sharer, thirds(spread), shared.at[place.x], keep_shared.wait)
    dim = wk.shape[1]
    heads = wq.shape[1] // dim
    step = HEADS_STEP * dim
    steps = heads // HEADS_STEP

    def pieces(q, k, v, o):
        made = [k, v]
        for i in range(steps):
            made += [q.at[:, pl.ds(i * step, step)], o.at[pl.ds(i * step, step)]]
        return made

    targets = pieces(wq, wk, wv, wo)
    ours, theirs = pieces(*dense_own), pieces(*dense_other)
    if layer:
        loads = pull(layer, ours, theirs, targets, sems)

        def arrive(i):
            loads[i].wait()

        fetching = load_weights(layer, expert_own, expert_other, (gate, up, down), expert_sems)
        met()
    else:
        lower = section == 0
        loads = [pltpu.make_async_copy(*pair, sems.at[i]) for i, pair in enumerate(zip(ours, targets))]
        late = [pltpu.make_async_copy(*pair, sems.at[i]) for i, pair in enumerate(zip(theirs, targets))]

        @pl.when(lower)
        def _():
            for load in loads:
                load.start()

        fill_pack(pack0, router_own, norm_attn, norm_moe, norm_query, norm_key)
        met()
        pusher = Sender(*take(2))
        first = [pusher.send(pack0, pack1, peer), pusher.send(routes0.at[1 - section], routes1, peer)]
        pushed = [pusher.send(*pair, peer) for pair in zip(ours, theirs)]
        for copy in first:
            copy.wait_recv()

        def prefetch(i):
            @pl.when(jnp.logical_not(lower))
            def _():
                pushed[i].wait_recv()
                late[i].start()

        def arrive(i):
            if i + 1 < len(pushed):
                prefetch(i + 1)
            loads[i].wait()

        prefetch(0)
    next(sharing)
    resid = rows[...].astype(F32)
    gain = of_layer(layer, pack0[PACK_ROUTER : PACK_ROUTER + 1], pack1[PACK_ROUTER : PACK_ROUTER + 1]).astype(F32)
    gains = of_layer(layer, pack0[PACK_ROUTER + 2 : PACK_ROUTER + 3], pack1[PACK_ROUTER + 2 : PACK_ROUTER + 3]).astype(F32)
    gain_query, gain_key = gains[:, :dim], gains[:, dim : 2 * dim]
    cosine, sine, allowed = tables(segments[place.section], dim)
    normed = (resid * inverse_rms(resid) * gain).astype(BF16)
    arrive(0)
    raw = dot_nn(normed, wk[...])
    key_raw[...] = raw
    key = turn(raw * inverse_rms(raw) * gain_key, cosine, sine).astype(BF16)
    arrive(1)
    value = dot_nn(normed, wv[...]).astype(BF16)
    value_low[...] = value
    for i in range(steps):
        if i == steps // 2:
            next(sharing)
        arrive(2 + 2 * i)
        raws = dot_nn(normed, wq[:, i * step : (i + 1) * step])
        query_raw[:, i * step : (i + 1) * step] = raws
        for h in range(HEADS_STEP):
            raw = raws[:, h * dim : (h + 1) * dim]
            query = turn(raw * inverse_rms(raw) * gain_query, cosine, sine).astype(BF16)
            scores = jnp.where(allowed, dot_nt(query, key) * (1.0 / math.sqrt(dim)), MASKED)
            raised = jnp.exp(scores - jnp.max(scores, axis=1, keepdims=True))
            probs = (raised / jnp.sum(raised, axis=1, keepdims=True)).astype(BF16)
            at = i * step + h * dim
            attended[:, at : at + dim] = dot_nn(probs, value).astype(BF16)
        arrive(3 + 2 * i)
        piece = dot_nn(attended[:, i * step : (i + 1) * step], wo[i * step : (i + 1) * step])
        if i == 0:
            total[...] = piece
        else:
            total[...] += piece
    quarter = part.shape[1]
    for i in range(part.shape[0]):
        part[i] = total[i * quarter : (i + 1) * quarter].astype(BF16)
        total[i * quarter : (i + 1) * quarter] = resid[i * quarter : (i + 1) * quarter]
    sender = Sender(send, recv)
    copies = send_x(place, sender, part, slots)
    if not layer:
        pushed_experts = [pusher.send(*pair, peer) for pair in zip(expert_own, expert_other)]
    chosen = of_layer(layer, routes0[section], routes1[...])
    number = lax.broadcasted_iota(jnp.int32, (GATED, chosen.shape[1]), 0)
    named = chosen[0:1] == number
    for i in range(1, chosen.shape[0]):
        named = named | (chosen[i : i + 1] == number)
    across = lax.broadcasted_iota(jnp.int32, (GATED, GATED), 0) == lax.broadcasted_iota(jnp.int32, (GATED, GATED), 1)
    named_all[...] = dot_tn(named.astype(F32).astype(BF16), across.astype(F32).astype(BF16))
    named = named_all[pl.ds(pl.multiple_of(place.x * quarter, 8), quarter)] > 0.5
    gain = of_layer(layer, pack0[PACK_ROUTER + 1 : PACK_ROUTER + 2], pack1[PACK_ROUTER + 1 : PACK_ROUTER + 2])
    router = of_layer(layer, pack0[:PACK_ROUTER], pack1[:PACK_ROUTER])
    mine = total[pl.ds(pl.multiple_of(place.x * quarter, 8), quarter)]
    mid_rows = mine + sum_x(place, copies, part, slots)
    mid[...] = mid_rows
    moe_in = (mid_rows * inverse_rms(mid_rows) * gain.astype(F32)).astype(BF16)
    logits = jnp.where(named, dot_nt(moe_in, router), MASKED)
    raised = jnp.where(named, jnp.exp(logits - jnp.max(logits, axis=-1, keepdims=True)), 0.0)
    weights = raised / jnp.sum(raised, axis=-1, keepdims=True)
    gates[...] = weights
    own[:, : moe_in.shape[1]] = moe_in
    own[:, moe_in.shape[1] :] = weights.astype(BF16)
    keep = pltpu.make_async_copy(own, all_in.at[place.z, place.y, place.x], local.at[0])
    keep.start()
    gathering = gather(place, sender, thirds(all_in), own, keep.wait)
    for _ in range(3):
        next(gathering)
    if not layer:
        for copy in pushed_experts:
            copy.wait_recv()
        fetching = load_weights(layer, expert_own, expert_other, (gate, up, down), expert_sems)
    run(gathering)
    store = pltpu.make_async_copy(all_in, rows_all, local.at[2])
    store.start()
    next(sharing)
    for copy in fetching:
        copy.wait()
    kept = Stream([acts], act_slots, act_sems)
    if layer:
        out_slots, out_sems = refs
        outs = Stream([out], out_slots, out_sems)
    else:
        settle_send, settle_recv, buffer, *settle_slots = refs
    width = gate.shape[1]
    units = gate.shape[0]
    tile_rows = BLOCKS * quarter
    tiles = acts.shape[0] // tile_rows
    half = BLOCKS // RING
    for i in range(tiles):
        at = i * half
        tile = all_in[at // RING, at % RING : at % RING + half].reshape(tile_rows, width + GATED)
        moe_in = tile[:, :width]
        gate_act = dot_nt(moe_in, gate[...])
        up_act = dot_nt(moe_in, up[...])
        hidden = gate_act / (1.0 + jnp.exp(-gate_act)) * up_act
        hidden = hidden * gate_columns(tile[:, width:], units // 2)
        if i >= 2:
            kept.stored(i - 2)
        act_slots[i % 2, :, :units] = gate_act.astype(BF16)
        act_slots[i % 2, :, units:] = up_act.astype(BF16)
        kept.store(i)
        made = dot_nn(hidden.astype(BF16), down[...])
        if layer:
            if i >= 2:
                outs.stored(i - 2)
            out_slots[i % 2] = made.astype(BF16)
            outs.store(i)
        else:
            for n in range(BLOCKS):
                block = i * BLOCKS + n
                here = (block // (RING * RING), block // RING % RING, block % RING)
                buffer[here] = made[n * quarter : (n + 1) * quarter].astype(BF16)
        if i == SHARE_TILE:
            next(sharing)
    if layer:
        run(sharing)
        for i in (tiles - 2, tiles - 1):
            outs.stored(i)
    else:
        settler = Sender(settle_send, settle_recv)
        run(in_turn([settle_job(place, settler, None, buffer, settle_slots, mid, out), sharing]))
        settler.finish()

        @pl.when(lower)
        def _():
            for copy in pushed:
                copy.wait_recv()

        pusher.finish()
    for i in (tiles - 2, tiles - 1):
        kept.stored(i)
    store.wait()
    sharer.finish()
    sender.finish()


def weight_scratch(dense):
    return [pltpu.VMEM(w.shape, BF16) for w in dense]


SHARE_TILE = 4


def forward(layer, rows, segments, packs, routes, upstream, own, other, expert_own, expert_other):
    count, width = rows.shape[-2:]
    quarter = count // RING
    dim, inner = own[1].shape[1], own[0].shape[1]
    pieces = 2 + 2 * (inner // dim // HEADS_STEP)
    units = 2 * expert_own[0].shape[1]
    everyone = (RING, RING, RING, quarter)
    total = RING**3 * quarter
    tile = BLOCKS * quarter

    def like(array):
        return jax.ShapeDtypeStruct(array.shape, array.dtype)

    if layer:
        out, out_spec = (total, width), ANYWHERE
        swapped, swapped_specs, push = (), (), ()
        tail = stream_scratch((width,), tile=tile)
        inputs = (rows, segments, routes[0], upstream, *packs, routes[1], *own, *other, *expert_own, *expert_other)
    else:
        out, out_spec = (RING, quarter, width), IN_VMEM
        pack = jax.ShapeDtypeStruct((PACK_ROWS, width), BF16)
        swapped = (pack, pack, jax.ShapeDtypeStruct(routes.shape[1:], routes.dtype), *map(like, own), *map(like, expert_own))
        swapped_specs = (IN_VMEM,) * 3 + (ANYWHERE,) * 7
        push = copy_sems(2 + pieces + 3)
        tail = [*copy_sems(3 + SENDS), pltpu.VMEM((*everyone, width), BF16), *third_slots(quarter, width)]
        inputs = (rows, segments, routes, upstream, *packs, *own, *expert_own)
    return pl.pallas_call(
        functools.partial(forward_kernel, layer),
        name="forward",
        out_shape=(
            jax.ShapeDtypeStruct((count, inner), BF16),
            jax.ShapeDtypeStruct((count, inner), F32),
            jax.ShapeDtypeStruct((count, dim), F32),
            jax.ShapeDtypeStruct((count, dim), BF16),
            jax.ShapeDtypeStruct((quarter, width), F32),
            jax.ShapeDtypeStruct((quarter, GATED), F32),
            jax.ShapeDtypeStruct((*everyone, width + GATED), BF16),
            jax.ShapeDtypeStruct((*everyone, width // 2), BF16),
            jax.ShapeDtypeStruct((total, 2 * units), BF16),
            jax.ShapeDtypeStruct(out, BF16),
            *swapped,
        ),
        in_specs=[IN_VMEM] * (7 if layer else 9) + [ANYWHERE] * (14 if layer else 7),
        out_specs=(IN_VMEM,) * 6 + (ANYWHERE,) * 3 + (out_spec,) + swapped_specs,
        scratch_shapes=[
            *weight_scratch(own),
            pltpu.VMEM((count, width), F32),
            pltpu.VMEM((RING, quarter, width), BF16),
            pltpu.VMEM((quarter, width + GATED), BF16),
            pltpu.VMEM((3, quarter, width), BF16),
            pltpu.SemaphoreType.DMA((pieces,)),
            *copy_sems(3 + SENDS),
            pltpu.SemaphoreType.DMA((3,)),
            *copy_sems(SENDS),
            *[pltpu.VMEM((units, width), BF16)] * 3,
            pltpu.SemaphoreType.DMA((6,)),
            pltpu.VMEM((*everyone, width + GATED), BF16),
            *stream_scratch((2 * units,), tile=tile),
            pltpu.VMEM((count, GATED), F32),
            *push,
            *tail,
        ],
        compiler_params=params(1 + layer),
    )(*inputs)


SMALL = 48


def gradient_shapes(dense):
    width, inner = dense[0].shape
    proj = inner + 2 * dense[1].shape[1]
    blocks = RING * RING
    return (RING, RING, width // blocks, proj), (RING, RING, inner // blocks, width)


def gradient_plans(array):
    one, two = cut(array.shape[-1], 2)
    return [(array, "yz", one), (array, "zy", two)]


GRADIENT_SENDS = 2 * 18


def gradient_slots(first, second):
    scratch = []
    for shape in (first, second):
        one, two = cut(shape[3], 2)
        scratch += slot_scratch([(shape[2], 2, one), (shape[2], 2, two)])
    return scratch


def gradient_reduces(place, sender, first, second, slots, beside=()):
    return [
        reduce(place, sender, gradient_plans(first), sort_slots(slots[:18], 2, 2)),
        reduce(place, sender, gradient_plans(second), sort_slots(slots[18:], 2, 2), beside),
    ]


def gradient_gathers(place, sender, first, second, beside=()):
    return [
        gather(place, sender, gradient_plans(first)),
        gather(place, sender, gradient_plans(second), None, None, beside),
    ]


LANES = 128


def output_products(heads, mids, second):
    def blocks(i, _):
        pair = dot_tn(heads[:, pl.ds(pl.multiple_of(i * LANES, LANES), LANES)], mids[...]).astype(BF16)
        at = 2 * i
        second[lax.div(at, RING), lax.rem(at, RING)] = pair[: LANES // 2]
        second[lax.div(at, RING), lax.rem(at, RING) + 1] = pair[LANES // 2 :]
        return 0

    lax.fori_loop(0, heads.shape[1] // LANES, blocks, 0)


def input_products(normed, proj, first):
    def blocks(i, _):
        block = dot_tn(normed[:, pl.ds(pl.multiple_of(i * LANES, LANES), LANES)], proj[...])
        first[lax.div(i, RING), lax.rem(i, RING)] = block.astype(BF16)
        return 0

    lax.fori_loop(0, normed.shape[1] // LANES, blocks, 0)


def attend_back_kernel(
    layer, rows, segments, pack0, pack1, attended, query_raw, key_raw, value_low, upstream, d_part,
    router_term, moe_gain_term, *refs
):
    last = layer == 0
    refs = list(refs)
    extra = [refs.pop(0) for _ in range(8 if last else 2)]
    q0, k0, v0, o0, q1, k1, v1, o1, d_input, normed_both, d_proj, heads_both, d_mid_low, smalls = refs[:14]
    refs = refs[14:]
    wide = [refs.pop(0) for _ in range(7 if last else 4)]
    wq, wk, wv, wo, total, d_mid, d_heads, part, own, slots, sems, send, recv, local, *side = refs
    place = Place()
    peer = place.peer()
    met = greet([peer, *neighbours(place)])
    if last:
        rows = rows.at[place.section]
    else:
        upstream = upstream.at[place.section]
    count = rows.shape[0]
    job = iter(())
    theirs, ours = pl.ds(count, count), pl.ds(0, count)
    if last:
        upper = place.section == 1
        first_own, second_own, grad_in, grad_down, out_zero, out_low, out_high, grad_one = extra
        first, second, got_in, got_down, outputs, input_grads, second_sum = wide
        lower = place.section == 0
        swapper = Sender(side[4], side[5])
        half = out_low.shape[2]
        my_rows, my_grads = outputs.at[place.section], input_grads.at[place.section]
        row_pairs = []
        for piece, above in enumerate((out_low, out_high)):
            columns = pl.ds(piece * half, half)
            row_pairs.append((out_zero.at[:, :, columns], above, my_rows.at[:, :, columns]))

        def keep_rows(index, low, high, target):
            one, two = (pltpu.make_async_copy(origin, target, side[6].at[index]) for origin in (low, high))
            pl.when(lower)(one.start)
            pl.when(upper)(two.start)
            return one

        kept_rows = [keep_rows(i, *pair) for i, pair in enumerate(row_pairs)]
        side_sender = Sender(side[0], side[1], upper)
        handing = Sender(side[2], side[3])

        def widen():
            first[place.z, place.y] = first_own[...]
            second[place.z, place.y] = second_own[...]
            yield
            met()
            yield from in_turn(gradient_gathers(place, side_sender, first, second))

        job = widen()
        summer = Sender(side[7], side[8], lower)
        second_parts, *second_slots = side[9:]

        def sum_second():
            handed_early()
            pl.when(lower)(lambda: output_products(heads_both, d_mid_low, second_parts))
            yield from reduce(place, summer, gradient_plans(second_parts), sort_slots(second_slots, 2, 2))
            second_sum[...] = second_parts[place.z, place.y]

        summing = sum_second()
    else:
        settling, settler = settle_part(1, place, side[3:5], extra[1], extra[0], wide[2], side[5:])
    dim = wk.shape[1]
    heads = wq.shape[1] // dim
    inner = heads * dim
    step = HEADS_STEP * dim
    steps = heads // HEADS_STEP
    quarter = d_part.shape[1]

    def pieces(q, k, v, o):
        return [*[o.at[pl.ds(i * step, step)] for i in range(steps)],
                *[q.at[:, pl.ds(i * step, step)] for i in range(steps)], k, v]

    loads = pull(layer, pieces(q0, k0, v0, o0), pieces(q1, k1, v1, o1), pieces(wq, wk, wv, wo), sems)
    for i in range(RING):
        grad = upstream[i].astype(F32) + d_part[i].astype(F32)
        d_mid[i] = grad
        total[i * quarter : (i + 1) * quarter] = grad
    grad_low = total[...].astype(BF16)
    d_mid_low[:count] = grad_low
    heads_both[:count] = attended[...]
    resid = rows[...].astype(F32)
    gain = of_layer(layer, pack0[PACK_ROUTER : PACK_ROUTER + 1], pack1[PACK_ROUTER : PACK_ROUTER + 1]).astype(F32)
    gains = of_layer(layer, pack0[PACK_ROUTER + 2 : PACK_ROUTER + 3], pack1[PACK_ROUTER + 2 : PACK_ROUTER + 3]).astype(F32)
    gain_query, gain_key = gains[:, :dim], gains[:, dim : 2 * dim]
    cosine, sine, allowed = tables(segments[place.section], dim)
    normed_both[:count] = (resid * inverse_rms(resid) * gain).astype(BF16)
    raw_key = key_raw[...]
    key = turn(raw_key * inverse_rms(raw_key) * gain_key, cosine, sine).astype(BF16)
    value = value_low[...]
    scale = 1.0 / math.sqrt(dim)
    d_key = jnp.zeros(key.shape, F32)
    d_value = jnp.zeros(key.shape, F32)
    gain_total = jnp.zeros(gain_query.shape, F32)
    handed_grads = None
    for i in range(steps):
        if i in WIDEN_POINTS:
            next(job, None)
        if not last and i in SETTLE_BESIDE:
            if i == 0:
                met()
            next(settling)
        if last and i == 1:
            handed_grads = handing.hand(upper, [(grad_in, got_in), (grad_down, got_down)], peer)
            handed_early = handing.hand(
                upper, [(ref.at[ours], ref.at[theirs]) for ref in (heads_both, d_mid_low, normed_both)], peer
            )
            swaps = [swapper.send_either(lower, high, low, target, peer) for low, high, target in row_pairs]
        if last and i == steps - 1:
            next(summing)
        loads[i].wait()
        d_heads[...] = dot_nt(grad_low, wo[i * step : (i + 1) * step]).astype(BF16)
        for h in range(HEADS_STEP):
            at = i * step + h * dim
            raw = query_raw[:, at : at + dim]
            query = turn(raw * inverse_rms(raw) * gain_query, cosine, sine).astype(BF16)
            scores = jnp.where(allowed, dot_nt(query, key) * scale, MASKED)
            raised = jnp.exp(scores - jnp.max(scores, axis=1, keepdims=True))
            probs = raised / jnp.sum(raised, axis=1, keepdims=True)
            d_head = d_heads[:, h * dim : (h + 1) * dim]
            d_probs = dot_nt(d_head, value)
            d_value = d_value + dot_tn(probs.astype(BF16), d_head)
            d_scores = (probs * (d_probs - jnp.sum(d_probs * probs, axis=1, keepdims=True))).astype(BF16)
            d_query = turn_back(dot_nn(d_scores, key) * scale, cosine, sine)
            d_key = d_key + dot_tn(d_scores, query) * scale
            d_raw, terms = rms_back(raw, gain_query, d_query)
            gain_total = gain_total + jnp.sum(terms, axis=0, keepdims=True)
            d_proj[:count, at : at + dim] = d_raw.astype(BF16)
        loads[steps + i].wait()
        piece = dot_nt(d_proj[:count, i * step : (i + 1) * step], wq[:, i * step : (i + 1) * step])
        if i == 0:
            total[...] = piece
        else:
            total[...] += piece
    d_raw, terms = rms_back(raw_key, gain_key, turn_back(d_key, cosine, sine))
    d_proj[:count, inner : inner + dim] = d_raw.astype(BF16)
    d_proj[:count, inner + dim :] = d_value.astype(BF16)
    smalls[0, 32:] = jnp.zeros((SMALL - 32, smalls.shape[2]), F32)
    smalls[0, :32] = router_term[...]
    smalls[0, 32:33] = moe_gain_term[...]
    smalls[0, 34:35, :dim] = gain_total
    smalls[0, 34:35, dim : 2 * dim] = jnp.sum(terms, axis=0, keepdims=True)
    loads[2 * steps].wait()
    loads[2 * steps + 1].wait()
    total[...] += dot_nt(d_proj[:count, inner : inner + dim], wk[...]) + dot_nt(d_proj[:count, inner + dim :], wv[...])
    for i in range(RING):
        part[i] = total[i * quarter : (i + 1) * quarter].astype(BF16)
    sender = Sender(send, recv)
    copies = send_x(place, sender, part, slots)
    handed = sender.hand(
        place.section != layer,
        [(ref.at[ours], ref.at[theirs]) for ref in ((d_proj,) if last else (normed_both, d_proj, heads_both, d_mid_low))],
        peer,
    )
    if last:
        next(summing, None)
    mine = resid[:quarter]
    for i in range(1, RING):
        mine = jnp.where(place.x == i, resid[i * quarter : (i + 1) * quarter], mine)
    d_resid, terms = rms_back(mine, gain, sum_x(place, copies, part, slots))
    smalls[0, 33:34] = jnp.sum(terms, axis=0, keepdims=True)
    handed_small = sender.hand(place.section != layer, [(smalls.at[0], smalls.at[1])], peer)
    d_rows = (d_mid[place.x] + d_resid).astype(BF16)
    if last:
        d_input[place.x] = d_rows
        gather_x(place, sender, d_input)
        swaps.append(swapper.send_either(lower, grad_one, d_input, my_grads, peer))
        kept_rows.append(keep_rows(2, d_input, grad_one, my_grads))
    else:
        own[...] = d_rows
        keep = pltpu.make_async_copy(own, d_input.at[place.z, place.y, place.x], local)
        keep.start()
        spread = gather(place, sender, thirds(d_input), own, keep.wait)
        for _ in range(3):
            next(spread)
            next(settling, None)
    handed()
    handed_small()
    if not last:
        owner = place.section == layer
        products, copy_out = side[:2], side[2]
        stores = [pltpu.make_async_copy(*pair, copy_out.at[i]) for i, pair in enumerate(zip(products, wide))]

        @pl.when(owner)
        def _():
            output_products(heads_both, d_mid_low, products[1])

        next(spread)

        @pl.when(owner)
        def _():
            stores[1].start()
            input_products(normed_both, d_proj, products[0])
            stores[0].start()

        run(in_turn([spread, settling]))
        settler.finish()
        fetch = pltpu.make_async_copy(d_input.at[place.z, place.y], wide[3], local)
        fetch.start()
        fetch.wait()

        @pl.when(owner)
        def _():
            for store in stores:
                store.wait()

    sender.finish()
    if last:
        handed_grads()
        for copy in swaps:
            copy.wait_recv()
        for copy in kept_rows:
            copy.wait()
        run(in_turn([job, summing]))
        summer.finish()
        swapper.finish()
        side_sender.finish()


def attend_back(layer, rows, segments, packs, saved, upstream, d_part, terms, extra, own, other):
    last = layer == 0
    first, second = gradient_shapes(own)
    wide = tuple(jax.ShapeDtypeStruct(shape, BF16) for shape in (first, second))
    side = (pltpu.VMEM(first, BF16), pltpu.VMEM(second, BF16), pltpu.SemaphoreType.DMA((2,)))
    if last:
        both = (2, *d_part.shape)
        shapes = (first, second, extra[2].shape, extra[3].shape, both, both, second[2:])
        wide = tuple(jax.ShapeDtypeStruct(shape, BF16) for shape in shapes)
        side = (
            *copy_sems(GRADIENT_SENDS),
            *copy_sems(2 + 3),
            *copy_sems(3),
            pltpu.SemaphoreType.DMA((3,)),
            *copy_sems(18),
            pltpu.VMEM(second, BF16),
            *slot_scratch([(second[2], 2, piece) for piece in cut(second[3], 2)]),
        )
    else:
        wide += (jax.ShapeDtypeStruct((*d_part.shape[:2], d_part.shape[2] // 2), BF16), jax.ShapeDtypeStruct(d_part.shape, BF16))
        side += tuple(settle_scratch(extra[1]))

    count, width = rows.shape[-2:]
    quarter = count // RING
    dim, inner = own[1].shape[1], own[0].shape[1]
    out = (RING, quarter, width) if layer == 0 else (RING, RING, RING, quarter, width)
    return pl.pallas_call(
        functools.partial(attend_back_kernel, layer),
        name="attend_back_last" if layer == 0 else "attend_back",
        out_shape=(
            jax.ShapeDtypeStruct(out, BF16),
            jax.ShapeDtypeStruct((2 * count, width), BF16),
            jax.ShapeDtypeStruct((2 * count, inner + 2 * dim), BF16),
            jax.ShapeDtypeStruct((2 * count, inner), BF16),
            jax.ShapeDtypeStruct((2 * count, width), BF16),
            jax.ShapeDtypeStruct((2, SMALL, width), F32),
            *wide,
        ),
        in_specs=[IN_VMEM] * 12 + ([IN_VMEM] * 2 + [ANYWHERE] * 2 + [IN_VMEM] * 4 if last else [IN_VMEM, ANYWHERE]) + [ANYWHERE] * 8,
        out_specs=(IN_VMEM if last else ANYWHERE,) + (IN_VMEM,) * (7 if last else 5) + (ANYWHERE,) * (4 if last else 2) + (IN_VMEM,) * (1 if last else 2),
        scratch_shapes=[
            *weight_scratch(own),
            pltpu.VMEM((count, width), F32),
            pltpu.VMEM((RING, quarter, width), F32),
            pltpu.VMEM((count, HEADS_STEP * dim), BF16),
            pltpu.VMEM((RING, quarter, width), BF16),
            pltpu.VMEM((quarter, width), BF16),
            pltpu.VMEM((3, quarter, width), BF16),
            pltpu.SemaphoreType.DMA((2 + 2 * (inner // dim // HEADS_STEP),)),
            *copy_sems(3 + 5 + (3 if layer == 0 else SENDS)),
            pltpu.SemaphoreType.DMA,
            *side,
        ],
        compiler_params=params(7 + layer),
    )(rows, segments, *packs, *saved, upstream, d_part, *terms, *extra, *own, *other)


def finish_kernel(
    normed0, proj0, second_sum, small0, small1, first_one, second_one,
    first, second, small_out,
    first_sums, normed, proj, terms, passing, small_slots, send, recv, flagged_send,
    flagged_recv, local, *slots
):
    place = Place()
    lower = place.section == 0
    upper = place.section == 1
    met = greet(neighbours(place))
    sender = Sender(send, recv)
    reducer = Sender(flagged_send, flagged_recv, lower)

    def keep(index, source, otherwise, target):
        one, two = (pltpu.make_async_copy(origin, target, local.at[index]) for origin in (source, otherwise))
        pl.when(lower)(one.start)
        pl.when(upper)(two.start)
        return one

    pairs = [(small0, small1, terms)]
    loads = ((normed0, normed), (proj0, proj))
    loads = [pltpu.make_async_copy(*pair, local.at[1 + i]) for i, pair in enumerate(loads)]
    ready = [
        pltpu.make_async_copy(*pair, local.at[3 + i]) for i, pair in enumerate(((first_one, first), (second_one, second)))
    ]

    @pl.when(upper)
    def _():
        for copy in ready:
            copy.start()

    @pl.when(lower)
    def _():
        for copy in loads:
            copy.start()
        second[place.z, place.y] = second_sum[...]

    kept = [keep(i, *pair) for i, pair in enumerate(pairs)]
    kept[0].wait()
    met()
    spreading = gather(place, reducer, gradient_plans(second))
    next(spreading)

    @pl.when(lower)
    def _():
        for copy in loads:
            copy.wait()
        input_products(normed, proj, first_sums)

    state = {}

    def exchange(step, total):
        passing[...] = total
        buffer = small_slots.at[step, 3]
        buffer[...] = total.astype(BF16)
        state["copies"] = [
            sender.send(buffer, small_slots.at[step, i], place.device("xyz"[step], delta))
            for i, delta in enumerate((1, -1, 2))
        ]

    def collect(step):
        for copy in state["copies"]:
            copy.wait_recv()
        total = passing[...]
        for i in range(3):
            total = total + small_slots[step, i].astype(F32)
        return total

    def small_last():
        small_out[...] = collect(2)

    def first_step():
        exchange(0, terms[0] + terms[1])

    def second_step():
        exchange(1, collect(0))

    summing = reduce(place, reducer, gradient_plans(first_sums), sort_slots(slots, 2, 2), (first_step, second_step))
    run(in_turn([summing, spreading]))

    @pl.when(lower)
    def _():
        first[place.z, place.y] = first_sums[place.z, place.y]

    beside = (lambda: exchange(2, collect(1)), small_last)
    run(gather(place, reducer, gradient_plans(first), None, None, beside))

    @pl.when(upper)
    def _():
        for copy in ready:
            copy.wait()

    sender.finish()
    reducer.finish()


def finish(factors, smalls, ready):
    first, second = ready[0].shape, ready[1].shape
    return pl.pallas_call(
        finish_kernel,
        name="finish",
        out_shape=(
            jax.ShapeDtypeStruct(first, BF16),
            jax.ShapeDtypeStruct(second, BF16),
            jax.ShapeDtypeStruct(smalls[0].shape[1:], F32),
        ),
        in_specs=[ANYWHERE] * 2 + [IN_VMEM] + [ANYWHERE] * 4,
        out_specs=(IN_VMEM,) * 3,
        scratch_shapes=[
            pltpu.VMEM(first, BF16),
            *[pltpu.VMEM(f.shape, BF16) for f in factors[:2]],
            pltpu.VMEM(smalls[0].shape, F32),
            pltpu.VMEM(smalls[0].shape[1:], F32),
            pltpu.VMEM((3, 4, *smalls[0].shape[1:]), BF16),
            *copy_sems(9),
            *copy_sems(18 + GRADIENT_SENDS),
            pltpu.SemaphoreType.DMA((5,)),
            *slot_scratch([(first[2], 2, piece) for piece in cut(first[3], 2)]),
        ],
        compiler_params=params(9),
    )(*factors, *smalls, *ready)


STEPS = 8


def widen_kernel(
    section, first, second, gate_own0, gate_own1, up_own0, up_own1, gate_got0, gate_got1, up_got0, up_got1,
    down_own0, down_own1, down_got0, down_got1, small, outputs_in, d_inputs_in,
    query, key, value, output, gate, up, down, router, gain_moe, gain_attn, gain_query, gain_key, outputs, d_inputs
):
    inner, dim = query.shape[1], key.shape[1]
    query[...] = first[:, :inner].astype(F32)
    key[...] = first[:, inner : inner + dim].astype(F32)
    value[...] = first[:, inner + dim :].astype(F32)
    output[...] = second[...].astype(F32)
    lower = section[0] == 0

    def either(low, high):
        return jnp.where(lower, low[...].astype(F32), high[...].astype(F32))

    gate[...] = either(gate_own0, gate_own1) + either(gate_got0, gate_got1)
    up[...] = either(up_own0, up_own1) + either(up_got0, up_got1)
    down[...] = either(down_own0, down_own1) + either(down_got0, down_got1)
    outputs[...] = outputs_in[...]
    d_inputs[...] = d_inputs_in[...].astype(F32)

    @pl.when(pl.program_id(0) == 0)
    def _():
        count = router.shape[0]
        router[...] = small[:count]
        gain_moe[...] = small[count : count + 1]
        gain_attn[...] = small[count + 1 : count + 2]
        gain_query[...] = small[count + 2 : count + 3, :dim]
        gain_key[...] = small[count + 2 : count + 3, dim : 2 * dim]


def widen(section, first, second, expert_grads, small, outputs, d_inputs, dim, expert_count):
    (in0, down0, got_in0, got_down0), (in1, down1, got_in1, got_down1) = expert_grads
    width = second.shape[1]
    inner = first.shape[1] - 2 * dim
    units = down0.shape[0]

    def rows(count, columns):
        return pl.BlockSpec((count // STEPS, columns), lambda i, section: (i, 0))

    def either(ahead=0):
        block = (units // STEPS, width)
        return [
            pl.BlockSpec(block, lambda i, section: (jnp.where(section[0] == 0, ahead + i, ahead), 0)),
            pl.BlockSpec(block, lambda i, section: (jnp.where(section[0] == 1, ahead + i, ahead), 0)),
        ]

    def whole(*shape):
        return pl.BlockSpec(shape, lambda i, section: (0,) * len(shape))

    def slab(array):
        return pl.BlockSpec((*array.shape[:-1], width // STEPS), lambda i, section: (0, 0, 0, i))

    def shape(*dims):
        return jax.ShapeDtypeStruct(dims, F32)

    return pl.pallas_call(
        widen_kernel,
        name="widen",
        out_shape=(
            shape(width, inner),
            shape(width, dim),
            shape(width, dim),
            shape(*second.shape),
            shape(units, width),
            shape(units, width),
            shape(units, width),
            shape(expert_count, width),
            shape(1, width),
            shape(1, width),
            shape(1, dim),
            shape(1, dim),
            jax.ShapeDtypeStruct(outputs.shape, BF16),
            shape(*d_inputs.shape),
        ),
        grid_spec=pltpu.PrefetchScalarGridSpec(
            num_scalar_prefetch=1,
            grid=(STEPS,),
            in_specs=[
                rows(width, first.shape[1]),
                rows(second.shape[0], width),
                *either(),
                *either(STEPS),
                *either(),
                *either(STEPS),
                *either(),
                *either(),
                whole(*small.shape),
                slab(outputs),
                slab(d_inputs),
            ],
            out_specs=(
                rows(width, inner),
                rows(width, dim),
                rows(width, dim),
                rows(second.shape[0], width),
                rows(units, width),
                rows(units, width),
                rows(units, width),
                whole(expert_count, width),
                whole(1, width),
                whole(1, width),
                whole(1, dim),
                whole(1, dim),
                slab(outputs),
                slab(d_inputs),
            ),
        ),
        compiler_params=pltpu.CompilerParams(vmem_limit_bytes=VMEM_LIMIT),
    )(
        section[None], first, second, in0, in1, in0, in1, got_in0, got_in1, got_in0, got_in1,
        down0, down1, got_down0, got_down1, small, outputs, d_inputs,
    )


def body(
    block_input,
    cotangent,
    segments,
    routes,
    norm_attn,
    w_query,
    key_matrix,
    value_matrix,
    norm_query,
    norm_key,
    w_output,
    norm_moe,
    w_router,
    w_gate,
    w_up,
    w_down,
):
    section = lax.axis_index("section")
    _, group_rows, width = block_input.shape
    expert_count = w_router.shape[2]
    quarter = group_rows // RING
    dim = norm_query.shape[1]

    dense_own = (w_query[0], key_matrix[0], value_matrix[0], w_output[0])
    expert_own = (jnp.swapaxes(w_gate[0], 1, 2), jnp.swapaxes(w_up[0], 1, 2), w_down[0])
    layer_gains = (w_router[0].T, norm_attn, norm_moe, norm_query, norm_key)
    routes = jnp.swapaxes(routes[0], 1, 2)
    upstream = cotangent.reshape(2, RING, quarter, width)
    rows_in = block_input
    saved, layer_ins, outs, grads_all = [], [], [], []
    for layer in range(2):
        layer_ins.append(rows_in)
        if layer == 0:
            made = forward(layer, rows_in, segments, layer_gains, routes, upstream, dense_own, None, expert_own, None)
            packs, routes_other = made[10:12], made[12]
            dense_other, expert_other = made[13:17], made[17:]
        else:
            made = forward(
                layer, rows_in, segments, packs, (routes, routes_other), upstream, dense_own, dense_other,
                expert_own, expert_other,
            )
        attn_saved, (mid, gates, rows_all, spread, acts, made) = made[:4], made[4:10]
        grads_all.append(spread)
        saved.append((attn_saved, mid, gates, rows_all, acts))
        if layer == 0:
            rows_in = made.reshape(group_rows, width)
            outs.append(made)
    made = made.reshape(RING, RING, RING, quarter, width)

    attn_saved, mid, gates, rows_all, acts = saved[1]
    d_part, *terms, grad_in, grad_down, out_low = experts_back_sum(
        1, rows_all, grads_all, acts, mid, gates, packs, expert_own, expert_other, made, expert_count
    )
    grads_one = (grad_in, grad_down)
    d_all, *_, smalls_one, products_first, products_second, out_high, upstream = attend_back(
        1, layer_ins[1], segments, packs, attn_saved, upstream, d_part, terms[::-1], (mid, made), dense_own, dense_other
    )
    outs += [out_low, out_high]
    attn_saved, mid, gates, rows_all, acts = saved[0]
    partial, *grads_zero, first_own, second_own, got_in_one, got_down_one = experts_back(
        0, rows_all, [d_all], acts, expert_own, expert_other, ((products_first, products_second), grads_one, dense_own)
    )
    d_part, *terms = moe_back(0, partial, mid, gates, packs, expert_count)
    _, *factors_zero, smalls_zero, first_one, second_one, got_in_zero, got_down_zero, outputs, d_inputs, second_sum = attend_back(
        0, layer_ins[0], segments, packs, attn_saved, upstream, d_part, terms[::-1],
        (first_own, second_own, *grads_zero, *outs, upstream), dense_own, dense_other,
    )
    expert_grads = ((*grads_zero, got_in_zero, got_down_zero), (*grads_one, got_in_one, got_down_one))
    first, second, small = finish((*factors_zero[:2], second_sum), (smalls_zero, smalls_one), (first_one, second_one))
    query, key, value, output, gate, up, down, router, gain_moe, gain_attn, gain_query, gain_key, outputs, d_inputs = widen(
        section, first.reshape(width, first.shape[-1]), second.reshape(-1, width), expert_grads, small, outputs, d_inputs,
        dim, expert_count,
    )
    units = w_gate.shape[3]

    def by_expert(array):
        return array.reshape(1, 2, units, width)

    return (
        outputs.reshape(1, 2, group_rows, width),
        d_inputs.reshape(1, 2, group_rows, width),
        gain_attn,
        query[None],
        key[None],
        value[None],
        gain_query,
        gain_key,
        output[None],
        gain_moe,
        router.T[None],
        jnp.swapaxes(by_expert(gate), 2, 3),
        jnp.swapaxes(by_expert(up), 2, 3),
        by_expert(down),
    )


def solution(mesh):
    placed = (
        P(None, "expert", None),
        P(None, "expert", None),
        P(None, "expert", None),
        P("section", None, "expert", None),
        P("section", None),
        P("section", None, "tensor"),
        P("section", None, "tensor"),
        P("section", None, "tensor"),
        P("section", None),
        P("section", None),
        P("section", "tensor", None),
        P("section", None),
        P("section", None, None),
        P("section", "expert", None, "tensor"),
        P("section", "expert", None, "tensor"),
        P("section", "expert", "tensor", None),
    )
    return jax.shard_map(
        body,
        mesh=mesh,
        in_specs=placed,
        out_specs=(
            P("section", None, "expert", None),
            P("section", None, "expert", None),
            P("section", None),
            P("section", None, "tensor"),
            P("section", None, "tensor"),
            P("section", None, "tensor"),
            P("section", None),
            P("section", None),
            P("section", "tensor", None),
            P("section", None),
            P("section", None, None),
            P("section", "expert", None, "tensor"),
            P("section", "expert", None, "tensor"),
            P("section", "expert", "tensor", None),
        ),
        check_vma=False,
    )
```
